32 devices in a mesh: batch: 16 (over z, y, core), heads: 2 (over x).
Axes of the slice: x: 2, y: 2, z: 4, core: 2. Of those that a mesh axis runs over, the one named last changes fastest.
Arguments:
- tokens: bfloat16 [86016, 128], P(('batch', 'heads')), may hold values from -6 to 6
- image_bands: int32 [16, 24], P('batch'), may hold values from 0 to 14, as said below
- cotangent: bfloat16 [86016, 128], P(('batch', 'heads')), may hold values from -6 to 6
- front_gains: float32 [2, 128], replicated, may hold values from 0.1 to 1.9
- front_shifts: float32 [4, 128], replicated, may hold values from -2 to 2
- query_w: bfloat16 [128, 128], P(None, 'heads'), may hold values from -1 to 1
- coarse_conv: bfloat16 [2048, 128], replicated, may hold values from -0.125 to 0.125
- coarse_gain: float32 [128], replicated, may hold values from 0.1 to 1.9
- coarse_shifts: float32 [3, 128], replicated, may hold values from -2 to 2
- coarse_kv: bfloat16 [128, 128], replicated, may hold values from -0.5 to 0.5
- coarse_taps: float32 [9, 64], replicated, may hold values from -2 to 2
- fine_conv: bfloat16 [512, 128], replicated, may hold values from -0.25 to 0.25
- fine_gain: float32 [128], replicated, may hold values from 0.1 to 1.9
- fine_shifts: float32 [3, 128], replicated, may hold values from -2 to 2
- fine_kv: bfloat16 [128, 128], replicated, may hold values from -0.5 to 0.5
- fine_taps: float32 [9, 64], replicated, may hold values from -2 to 2
- proj_w: bfloat16 [128, 128], replicated, may hold values from -1.5 to 1.5
- hidden_shifts: float32 [2, 1024], P(None, 'heads'), may hold values from -2 to 2
- fc1_w: bfloat16 [128, 1024], P(None, 'heads'), may hold values from -0.5 to 0.5
- depth_taps: float32 [9, 1024], P(None, 'heads'), may hold values from -2 to 2
- fc2_w: bfloat16 [1024, 128], P('heads'), may hold values from -0.1875 to 0.1875
Outputs:
- output: bfloat16 [86016, 128], P(('batch', 'heads'))
- tokens_grad: float32 [86016, 128], P(('batch', 'heads'))
- front_gains_grad: float32 [2, 128], replicated
- front_shifts_grad: float32 [4, 128], replicated
- query_w_grad: float32 [128, 128], P(None, 'heads')
- coarse_conv_grad: float32 [2048, 128], replicated
- coarse_gain_grad: float32 [128], replicated
- coarse_shifts_grad: float32 [3, 128], replicated
- coarse_kv_grad: float32 [128, 128], replicated
- coarse_taps_grad: float32 [9, 64], replicated
- fine_conv_grad: float32 [512, 128], replicated
- fine_gain_grad: float32 [128], replicated
- fine_shifts_grad: float32 [3, 128], replicated
- fine_kv_grad: float32 [128, 128], replicated
- fine_taps_grad: float32 [9, 64], replicated
- proj_w_grad: float32 [128, 128], replicated
- hidden_shifts_grad: float32 [2, 1024], P(None, 'heads')
- fc1_w_grad: float32 [128, 1024], P(None, 'heads')
- depth_taps_grad: float32 [9, 1024], P(None, 'heads')
- fc2_w_grad: float32 [1024, 128], P('heads')
The draws below stay inside these ranges and needn't reach their ends.
Inputs may be any that keep to these rules, and one draw needn't show every extreme that they name: `image_bands`: each row lists the heights, in bands of 4 rows of 56 patches, of one group's images, nonzero heights first and zeros after; a row adds up to at most 24; one row adds up to exactly 24 and begins with an image of 14 bands.
All inputs are finite; a program needn't handle non-finite values.
Results may differ from the reference program's by a relative error of at most 0.018.
Values may be sent and summed in bfloat16 or wider, within the bound.
A program may use at most 192 MiB of HBM per device.

```python
import jax
import jax.numpy as jnp
from jax import lax

D = 128
FF = 1024
W = 56
BANDS_DEV = 24
MAX_BANDS = 14
TOK_DEV = 5376
TOKENS = 86016
N_BATCH = 16


def draw_image_bands(key, part):
    key = jax.random.fold_in(key, 11)
    live_key, full_key, height_key = jax.random.split(key, 3)
    groups = jnp.arange(N_BATCH, dtype=jnp.int32)
    live_bands = jax.random.randint(live_key, (N_BATCH,), BANDS_DEV // 2, BANDS_DEV + 1, dtype=jnp.int32)
    full_group = jax.random.randint(full_key, (), 0, N_BATCH, dtype=jnp.int32)
    live_bands = jnp.where(groups == full_group, BANDS_DEV, live_bands).astype(jnp.int32)
    heights = jax.random.randint(height_key, (N_BATCH, BANDS_DEV), 1, MAX_BANDS + 1, dtype=jnp.int32)
    first_height = jnp.where(groups == full_group, MAX_BANDS, heights[:, 0]).astype(jnp.int32)
    heights = jnp.concatenate([first_height[:, None], heights[:, 1:]], axis=1)
    running = jnp.cumsum(heights, axis=1).astype(jnp.int32)
    kept_heights = jnp.where(running <= live_bands[:, None], heights, 0).astype(jnp.int32)
    remain = (live_bands - jnp.sum(kept_heights, axis=1)).astype(jnp.int32)
    placed = jnp.sum((kept_heights > 0).astype(jnp.int32), axis=1).astype(jnp.int32)
    slot_index = jnp.arange(BANDS_DEV, dtype=jnp.int32)
    return jnp.where(slot_index[None, :] == placed[:, None], remain[:, None], kept_heights).astype(jnp.int32)


def block_levels(stream_key, dims, cuts, smallest, high):
    gain = 1.0
    for dim, blocks in cuts:
        draws = jax.random.uniform(jax.random.fold_in(jax.random.fold_in(stream_key, 6), dim), (blocks,), jnp.float32, smallest / len(cuts), high / len(cuts))
        gain = gain * jnp.repeat(jnp.exp(draws), dims[dim] // blocks).reshape((-1,) + (1,) * (len(dims) - 1 - dim))
    return gain


def normal_values(stream_key, extent, width, reach, cuts=(), kind=jnp.bfloat16):
    values = width * jax.random.normal(stream_key, extent, jnp.float32)
    if cuts:
        values = values * block_levels(stream_key, extent, cuts, -0.22, 0.18)
    return jnp.clip(values, -reach, reach).astype(kind)


def setup_inputs(seed: int = 0) -> dict:
    key_list = jax.random.split(jax.random.key(seed), 22)
    return {
        "tokens": normal_values(key_list[0], (TOKENS, D), 1.0, 6.0, ((0, 32),)),
        "image_bands": draw_image_bands(jax.random.fold_in(key_list[21], 71), 0),
        "cotangent": normal_values(key_list[2], (TOKENS, D), 1.0, 6.0, ((0, 32),)),
        "front_gains": jnp.clip(1.0 + 0.18 * jax.random.normal(key_list[3], (2, D), jnp.float32), 0.1, 1.9),
        "front_shifts": normal_values(key_list[4], (4, D), 0.3, 2.0, (), jnp.float32),
        "query_w": normal_values(key_list[5], (D, D), (D // 4) ** -0.5, 1.0, ((1, 2),)),
        "coarse_conv": normal_values(key_list[6], (16 * D, D), (16 * D) ** -0.5, 0.125),
        "coarse_gain": jnp.clip(1.0 + 0.18 * jax.random.normal(key_list[7], (D,), jnp.float32), 0.1, 1.9),
        "coarse_shifts": normal_values(key_list[8], (3, D), 0.3, 2.0, (), jnp.float32),
        "coarse_kv": normal_values(key_list[9], (D, D), D ** -0.5, 0.5),
        "coarse_taps": normal_values(key_list[10], (9, D // 2), 9 ** -0.5, 2.0, (), jnp.float32),
        "fine_conv": normal_values(key_list[11], (4 * D, D), (4 * D) ** -0.5, 0.25),
        "fine_gain": jnp.clip(1.0 + 0.18 * jax.random.normal(key_list[12], (D,), jnp.float32), 0.1, 1.9),
        "fine_shifts": normal_values(key_list[13], (3, D), 0.3, 2.0, (), jnp.float32),
        "fine_kv": normal_values(key_list[14], (D, D), D ** -0.5, 0.5),
        "fine_taps": normal_values(key_list[15], (9, D // 2), 9 ** -0.5, 2.0, (), jnp.float32),
        "proj_w": normal_values(key_list[16], (D, D), (D // 8) ** -0.5, 1.5),
        "hidden_shifts": normal_values(key_list[17], (2, FF), 0.3, 2.0, ((1, 2),), jnp.float32),
        "fc1_w": normal_values(key_list[18], (D, FF), D ** -0.5, 0.5, ((1, 2),)),
        "depth_taps": normal_values(key_list[19], (9, FF), 9 ** -0.5, 2.0, ((1, 2),), jnp.float32),
        "fc2_w": normal_values(key_list[20], (FF, D), FF ** -0.5, 0.1875, ((0, 2),)),
    }


HIGH_PRECISION = lax.Precision.HIGHEST
EPS = 1e-06

@jax.custom_vjp
def low(v):
    return lax.optimization_barrier(v.astype(jnp.bfloat16)).astype(jnp.float32)

@jax.custom_vjp
def lower_backward(v):
    return v

def low_keep(v):
    return (low(v), None)

def low_pass(kept, grad):
    return (grad,)

def back_keep(v):
    return (v, None)

def back_low(kept, grad):
    return (low(grad),)
low.defvjp(low_keep, low_pass)
lower_backward.defvjp(back_keep, back_low)

def matmul(left, right):
    return jnp.dot(left, right, precision=HIGH_PRECISION)

def normalize(values, norm_gain, norm_shift):
    mean_val = lax.optimization_barrier(jnp.mean(values, axis=-1, keepdims=True))
    centred = values - mean_val
    variance = lax.optimization_barrier(jnp.mean(centred * centred, axis=-1, keepdims=True))
    return centred * lax.rsqrt(variance + EPS) * norm_gain + norm_shift

def band_images(heights, band_count):
    ends = jnp.cumsum(heights).astype(jnp.int32)
    band_index = jnp.arange(band_count, dtype=jnp.int32)
    image_num = lax.optimization_barrier(jnp.sum((band_index[:, None] >= ends[None, :]).astype(jnp.int32), axis=1)).astype(jnp.int32)
    return jnp.where(band_index < ends[-1], image_num, -1).astype(jnp.int32)

def depthwise(grid, tap_weights, row_ids):
    grid_rows, grid_cols = (grid.shape[0], grid.shape[1])
    padded = jnp.pad(grid, ((1, 1), (1, 1), (0, 0)))
    padded_ids = jnp.pad(row_ids, 1, constant_values=-2)
    result = jnp.zeros_like(grid)
    for above in range(3):
        same_image = (padded_ids[above:above + grid_rows] == row_ids).astype(grid.dtype)[:, None, None]
        for across in range(3):
            result = result + padded[above:above + grid_rows, across:across + grid_cols] * tap_weights[3 * above + across] * same_image
    return result

def patchify(grid, stride_len):
    grid_rows, grid_cols, channels = grid.shape
    blocks = grid.reshape(grid_rows // stride_len, stride_len, grid_cols // stride_len, stride_len, channels)
    blocks = blocks.transpose(0, 2, 1, 3, 4)
    return blocks.reshape(grid_rows // stride_len * (grid_cols // stride_len), stride_len * stride_len * channels)

def attend(queries, key_part, value_part, query_ids, key_ids):
    tok_count = queries.shape[0]
    head_width = key_part.shape[1] // 2
    block_rows = min(tok_count, 16 * W)
    key_head_rows = key_part.reshape(-1, 2, head_width)
    value_head_rows = value_part.reshape(-1, 2, head_width)

    def score_block(entry_now):
        query_block_rows, block_ids = entry_now
        score_matrix = lower_backward(jnp.einsum('lfq,tfq->flt', query_block_rows, key_head_rows, precision=HIGH_PRECISION) * head_width ** (-0.5))
        allowed = (block_ids[:, None] == key_ids[None, :]) & (block_ids[:, None] >= 0)
        score_matrix = jnp.where(allowed[None], score_matrix, -1000000000.0)
        largest = lax.optimization_barrier(jnp.max(score_matrix, axis=-1, keepdims=True))
        expo = jnp.exp(score_matrix - largest)
        softmax_weight_rows = low(expo / lax.optimization_barrier(jnp.sum(expo, axis=-1, keepdims=True)))
        return jnp.einsum('vyq,qvz->yvz', softmax_weight_rows, value_head_rows, precision=HIGH_PRECISION)
    blocks_out = lax.map(jax.checkpoint(score_block), (queries.reshape(tok_count // block_rows, block_rows, 2, head_width), query_ids.reshape(tok_count // block_rows, block_rows)))
    return blocks_out.reshape(tok_count, 2 * head_width)

def canvas_forward(inputs, heights, params):
    front_gains, front_shifts, query_w, coarse_conv, coarse_gain, coarse_shifts, coarse_kv, coarse_taps, fine_conv, fine_gain, fine_shifts, fine_kv, fine_taps, proj_w, hidden_shifts, fc1_w, depth_taps, fc2_w = params
    tok_count = inputs.shape[0]
    grid_rows = tok_count // W
    band_ids = band_images(heights, grid_rows // 4)
    token_ids = jnp.repeat(band_ids, 4 * W)
    live_mask = (token_ids >= 0).astype(jnp.float32)[:, None]
    half_width = D // 2
    normed = low(normalize(inputs, front_gains[0], front_shifts[0]))
    queries = lower_backward(low(matmul(normed, query_w)))
    token_grid = normed.reshape(grid_rows, W, D)
    outputs = []
    rates = ((4, coarse_conv, coarse_gain, coarse_shifts, coarse_kv, coarse_taps), (2, fine_conv, fine_gain, fine_shifts, fine_kv, fine_taps))
    for branch_index in range(2):
        stride_len, conv_w, norm_gain, shifts, kv_weight, tap_weights = rates[branch_index]
        reduced = lower_backward(matmul(patchify(token_grid, stride_len), conv_w) + shifts[0])
        active = low(jax.nn.gelu(normalize(reduced, norm_gain, shifts[1]), approximate=False))
        key_value = matmul(active, kv_weight)
        key_part = lower_backward(low(key_value[:, :half_width]))
        values = lower_backward(key_value[:, half_width:] + shifts[2, :half_width])
        key_rows = jnp.repeat(band_ids, 4 // stride_len)
        value_grid = values.reshape(grid_rows // stride_len, W // stride_len, half_width)
        value_part = lower_backward(low(values + depthwise(value_grid, tap_weights, key_rows).reshape(-1, half_width) + shifts[2, half_width:]))
        key_ids = jnp.repeat(key_rows, W // stride_len)
        own_queries = queries[:, branch_index * half_width:(branch_index + 1) * half_width]
        outputs.append(attend(own_queries.reshape(tok_count, 2, -1), key_part, value_part, token_ids, key_ids))
    heads_out = lower_backward(low(jnp.concatenate(outputs, axis=1) * live_mask))
    middle = inputs + lower_backward(matmul(heads_out, proj_w) + front_shifts[1])
    normed_mid = low(normalize(middle, front_gains[1], front_shifts[2]))
    hidden = lower_backward(matmul(normed_mid, fc1_w) + hidden_shifts[0])
    spread = hidden + depthwise(hidden.reshape(grid_rows, W, FF), depth_taps, jnp.repeat(band_ids, 4)).reshape(tok_count, FF) + hidden_shifts[1]
    activated = low(jax.nn.gelu(spread, approximate=False))
    return (middle + lower_backward(matmul(activated, fc2_w) + front_shifts[3])) * live_mask

def reference(tokens, image_bands, cotangent, front_gains, front_shifts, query_w, coarse_conv, coarse_gain, coarse_shifts, coarse_kv, coarse_taps, fine_conv, fine_gain, fine_shifts, fine_kv, fine_taps, proj_w, hidden_shifts, fc1_w, depth_taps, fc2_w):
    params = tuple((weight.astype(jnp.float32) for weight in (front_gains, front_shifts, query_w, coarse_conv, coarse_gain, coarse_shifts, coarse_kv, coarse_taps, fine_conv, fine_gain, fine_shifts, fine_kv, fine_taps, proj_w, hidden_shifts, fc1_w, depth_taps, fc2_w)))
    inputs = tokens.astype(jnp.float32).reshape(N_BATCH, TOK_DEV, D)
    grads_in = cotangent.astype(jnp.float32).reshape(N_BATCH, TOK_DEV, D)

    def one_canvas(totals, entry_now):
        canvas, canvas_grad, heights = entry_now

        def forward(inputs_now, params_now):
            return canvas_forward(inputs_now, heights, params_now)
        result, pullback = jax.vjp(forward, canvas, params)
        input_grad, param_grads = pullback(canvas_grad)
        summed = tuple((running + grad_now for running, grad_now in zip(totals, param_grads)))
        return (summed, (result.astype(jnp.bfloat16), input_grad))
    initial = tuple((jnp.zeros(weight.shape, jnp.float32) for weight in params))
    sums, (results, input_grads) = lax.scan(one_canvas, initial, (inputs, grads_in, image_bands))
    return (results.reshape(TOKENS, D), input_grads.reshape(TOKENS, D)) + sums
```

```python
import functools

import jax
import jax.numpy as jnp
from jax import lax
from jax.experimental import pallas as pl
from jax.experimental.pallas import tpu as pltpu
from jax.sharding import PartitionSpec as P

W = 56
BAND = 4 * W
SLOTS = 256
COARSE = 16
FINE = 64
CELLS = COARSE + FINE
MAX_BANDS = 14
EPS = 1e-06
F32 = jnp.float32
BF16 = jnp.bfloat16
SCALE = 32**-0.5
LOG2E = 1.4426950408889634
ROOT = 0.7071067811865476
EXP_SCALE = SCALE * LOG2E
BIG = -1e9
MIB = 1024 * 1024
STEP = 256
SPAN = 512
MESH = pl.DeviceIdType.MESH
TAPS = 9
KEPT = TAPS * 128 + 16
WIDE = (TAPS + 1) * 128
QUARTER = 768
CONV = 512
REST = QUARTER - CONV
SMALL = 48
SPLIT = 544


def dot(left, right):
    return jnp.dot(left, right, preferred_element_type=F32)


def dot_t(left, right):
    return lax.dot_general(left, right, (((1,), (1,)), ((), ())), preferred_element_type=F32)


def dot_in(left, right):
    return lax.dot_general(left, right, (((0,), (0,)), ((), ())), preferred_element_type=F32)


def gauss(values):
    return 0.5 + 0.5 * lax.erf(values * ROOT), jnp.exp2(values * values * (-0.5 * LOG2E))


def gelu_slope(values, cdf, bell):
    return cdf + values * bell * 0.3989422804014327


def fold_rows(values):
    wide = jnp.sum(values.reshape(-1, 64, 128), axis=0)
    return jnp.sum(wide.reshape(8, 8, 128), axis=0)


def norm_hat(values):
    centred = values - jnp.mean(values, axis=-1, keepdims=True)
    inverse = lax.rsqrt(jnp.mean(centred * centred, axis=-1, keepdims=True) + EPS)
    return centred * inverse, inverse


def norm_back(grad_scaled, hat, inverse):
    centre = jnp.mean(grad_scaled, axis=-1, keepdims=True)
    along = jnp.mean(grad_scaled * hat, axis=-1, keepdims=True)
    return inverse * (grad_scaled - centre - hat * along)


def slot_map(slot, token):
    a, b, c = slot >> 6, (slot >> 4) & 3, slot & 15
    hit = (token == a * W + 4 * c + b) & (c < 14)
    return jnp.where(hit, 1.0, 0.0).astype(BF16)


def to_slots():
    shape = (SLOTS, BAND)
    return slot_map(
        lax.broadcasted_iota(jnp.int32, shape, 0), lax.broadcasted_iota(jnp.int32, shape, 1)
    )


def from_slots():
    shape = (BAND, SLOTS)
    return slot_map(
        lax.broadcasted_iota(jnp.int32, shape, 1), lax.broadcasted_iota(jnp.int32, shape, 0)
    )


def cell_valid(shape, axis):
    return (lax.broadcasted_iota(jnp.int32, shape, axis) & 15) < 14


def roll_cells(values, step):
    lead = values.shape[:-2]
    flat = values.reshape(-1, values.shape[-1])
    flat = pltpu.roll(flat, step % flat.shape[0], 0)
    return flat.reshape(lead + values.shape[-2:])


def by_band(values, mask):
    count = values.shape[0]
    wide = values.reshape(count, -1, 8, 128) * mask.reshape(count, 1, 8, 128)
    return wide.reshape(values.shape)


def row_taps(taps, flip):
    order = [8 - i for i in range(9)] if flip else list(range(9))
    return [taps[i : i + 1, :] for i in order]


def depthwise_coarse(ext, above, below, taps, flip=False):
    t = row_taps(taps, flip)
    up, mid, down = by_band(ext[:-2], above), ext[1:-1], by_band(ext[2:], below)
    left, centre, right = (up * t[b] + mid * t[3 + b] + down * t[6 + b] for b in range(3))
    return centre + roll_cells(left, 1) + roll_cells(right, -1)


def fine_rows(ext, above, below):
    bands = ext.shape[0] - 2
    grid = ext.reshape(bands + 2, 2, 2, 16, 128)
    first, second = grid[:, 0], grid[:, 1]
    up = (by_band(second[:-2], above), first[1:-1])
    mid = (first[1:-1], second[1:-1])
    down = (second[1:-1], by_band(first[2:], below))
    return up, mid, down


def depthwise_fine(ext, above, below, taps, flip=False):
    t = row_taps(taps, flip)
    ups, mids, downs = fine_rows(ext, above, below)
    rows = []
    for up, mid, down in zip(ups, mids, downs):
        left, centre, right = (up * t[b] + mid * t[3 + b] + down * t[6 + b] for b in range(3))
        even = centre[:, 0] + roll_cells(left[:, 1], 1) + right[:, 1]
        odd = centre[:, 1] + left[:, 0] + roll_cells(right[:, 0], -1)
        rows.append((even, odd))
    return rows


def greet(*peers):
    barrier = pltpu.get_barrier_semaphore()
    for peer in peers:
        pl.semaphore_signal(barrier, inc=1, device_id=peer, device_id_type=MESH)


def met(count):
    pl.semaphore_wait(pltpu.get_barrier_semaphore(), count)


def fetch(pairs, sems):
    loads = [pltpu.make_async_copy(source, target, sems.at[i]) for i, (source, target) in enumerate(pairs)]
    for load in loads:
        load.start()
    return loads


def link(source, target, send_sem, recv_sem, peer):
    return pltpu.make_async_remote_copy(
        src_ref=source,
        dst_ref=target,
        send_sem=send_sem,
        recv_sem=recv_sem,
        device_id=peer,
        device_id_type=MESH,
    )


def remote(source, target, send_sem, recv_sem, peer):
    made = link(source, target, send_sem, recv_sem, peer)
    made.start()
    return made


def across():
    return (lax.axis_index("batch"), 1 - lax.axis_index("heads"))


def swap_lanes(values):
    half = values.shape[1] // 2
    return jnp.concatenate([values[:, half:], values[:, :half]], axis=1)


def keep_lanes(values, upper):
    lane = lax.broadcasted_iota(jnp.int32, values.shape, 1)
    return jnp.where((lane >= 64) if upper else (lane < 64), values, 0.0)


def pad_taps(taps, upper):
    gap = jnp.zeros(taps.shape, F32)
    return jnp.concatenate([gap, taps] if upper else [taps, gap], axis=1)


def band_tables(heights, table, meta, total):
    count = heights.shape[1]
    number = jnp.int32(0)
    start = jnp.int32(0)
    end = heights[0, 0]
    last = jnp.int32(-2)
    images, sames = [], []
    for band in range(total):
        passed = band >= end
        number = jnp.where(passed, number + 1, number)
        start = jnp.where(passed, end, start)
        grown = heights[0, jnp.minimum(number, count - 1)]
        grown = jnp.where(number < count, grown, 0)
        end = jnp.where(passed, end + grown, end)
        image = jnp.where(band < end, number, -1)
        same = jnp.where(image == last, 1, 0)
        last = image
        table[0, band] = image
        table[1, band] = jnp.minimum(start, total - MAX_BANDS)
        table[2, band] = same
        images.append(image)
        sames.append(same)
    for band in range(total, table.shape[1]):
        for row in range(3):
            table[row, band] = jnp.int32(0)
    sames.append(jnp.int32(0))
    for band in range(total):
        for row, value in enumerate((sames[band], sames[band + 1], images[band])):
            meta[row, band] = jnp.full((8, 128), value.astype(F32), F32)


def front_kernel(
    heights, tok, gains, shifts, conv_c, gain_c, shifts_c, kv_c, conv_f, gain_f, shifts_f, kv_f,
    query_t,
    table, meta, xn_out, hat_out, red_c, red_f, slab, other, query_o,
    send, send_sems, recv_sems,
):
    bands = xn_out.shape[0]
    peer = across()
    greet(peer)
    copies = []

    def give(source, target):
        at = len(copies)
        copies.append(remote(source, target, send_sems.at[at], recv_sems.at[at], peer))

    place = to_slots()

    def one_band(band, carry):
        values = tok[pl.ds(pl.multiple_of(band * BAND, 16), BAND), :].astype(F32)
        hat, _ = norm_hat(values)
        normed = (hat * gains[0:1, :] + shifts[0:1, :]).astype(BF16)
        both = dot(place, jnp.concatenate([normed, hat.astype(BF16)], axis=1)).astype(BF16)
        xn_out[band] = both[:, :128]
        hat_out[band] = both[:, 128:]
        return carry

    def reduce(patches, conv, gain, shift, kv, out, at):
        red = dot(patches, conv) + shift[0:1, :]
        out[at : at + red.shape[0], :] = red
        hat, _ = norm_hat(red)
        normed = hat * gain[...] + shift[1:2, :]
        cdf, _ = gauss(normed)
        return dot((normed * cdf).astype(BF16), kv)

    kv_f_sw = swap_lanes(kv_f[...])
    part = bands // 2
    for first in (0, part):
        lax.fori_loop(first, first + part, one_band, 0, unroll=2)
        grid = xn_out[first : first + part].reshape(part, 16, 16, 128)
        patches = jnp.concatenate([fine_patch(grid, i) for i in range(4)], axis=1)
        pair = reduce(patches, conv_f[...], gain_f, shifts_f, kv_f_sw, red_f, first * FINE)
        pair = pair + keep_lanes(shifts_f[2:3, :], False)
        pair = jnp.where(cell_valid(pair.shape, 0), pair, 0.0).reshape(part, FINE, 128)
        slab[first : first + part, COARSE:CELLS, :] = pair
        send[first : first + part, COARSE:CELLS, :] = pair.astype(BF16)
        here = (pl.ds(first, part), pl.ds(COARSE, FINE))
        if first == 0:
            met(1)
        give(send.at[here], other.at[here])
        if first == 0:
            give(query_t, query_o)
    grid = xn_out[...].reshape(bands, 16, 16, 128)
    patches = jnp.concatenate([grid[:, i].reshape(bands * 16, 128) for i in range(16)], axis=1)
    pair = reduce(patches, conv_c[...], gain_c, shifts_c, kv_c[...], red_c, 0)
    pair = pair + keep_lanes(swap_lanes(shifts_c[2:3, :]), True)
    pair = jnp.where(cell_valid(pair.shape, 0), pair, 0.0).reshape(bands, COARSE, 128)
    slab[:, 0:COARSE, :] = pair
    send[:, 0:COARSE, :] = pair.astype(BF16)
    here = pl.ds(0, COARSE)
    give(send.at[:, here], other.at[:, here])
    band_tables(heights, table, meta, 2 * bands)
    for made in copies:
        made.wait()


def fine_slot(part, row, column):
    return (2 * row + (part >> 1)) * 4 + 2 * column + (part & 1)


def fine_patch(grid, part):
    bands = grid.shape[0]
    blocks = [
        grid[:, fine_slot(part, row, column)].reshape(bands, 1, 16, 128)
        for row in range(2)
        for column in range(2)
    ]
    return jnp.concatenate(blocks, axis=1).reshape(bands * FINE, 128)


def head_lanes(values, head):
    lane = lax.broadcasted_iota(jnp.int32, values.shape, 1)
    return jnp.where((lane >> 5) == head, values, jnp.zeros((), BF16))


def head_rows(values, head):
    row = lax.broadcasted_iota(jnp.int32, values.shape, 0)
    return jnp.where((row >> 5) == head, values, jnp.zeros((), BF16))


def score_rows(query_t, head, image, fine):
    row = lax.broadcasted_iota(jnp.int32, query_t.shape, 0)
    tag = row if fine else row - 64
    fill = jnp.where((tag >= 0) & (tag <= NOBODY) & (tag != image), BIG, 0.0).astype(BF16)
    return jnp.where((row >> 5) == head, query_t, fill)


def with_offset(rows, at, offset):
    start = at // 16 * 16
    block = rows[start : start + 16]
    row = lax.broadcasted_iota(jnp.int32, block.shape, 0)
    for i in range(3):
        term = offset.astype(BF16)
        block = jnp.where(row == at - start + i, term, block)
        offset = offset - term.astype(F32)
    parts = [rows[:start]] if start else []
    return jnp.concatenate(parts + [block, rows[start + 16 :]], axis=0)


def full_query(query_t, query_o, side):
    own, other = query_t[...].astype(F32), query_o[...].astype(F32)
    return jnp.where(
        side == 0,
        jnp.concatenate([own, other], axis=0),
        jnp.concatenate([other, own], axis=0),
    )


def window(ref, first):
    part = ref[pl.ds(first, MAX_BANDS)]
    return part.reshape(-1, 128).astype(BF16)


PACKED = 56
CHUNKS = ((0, 224), (224, 224), (448, 224), (672, 112))
HALVES = ((0, 8), (8, 6))
NOBODY = 32
ONES = 40


def tree_max(values):
    count = values.shape[0]
    while count % 16 == 0:
        count //= 2
        values = jnp.maximum(values[:count], values[count:])
    return jnp.max(values, axis=0, keepdims=True)


def attend_kernel(
    table, slab, other, meta, taps_c, taps_f, shifts_c, shifts_f, xn, tok, query_t, query_o, proj_w,
    gains, shifts, fc1, fc2, depth, hidden, cot,
    x1_out, xm_out, o_out, ot_out, lse_out, key_c, key_f, val_c, val_f, fc1_o, fc2_o, depth_o,
    hidden_o, cot_o,
    grid_ref, query_ref, place_ref, send_sems, recv_sems,
):
    step = pl.program_id(0)
    bands = slab.shape[0]
    total = 2 * bands
    side = lax.axis_index("heads")
    peer = across()
    halo = 2 * W
    edge = pl.multiple_of((1 - side) * (cot.shape[0] - halo), 16)
    swaps = [
        link(source, target, send_sems.at[i], recv_sems.at[i], peer)
        for i, (source, target) in enumerate(
            (
                (cot.at[pl.ds(edge, halo)], cot_o),
                (depth, depth_o),
                (hidden, hidden_o),
                (fc1, fc1_o),
                (fc2, fc2_o),
            )
        )
    ]

    @pl.when(step == 0)
    def _():
        greet(peer)
        place_ref[...] = from_slots()
        query_ref[...] = full_query(query_t, query_o, side).T.astype(BF16)
        grid_ref[0] = jnp.zeros((CELLS, 128), F32)
        grid_ref[total + 1] = jnp.zeros((CELLS, 128), F32)
        grid_ref[pl.ds(1 + side * bands, bands)] = slab[...]
        grid_ref[pl.ds(1 + (1 - side) * bands, bands)] = other[...].astype(F32)
        above, below, image = meta[0], meta[1], meta[2]
        lane = lax.broadcasted_iota(jnp.int32, (total, 16, 128), 2).astype(F32)
        valid = cell_valid((total, 16, 128), 1)
        wide = jnp.broadcast_to(image.reshape(total, 1, 8, 128), (total, 2, 8, 128))
        wide = wide.reshape(total, 16, 128)
        mark = jnp.where(valid & (wide >= 0.0), wide, float(NOBODY))

        ext = grid_ref[:, 0:COARSE, :]
        own = ext[1:-1]
        local = keep_lanes(shifts_c[2:3, :], True)
        mixed = own + depthwise_coarse(ext, above, below, pad_taps(taps_c[...], True)) + local
        val_c[...] = jnp.where(lane < 3.0, 1.0, mixed).astype(BF16)
        place = lane - 64.0
        one = (place >= ONES) & (place < ONES + 3)
        tag = jnp.where((place == mark) | one, 1.0, 0.0)
        keys = jnp.where(lane < 64.0, own, tag)
        key_c[...] = keys.astype(BF16)

        ext = grid_ref[:, COARSE:CELLS, :]
        local = keep_lanes(swap_lanes(shifts_f[2:3, :]), False)
        rows = depthwise_fine(ext, above, below, pad_taps(taps_f[...], False))
        tag = jnp.where((lane == mark) | ((lane >= ONES) & (lane < ONES + 3)), 1.0, 0.0)
        one = (lane >= 64.0) & (lane < 67.0)
        for row in range(2):
            for column in range(2):
                at = (2 * row + column) * 16
                own = ext[1:-1, at : at + 16, :]
                mixed = own + rows[row][column] + local
                cell = (2 * row + column) * 14
                val_f[:, cell : cell + 14, :] = jnp.where(one, 1.0, mixed)[:, 0:14]
                keys = jnp.where(lane >= 64.0, own.astype(BF16).astype(F32), tag)
                key_f[:, cell : cell + 14, :] = keys[:, 0:14]
        met(1)
        for swap in swaps:
            swap.start()

    each = xn.shape[0]
    images = [table[0, side * bands + each * step + i] for i in range(each)]
    firsts = [table[1, side * bands + each * step + i] for i in range(each)]
    queries = [
        dot(xn[i], query_ref[...]).astype(BF16).astype(F32).T.astype(BF16) for i in range(each)
    ]
    turned, windows = {}, {}

    def score(unit):
        i, head, part = unit
        fine = head >= 2
        start, size = CHUNKS[part]
        rows = slice(start, start + size)
        if not head & 1:
            if part == 0:
                windows[i, fine] = [
                    window(ref, firsts[i]) for ref in ((key_f, val_f) if fine else (key_c, val_c))
                ]
            turned[i, fine, part] = windows[i, fine][1][rows].T
        keys = windows[i, fine][0][rows]
        return dot(keys, score_rows(queries[i], head, images[i], fine))

    outs = [[None] * 4 for _ in range(each)]
    mixed = {}
    lse_out[...] = jnp.zeros(lse_out.shape, F32)

    def mix(unit, scores):
        i, head, part = unit
        fine = head >= 2
        top = tree_max(scores) * EXP_SCALE
        expo = jnp.exp2(scores * EXP_SCALE - top).astype(BF16)
        row = 32 * (head & 1) + (0 if fine else 64)
        vals = turned[i, fine, part][row : row + 32]
        left = jnp.concatenate([vals, jnp.ones((16, CHUNKS[part][1]), BF16)], axis=0)
        done = mixed.setdefault((i, head), [])
        done.append((top, dot(left, expo)))
        if len(done) < (4 if fine else 1):
            return
        top = functools.reduce(jnp.maximum, [part_top for part_top, _ in done])
        total = None
        for part_top, value in done:
            value = value * jnp.exp2(part_top - top)
            total = value if total is None else total + value
        sums = total[32:33]
        lse_out[i, head : head + 1, :] = top + jnp.log2(sums)
        outs[i][head] = total[0:32] * (1.0 / sums)

    waiting = []
    for i in range(each):
        for head, parts in ((2, 4), (0, 1), (3, 4), (1, 1)):
            for part in range(parts):
                waiting.append(((i, head, part), score((i, head, part))))
                if len(waiting) > 6:
                    mix(*waiting.pop(0))
    for unit, scores in waiting:
        mix(unit, scores)
    place = place_ref[...]
    for i in range(each):
        live = jnp.where(images[i] >= 0, 1.0, 0.0)
        out_t = jnp.concatenate(outs[i], axis=0) * live
        ot_out[i] = out_t
        heads_out = dot(place, out_t.T.astype(BF16)).astype(BF16)
        at = slice(i * BAND, (i + 1) * BAND)
        o_out[at, :] = heads_out
        middle = tok[at, :].astype(F32) + dot(heads_out, proj_w[...]) + shifts[1:2, :]
        x1_out[at, :] = middle
        hat, _ = norm_hat(middle)
        xm_out[at, :] = (hat * gains[1:2, :] + shifts[2:3, :]).astype(BF16)

    @pl.when(step == pl.num_programs(0) - 1)
    def _():
        for swap in swaps:
            swap.wait()


def shift_right(values):
    column = lax.broadcasted_iota(jnp.int32, values.shape, 0)
    return jnp.where(column == 0, 0.0, pltpu.roll(values, 1, 0))


def shift_left(values):
    column = lax.broadcasted_iota(jnp.int32, values.shape, 0)
    return jnp.where(column == W - 1, 0.0, pltpu.roll(values, W - 1, 0))


def mask_lanes():
    lane = lax.broadcasted_iota(jnp.int32, (W, 128), 1)
    column = lax.broadcasted_iota(jnp.int32, (W, 128), 0)
    tap = jnp.where(lane < 32, lane & 15, 15)
    parts = []
    for a in range(3):
        hit = tap == 3 * a + 1
        hit = hit | ((tap == 3 * a) & (column > 0)) | ((tap == 3 * a + 2) & (column < W - 1))
        if a == 1:
            hit = hit | (tap == TAPS)
        parts.append(jnp.where(hit, 1.0, 0.0))
    return parts


def hidden_kernel(
    table, x1_in, xm, cot, cot_o, heads_in, fc1, fc1_o, fc2, fc2_o, depth, depth_o, hidden, hidden_o,
    gains, shifts, proj_w,
    out, dx1_out, do_out, split_g, mid_g,
    xm_ext, halo_ref, moved, wide, wide_t, weights, weights_t, taps, bias, base_ref, fc2_t, dy, dy_t, act, du,
    sums, dxm, out_acc, x1, heads_out, send_sem, recv_sem, load_sems,
):
    side = lax.axis_index("heads")
    peer = across()
    tokens = x1.shape[0]
    rows = tokens // W
    bands = tokens // BAND
    halo = 2 * W
    extra = wide.shape[0] - tokens
    mine = fc1.shape[1]
    width = 2 * mine
    halo_at = pl.multiple_of((1 - side) * (halo + tokens), 16)
    halo_row = 1 + (1 - side) * (rows + 1)
    greet(peer)
    loads = fetch(((x1_in, x1), (heads_in, heads_out)), load_sems)
    edge = pl.multiple_of((1 - side) * (tokens - halo), 16)
    swap = link(xm.at[pl.ds(edge, halo)], halo_ref, send_sem, recv_sem, peer)

    def live_band(band):
        return jnp.where(table[0, band] >= 0, 1.0, 0.0)

    def neighbour(row):
        place = side * rows - 2 + row
        band = jnp.maximum(place, 0) >> 2
        up = jnp.where((place & 3) == 0, table[2, band], 1)
        down = jnp.where((place & 3) == 3, table[2, band + 1], 1)
        return up.astype(F32), down.astype(F32)

    xm_ext[0:halo, :] = jnp.zeros((halo, 128), BF16)
    xm_ext[halo + tokens : tokens + 2 * halo, :] = jnp.zeros((halo, 128), BF16)
    xm_ext[halo : halo + tokens, :] = xm[...]
    for band in range(bands):
        at = slice(band * BAND, (band + 1) * BAND)
        dy[at, :] = (cot[at, :].astype(F32) * live_band(side * bands + band)).astype(BF16)
    tail = cot_o[...].astype(F32)
    tail = jnp.where(side == 0, tail[:W], tail[W:]) * live_band((1 - side) * bands + side * (bands - 1))
    tail = jnp.concatenate([tail, jnp.zeros((extra - W, 128), F32)], axis=0)
    dy[tokens : tokens + extra, :] = tail.astype(BF16)

    taps[...] = jnp.zeros(taps.shape, F32)
    bias[...] = jnp.zeros(bias.shape, F32)
    for part, (taps_ref, shift_ref, fc1_ref, fc2_ref) in enumerate(
        ((depth, hidden, fc1, fc2), (depth_o, hidden_o, fc1_o, fc2_o))
    ):
        lanes = slice(part * mine, part * mine + mine)
        taps[0:TAPS, lanes] = taps_ref[...]
        taps[TAPS : TAPS + 1, lanes] = shift_ref[0:1, :]
        bias[0:TAPS, lanes] = taps_ref[...] * shift_ref[0:1, :]
        bias[TAPS : TAPS + 1, lanes] = shift_ref[0:1, :] + shift_ref[1:2, :]
        fc2_t[:, lanes] = fc2_ref[...].T
        base_ref[:, lanes] = fc1_ref[...]
        base = fc1_ref[...].astype(F32)
        for k in range(TAPS):
            factor = taps_ref[k : k + 1, :] + (1.0 if k == 4 else 0.0)
            weights[k * 128 : k * 128 + 128, lanes] = (base * (factor * ROOT)).astype(BF16)
    scaled = bias[...] * ROOT
    high = scaled.astype(BF16)
    weights[TAPS * 128 : TAPS * 128 + 16, :] = high
    weights[TAPS * 128 + 16 : TAPS * 128 + 32, :] = (scaled - high.astype(F32)).astype(BF16)
    weights[TAPS * 128 + 32 : WIDE, :] = jnp.zeros((96, width), BF16)

    met(1)
    swap.start()

    def move_rows(pair, carry):
        both = xm_ext[pl.ds(pl.multiple_of(pair * halo, 16), halo), :].astype(F32)
        for i in range(2):
            row = both[W * i : W * i + W]
            moved[0, 2 * pair + i] = shift_right(row)
            moved[1, 2 * pair + i] = row
            moved[2, 2 * pair + i] = shift_left(row)
        return carry

    lax.fori_loop(1, rows // 2 + 1, move_rows, 0, unroll=2)
    swap.wait()
    xm_ext[pl.ds(halo_at, halo), :] = halo_ref[...]
    move_rows(0, 0)
    move_rows(rows // 2 + 1, 0)

    masks = mask_lanes()

    def gather_row(row, block):
        up, down = neighbour(row)
        if block == TAPS:
            return masks[0] * up + masks[1] + masks[2] * down
        a, b = divmod(block, 3)
        values = moved[b, row + a - 1]
        return values if a == 1 else values * (up if a == 0 else down)

    inner = masks[0] + masks[1] + masks[2]

    def gather_band(band, carry):
        row = 2 + 4 * band
        up, _ = neighbour(row)
        _, down = neighbour(row + 3)
        for block in range(TAPS + 1):
            if block == TAPS:
                first = masks[0] * up + masks[1] + masks[2]
                last = masks[0] + masks[1] + masks[2] * down
                parts = [first, inner, inner, last]
            else:
                a, b = divmod(block, 3)
                parts = [moved[b, row + i + a - 1] for i in range(4)]
                if a == 0:
                    parts[0] = parts[0] * up
                elif a == 2:
                    parts[3] = parts[3] * down
            both = jnp.concatenate(parts, axis=0).astype(BF16)
            wide[pl.ds(pl.multiple_of(band * BAND, 16), BAND), block * 128 : block * 128 + 128] = both
        return carry

    lax.fori_loop(0, bands, gather_band, 0)
    for block in range(TAPS + 1):
        lanes = slice(block * 128, block * 128 + 128)
        tail = jnp.concatenate([gather_row(halo_row, block), jnp.zeros((extra - W, 128), F32)], axis=0)
        wide[tokens : tokens + extra, lanes] = tail.astype(BF16)

    def fc2_part(n):
        ref, at = (fc2, n * SPAN) if n * SPAN < mine else (fc2_o, n * SPAN - mine)
        return ref[at : at + SPAN, :]

    def one_block(at, own):
        total = None
        coming = dot(wide[at, :], weights[:, 0:SPAN])
        for n in range(width // SPAN):
            lanes = slice(n * SPAN, n * SPAN + SPAN)
            spread = coming
            if (n + 1) * SPAN < width:
                coming = dot(wide[at, :], weights[:, (n + 1) * SPAN : (n + 2) * SPAN])
            grad = dot(dy[at, :], fc2_t[:, lanes])
            bell = jnp.exp2(spread * spread * -LOG2E)
            share = 1.0 + lax.erf(spread)
            du[at, lanes] = (grad * (share + spread * bell * 1.1283791670955126)).astype(BF16)
            if own:
                active = (spread * share).astype(BF16)
                act[at, lanes] = active
                part = dot(active, fc2_part(n))
                total = part if total is None else total + part
        return total

    size = 896

    def own_block(block, carry):
        at = pl.ds(pl.multiple_of(block * size, 128), size)
        for part in range(TAPS + 1):
            kept = min(128, KEPT - part * 128)
            turned = wide[at, part * 128 : part * 128 + 128].T
            wide_t[part * 128 : part * 128 + kept, at] = turned[0:kept]
        dy_t[:, at] = dy[at, :].T
        out_acc[at, :] = one_block(at, True) * ROOT
        return carry

    lax.fori_loop(0, tokens // size, own_block, 0)
    one_block(slice(tokens, tokens + extra), False)

    def fold(half):
        lanes = pl.ds(pl.multiple_of(half * SPAN, SPAN), SPAN)
        base = base_ref[:, lanes].astype(F32)
        grad = sums[4 * 128 : 5 * 128, :]
        marks = sums[TAPS * 128 : KEPT, :]
        mean = marks[TAPS : TAPS + 1]
        bias_g = mean
        rows_g = []
        factors = taps[:, lanes]
        for k in range(TAPS):
            part = sums[k * 128 : k * 128 + 128, :]
            mark = marks[k : k + 1]
            factor = factors[k : k + 1]
            grad = grad + part * factor
            bias_g = bias_g + mark * factor
            rows_g.append(jnp.sum(part * base, axis=0, keepdims=True) + mark * factors[TAPS : TAPS + 1])
        rows_g = jnp.concatenate(rows_g + [bias_g, mean, jnp.zeros((5, SPAN), F32)], axis=0)
        for i in range(SPAN // 128):
            core, row = divmod(i, STEP // 128)
            piece = slice(i * 128, i * 128 + 128)
            split_g[half, core, row * 128 : row * 128 + 128, :] = grad[:, piece] * 0.5
            split_g[half, core, 512 + 16 * row : 528 + 16 * row, :] = rows_g[:, piece] * 0.5

    def gradients(half, carry):
        lanes = pl.ds(pl.multiple_of(half * SPAN, SPAN), SPAN)
        for part in (slice(0, 592), slice(592, KEPT)):
            sums[part, :] = dot(wide_t[part, :], du[0:tokens, lanes])
        turned = dot(dy_t[...], act[:, lanes]).T * ROOT
        for core in range(2):
            split_g[half, core, 256:512, :] = turned[core * STEP : core * STEP + STEP]
        for k in range(TAPS):
            weights_t[lanes, k * 128 : k * 128 + 128] = weights[k * 128 : k * 128 + 128, lanes].T
        fold(half)
        return carry

    lax.fori_loop(0, width // SPAN, gradients, 0)

    groups = ((4, 1, 7, 0), (3, 6, 2, 5), (8,))

    def collect_row(group, base, row):
        total = [None] * 3
        for i, k in enumerate(group):
            a, b = divmod(k, 3)
            source = row + 3 - a
            part = moved[base + i, source]
            if a != 1:
                up, down = neighbour(source)
                part = part * (up if a == 0 else down)
            total[b] = part if total[b] is None else total[b] + part
        if total[0] is not None:
            total[0] = shift_left(total[0])
        if total[2] is not None:
            total[2] = shift_right(total[2])
        total = functools.reduce(jnp.add, [part for part in total if part is not None])
        at = pl.ds(pl.multiple_of(row * W, 8), W)
        if group[0] == 4:
            dxm[at, :] = total
        else:
            dxm[at, :] += total

    for number, group in enumerate(groups):
        base = 4 * (number & 1)
        for i in range(len(group)):
            moved[base + i, 1] = jnp.zeros((W, 128), F32)
            moved[base + i, rows + 2] = jnp.zeros((W, 128), F32)

        def back(at):
            parts = [weights_t[:, k * 128 : k * 128 + 128] for k in group]
            return dot(du[at, :], jnp.concatenate(parts, axis=1))

        tail = back(slice(tokens, tokens + extra))
        for i in range(len(group)):
            moved[base + i, halo_row] = tail[0:W, i * 128 : i * 128 + 128]

        def back_block(block, carry):
            result = back(pl.ds(pl.multiple_of(block * 4 * BAND, 16), 4 * BAND))
            for i in range(len(group)):
                moved[base + i, pl.ds(2 + 16 * block, 16)] = result[
                    :, i * 128 : i * 128 + 128
                ].reshape(16, W, 128)
            if number:
                for i in range(16):
                    collect_row(groups[number - 1], 4 - base, 16 * block + i)
            return carry

        lax.fori_loop(0, bands // 4, back_block, 0)

    def last_rows(row, carry):
        collect_row(groups[-1], 4 * ((len(groups) - 1) & 1), row)
        return carry

    lax.fori_loop(0, rows, last_rows, 0, unroll=4)

    mid_g[...] = jnp.zeros(mid_g.shape, F32)
    for load in loads:
        load.wait()
    place = to_slots()
    proj = proj_w[...].astype(F32)
    proj_sw = jnp.concatenate([proj[64:], proj[:64]], axis=0).T.astype(BF16)

    def one_band(band, carry):
        at = pl.ds(pl.multiple_of(band * BAND, 16), BAND)
        live = live_band(side * bands + band)
        middle = x1[at, :]
        out[at, :] = ((middle + out_acc[at, :] + shifts[3:4, :]) * live).astype(BF16)
        hat, inverse = norm_hat(middle)
        grad = dxm[at, :] * ROOT
        grad_y = dy[at, :].astype(F32)
        dx1 = grad_y + norm_back(grad * gains[1:2, :], hat, inverse)
        dx1_out[at, :] = dx1
        dz = dx1.astype(BF16)
        mid_g[8:136, :] += dot_in(heads_out[at, :], dz)
        mid_g[0:1, :] += jnp.sum(grad * hat, axis=0, keepdims=True)
        mid_g[1:2, :] += jnp.sum(grad, axis=0, keepdims=True)
        mid_g[2:3, :] += jnp.sum(dz.astype(F32), axis=0, keepdims=True)
        mid_g[3:4, :] += jnp.sum(grad_y, axis=0, keepdims=True)
        do = (dot(dz, proj_sw) * live).astype(BF16)
        do_out[band] = dot(place, do).astype(BF16)
        return carry

    lax.fori_loop(0, bands, one_band, 0, unroll=2)


def stages(levels, shared):
    rest = list(range(2, levels))
    pairs = [rest[i : i + 2] for i in range(0, len(rest), 2)]
    return [[0], ["x", 1]] + pairs if shared else [[0], [1]] + pairs + [["x"]]


def group_size(levels, rows):
    unit = 16 * 2 ** (levels - 1)
    return -(-rows // unit) * unit


def stage_shapes(levels, shared, rows):
    halves, shapes = 2, [(1, 2, rows, 128)]
    for dims in stages(levels, shared)[1:]:
        if "x" in dims:
            halves = 1
        rows >>= sum(1 for dim in dims if dim != "x")
        shapes.append((2 ** len(dims) - 1, halves, rows, 128))
    return shapes


def group_scratch(levels, shared, rows):
    buffers = [pltpu.VMEM(part, BF16) for part in stage_shapes(levels, shared, rows)]
    return [pltpu.VMEM((2, rows, 128), F32)] + buffers + buffers


def group_links(levels, shared):
    return sum(2 ** len(dims) - 1 for dims in stages(levels, shared))


def everyone(levels):
    batch, side = lax.axis_index("batch"), lax.axis_index("heads")
    peers = []
    for dims in stages(levels, True):
        for flips in range(1, 2 ** len(dims)):
            peers.append(flipped(batch, side, dims, flips))
    return peers


def flipped(batch, side, dims, flips):
    for i, dim in enumerate(dims):
        if flips >> i & 1:
            if dim == "x":
                side = 1 - side
            else:
                batch = batch + (1 - 2 * ((batch // 2**dim) % 2)) * 2**dim
    return batch, side


class Group:
    def __init__(self, levels, shared, buffers, sems, base):
        self.stages = stages(levels, shared)
        count = len(self.stages)
        self.cur, self.sends, self.recvs = buffers[0], buffers[1 : 1 + count], buffers[1 + count :]
        self.sems, self.base = sems, base
        self.batch, self.side = lax.axis_index("batch"), lax.axis_index("heads")
        self.core = self.batch % 2
        at, rows = 0, self.cur.shape[1]
        self.kept, self.given = [(at, rows)], [None]
        for dims in self.stages[1:]:
            bits = [dim for dim in dims if dim != "x"]
            starts = []
            for flips in range(2 ** len(dims)):
                batch, _ = flipped(self.batch, self.side, dims, flips)
                start = at
                for i, bit in enumerate(bits):
                    start = start + ((batch // 2**bit) % 2) * (rows >> (i + 1))
                starts.append(pl.multiple_of(start, 16))
            rows >>= len(bits)
            at = starts[0]
            self.kept.append((at, rows))
            self.given.append(starts)
        self.left = list(range(count))

    def link(self, stage, flips):
        number = self.base + sum(2 ** len(part) - 1 for part in self.stages[:stage]) + flips - 1
        peer = flipped(self.batch, self.side, self.stages[stage], flips)
        source, target = self.sends[stage].at[flips - 1], self.recvs[stage].at[flips - 1]
        return link(source, target, self.sems[0].at[number], self.sems[1].at[number], peer)

    def wait(self, stage):
        for flips in range(1, 2 ** len(self.stages[stage])):
            self.link(stage, flips).wait()

    def add(self, stage):
        at, rows = self.kept[stage]
        here, recv = pl.ds(at, rows), self.recvs[stage]
        if recv.shape[1] == 2:
            total = self.cur[:, here, :]
            for i in range(recv.shape[0]):
                total = total + recv[i].astype(F32)
            self.cur[:, here, :] = total
            return
        total = self.cur[self.side, here, :]
        for i in range(recv.shape[0]):
            total = total + recv[i, 0].astype(F32)
        self.cur[self.side, here, :] = total

    def advance(self, count=1, pieces=None):
        for number in self.left[:count]:
            self.phase(number, pieces)
        del self.left[:count]

    def phase(self, number, pieces):
        count = len(self.stages)
        if number == 0:
            for half in range(2):
                for row, value in pieces(half, 1 - self.core):
                    self.sends[0][0, half, row : row + value.shape[0], :] = value.astype(BF16)
            self.link(0, 1).start()
            for half in range(2):
                for row, value in pieces(half, self.core):
                    self.cur[half, row : row + value.shape[0], :] = value
        else:
            self.wait(number - 1)
            self.add(number - 1)
            dims = self.stages[number]
            _, rows = self.kept[number]
            for flips in range(1, 2 ** len(dims)):
                crossing = "x" in dims and flips >> dims.index("x") & 1
                here = pl.ds(self.given[number][flips], rows)
                if self.sends[number].shape[1] == 2:
                    self.sends[number][flips - 1] = self.cur[:, here, :].astype(BF16)
                else:
                    half = 1 - self.side if crossing else self.side
                    self.sends[number][flips - 1, 0] = self.cur[half, here, :].astype(BF16)
                self.link(number, flips).start()

    def finish(self):
        self.wait(len(self.stages) - 1)
        self.add(len(self.stages) - 1)
        at, rows = self.kept[-1]
        return self.cur[self.side, pl.ds(at, rows), :].astype(BF16)


class Gather:
    def __init__(self, levels, out, shared, sems, base):
        self.stages, self.out, self.shared = stages(levels, True), out, shared
        self.sems, self.base = sems, base
        self.batch, self.side = lax.axis_index("batch"), lax.axis_index("heads")
        self.core = self.batch % 2
        at, count = 0, out.shape[2]
        self.kept = [(at, count)]
        for dims in self.stages[1:]:
            for bit in dims:
                if bit != "x":
                    count //= 2
                    at = at + ((self.batch // 2**bit) % 2) * count
            self.kept.append((at, count))
        self.left = list(range(len(self.stages)))

    def links(self, stage):
        dims = self.stages[stage]
        at, count = self.kept[stage]
        number = self.base + sum(2 ** len(part) for part in self.stages[:stage])
        mine = self.out.at[self.core, self.side, pl.ds(at, count)]
        for flips in range(1, 2 ** len(dims)):
            part = mine
            if "x" in dims and flips >> dims.index("x") & 1:
                part = self.out.at[self.core, self.side, pl.ds(at, count), pl.ds(0, self.shared)]
            yield self.made(part, number, flipped(self.batch, self.side, dims, flips))
            number += 1
        if stage == 0:
            part = self.out.at[self.core, 1 - self.side, :, pl.ds(0, self.shared)]
            yield self.made(part, number, flipped(self.batch, self.side, dims, 1))

    def made(self, part, number, peer):
        return link(part, part, self.sems[0].at[number], self.sems[1].at[number], peer)

    def begin(self, pieces):
        at, _ = self.kept[-1]
        row = 0
        for piece in pieces:
            self.out[self.core, self.side, at, row : row + piece.shape[0], :] = piece
            row += piece.shape[0]
        for made in self.links(len(self.stages) - 1):
            made.start()

    def advance(self):
        stage = len(self.left) - 1
        for made in self.links(stage):
            made.wait()
        if stage:
            for made in self.links(stage - 1):
                made.start()
        del self.left[-1]


def attend_back_kernel(
    table, key_c, key_f, val_c, val_f, xn, query_t, query_o, do_ref, ot_ref, lse, output,
    dq_out, own_out, send_out, output_out,
    acc_c, acc_f, query_ref, turned_c, turned_f, keys_ref, vals_ref, kept,
):
    step = pl.program_id(0)
    each = xn.shape[0]
    bands = each * pl.num_programs(0)
    side = lax.axis_index("heads")

    @pl.when(step == 0)
    def _():
        acc_c[...] = jnp.zeros(acc_c.shape, F32)
        acc_f[...] = jnp.zeros(acc_f.shape, F32)
        query_ref[...] = full_query(query_t, query_o, side).T.astype(BF16)

    output_out[...] = output[...]
    firsts = [table[1, side * bands + each * step + i] for i in range(each)]
    for i in range(each):

        @pl.when((step == 0) | (kept[i] != firsts[i]))
        def _():
            kept[i] = firsts[i]
            keys = window(key_f, firsts[i])
            keys_ref[i] = keys
            vals_ref[i] = window(val_f, firsts[i])
            for part, (start, count) in enumerate(HALVES):
                rows = slice(start * PACKED, (start + count) * PACKED)
                turned_f[i, part, :, 0 : count * PACKED] = keys[rows].T[64:128]
            turned_c[i] = window(key_c, firsts[i]).T[0:64]

    queries, query_rows, grads_t, grads_low = [], [], [], []
    for i in range(each):
        query = dot(xn[i], query_ref[...]).astype(BF16)
        queries.append(query)
        query_rows.append(query.astype(F32).T.astype(BF16))
        grads_t.append(do_ref[i].astype(F32).T)
        grads_low.append(grads_t[i].astype(BF16))
    dq = [[None] * 4 for _ in range(each)]

    def products(unit):
        i, head, part = unit
        fine = head >= 2
        image = table[0, side * bands + each * step + i]
        start, count = HALVES[part]
        if fine:
            rows = slice(start * PACKED, (start + count) * PACKED)
            keys, vals = keys_ref[i, rows], vals_ref[i, rows]
        else:
            keys, vals = window(key_c, firsts[i]), window(val_c, firsts[i])
        swapped = (head + 2) & 3
        delta = jnp.sum(
            ot_ref[i, 32 * head : 32 * head + 32]
            * grads_t[i][32 * swapped : 32 * swapped + 32],
            axis=0,
            keepdims=True,
        )
        offset = lse[i, head : head + 1, :] * (-1.0 / EXP_SCALE)
        left = score_rows(query_rows[i], head, image, fine)
        left = with_offset(left, ONES + (0 if fine else 64), offset)
        right = with_offset(head_rows(grads_low[i], swapped), 64 if fine else 0, -delta)
        return dot(keys, left), dot(vals, right)

    held = {}

    def back(unit, score, prob_grad):
        i, head, part = unit
        fine = head >= 2
        swapped = (head + 2) & 3
        prob = jnp.exp2(score * EXP_SCALE)
        score_grad = (prob * prob_grad).astype(BF16)
        row = 32 * (head & 1)
        start, count = HALVES[part]
        turned = turned_c[i, row : row + 32]
        if fine:
            turned = turned_f[i, part, row : row + 32, 0 : count * PACKED]
        grad = dot(turned, score_grad)
        dq[i][head] = grad if part == 0 else dq[i][head] + grad
        pair = held.setdefault((i, fine, part), ([], []))
        pair[0].extend([score_grad, prob.astype(BF16)])
        pair[1].extend([head_lanes(queries[i], head), head_lanes(do_ref[i], swapped)])
        if head & 1:
            both = dot(jnp.concatenate(pair[0], axis=1), jnp.concatenate(pair[1], axis=0))
            if fine:
                at = pl.ds(firsts[i] + start, count)
                acc_f[at, 0:PACKED, :] += both.reshape(count, PACKED, 128)
            else:
                acc_c[pl.ds(firsts[i], MAX_BANDS)] += both.reshape(MAX_BANDS, COARSE, 128)

    waiting = []
    for i in range(each):
        for head, parts in ((2, 2), (3, 2), (0, 1), (1, 1)):
            for part in range(parts):
                waiting.append(((i, head, part), *products((i, head, part))))
                if len(waiting) > 3:
                    back(*waiting.pop(0))
    for unit in waiting:
        back(*unit)
    for i in range(each):
        dq_out[i] = (jnp.concatenate(dq[i], axis=0).T * SCALE).astype(BF16)

    @pl.when(step == pl.num_programs(0) - 1)
    def _():
        span = bands + 1
        lane = lax.broadcasted_iota(jnp.int32, (1, 128), 1)
        scale_c = jnp.where(lane < 64, SCALE, 1.0)
        scale_f = jnp.where(lane < 64, 1.0, SCALE)
        for dest, at, kind in (
            (own_out, side * (bands - 1), F32),
            (send_out, (1 - side) * (bands - 1), BF16),
        ):
            dest[:, 0:COARSE, :] = (acc_c[pl.ds(at, span)] * scale_c).astype(kind)
            for cell in range(4):
                part = acc_f[pl.ds(at, span), 14 * cell : 14 * cell + 16, :] * scale_f
                part = jnp.where(cell_valid(part.shape, 1), part, 0.0)
                row = COARSE + 16 * cell
                dest[:, row : row + 16, :] = part.astype(kind)


def tail_kernel(
    levels, own_in, given, split_in, mid_g, slab_in, other, meta, xn_in, hat_in, dq_in, query_t,
    query_o, dx1_in, tok_in, gains,
    red_c_in, conv_c_in, gain_c, shifts_c, kv_c, taps_c_ref,
    red_f_in, conv_f_in, gain_f, shifts_f, kv_f, taps_f_ref,
    tok_grad, joint, little,
    pack, small, small_in, small_sems, recv, grad_ref, val_ref, dxn, send_sem, recv_sem, send_sems, recv_sems, turned_c, turned_f,
    dx1, tok, hat_ref, own, split_g, slab, xn, dq, red_c, conv_c, red_f, conv_f, xt, load_sems,
    *buffers,
):
    bands = xn.shape[0]
    side = lax.axis_index("heads")
    greet(*everyone(levels))
    early_pairs = (
        (split_in, split_g), (dq_in, dq), (xn_in, xn), (own_in, own), (slab_in, slab),
        (conv_c_in, conv_c), (conv_f_in, conv_f),
    )
    loads = fetch(early_pairs, load_sems)
    met(len(everyone(levels)))
    swaps = [
        remote(given.at[:, here], recv.at[:, here], send_sem.at[i], recv_sem.at[i], across())
        for i, here in enumerate((pl.ds(0, COARSE), pl.ds(COARSE, FINE)))
    ]
    late_pairs = (
        (red_c_in, red_c), (red_f_in, red_f), (hat_in, hat_ref), (tok_in, tok), (dx1_in, dx1),
    )
    loads += fetch(late_pairs, load_sems.at[pl.ds(len(early_pairs), len(late_pairs))])
    sems = (send_sems, recv_sems)
    split_count, shared_count = (1 + 2 * len(stages(levels, shared)) for shared in (False, True))
    before = Group(levels, False, buffers[:split_count], sems, 0)
    base = group_links(levels, False)
    buffers = buffers[split_count:]
    conv = Group(levels, True, buffers[:shared_count], sems, base)
    base += group_links(levels, True)
    rest = Group(levels, True, buffers[shared_count:], sems, base)
    base += group_links(levels, True)
    early_rows, late_rows, later_rows = (group.cur.shape[1] for group in (before, conv, rest))
    gather = Gather(levels, joint, (late_rows + later_rows) // joint.shape[2], sems, base)

    def split_pieces(half, which):
        yield 0, split_g[(half + side) % 2, which]
        if early_rows > SPLIT:
            yield SPLIT, jnp.zeros((early_rows - SPLIT, 128), F32)

    def shared_pieces(first, used, rows):
        def pieces(half, which):
            at = pl.multiple_of(first + used * (2 * half + which), 16)
            yield 0, pack[pl.ds(at, used), :]
            if rows > used:
                yield used, jnp.zeros((rows - used, 128), F32)

        return pieces

    batch, order = lax.axis_index("batch"), stages(levels, True)

    def small_links(stage):
        before = sum(2 ** len(dims) - 1 for dims in order[:stage])
        for flips in range(1, 2 ** len(order[stage])):
            at = before + flips - 1
            yield at, link(
                small.at[stage], small_in.at[at], small_sems.at[0, at], small_sems.at[1, at],
                flipped(batch, side, order[stage], flips),
            )

    def small_phase(stage):
        if stage:
            total = small[stage - 1]
            for at, made in small_links(stage - 1):
                made.wait()
                total = total + small_in[at]
            if stage == len(order):
                little[...] = total
                return
            small[stage] = total
        for _, made in small_links(stage):
            made.start()

    for load in loads[:7]:
        load.wait()
    before.advance(1, split_pieces)

    start = 0
    parts = []
    for count in (conv_c.shape[0], conv_f.shape[0], 128, 128, 128, 128):
        parts.append(pack.at[start : start + count])
        start += count
    conv_c_g, conv_f_g, kv_c_g, kv_f_g, query_g, proj_g = parts
    small_c, small_f, front_g = small.at[0, 0:16], small.at[0, 16:32], small.at[0, 32:40]
    small[0, 40:48, :] = mid_g[0:8, :]
    proj_g[...] = mid_g[8:136, :]
    taps_c, taps_f = pad_taps(taps_c_ref[...], True), pad_taps(taps_f_ref[...], False)
    kv_f_sw = swap_lanes(kv_f[...])

    val_ref[0] = jnp.zeros((CELLS, 128), F32)
    val_ref[bands + 1] = jnp.zeros((CELLS, 128), F32)
    val_ref[1 : bands + 1] = slab[...]
    val_ref[pl.ds((1 - side) * (bands + 1), 1)] = other[
        pl.ds(side * (bands - 1), 1)
    ].astype(F32)
    at = pl.ds(side * bands, bands)
    above, below = meta[0, at], meta[1, at]
    grid = xn[...].reshape(bands, 16, 16, 128)
    slot_grads = dq[...].reshape(bands, 16, 16, 128)
    total = None
    for i in range(16):
        turned = grid[:, i].reshape(bands * 16, 128).T
        xt[i] = turned
        part = dot(turned, slot_grads[:, i].reshape(bands * 16, 128))
        total = part if total is None else total + part
    query_g[...] = total
    full = full_query(query_t, query_o, side).astype(BF16)
    dxn[...] = dot(dq[...].reshape(-1, 128), full).reshape(bands, SLOTS, 128)
    grad_ref[0] = jnp.zeros((CELLS, 128), F32)
    grad_ref[bands + 1] = jnp.zeros((CELLS, 128), F32)
    turned_c[...] = conv_c[...].T
    turned_f[...] = conv_f[...].T
    before.advance()
    swaps[0].wait()
    here = pl.ds(1 - side, bands + 1)
    for load in loads[7:]:
        load.wait()
    grad_ref[here, 0:COARSE] = own[:, 0:COARSE] + recv[:, 0:COARSE].astype(F32)
    lane = lax.broadcasted_iota(jnp.int32, (1, 1, 128), 2)

    def tap_sum(values, grads):
        return fold_rows(values * grads)

    def reduce_back(pair, red, conv, gain, shifts, kv, small, kv_g):
        hat, inverse = norm_hat(red[...])
        normed = hat * gain[...] + shifts[1:2, :]
        cdf, bell = gauss(normed)
        active = (normed * cdf).astype(BF16)
        kv_g[...] = dot_in(active, pair)
        small[9:10, :] = jnp.sum(pair.astype(F32), axis=0, keepdims=True)
        grad = dot_t(pair, kv) * gelu_slope(normed, cdf, bell)
        small[11:12, :] = jnp.sum(grad * hat, axis=0, keepdims=True)
        small[12:13, :] = jnp.sum(grad, axis=0, keepdims=True)
        dc = norm_back(grad * gain[...], hat, inverse).astype(BF16)
        small[13:14, :] = jnp.sum(dc.astype(F32), axis=0, keepdims=True)
        return dc

    small_c[...] = jnp.zeros(small_c.shape, F32)
    small_f[...] = jnp.zeros(small_f.shape, F32)

    vals = val_ref[:, 0:COARSE, :]
    ext = grad_ref[:, 0:COARSE, :]
    ext = jnp.where(lane < 64, ext, ext.astype(BF16).astype(F32))
    mid = ext[1:-1]
    near = (by_band(vals[:-2], above), vals[1:-1], by_band(vals[2:], below))
    for a in range(3):
        for b in range(3):
            moved = near[a] if b == 1 else roll_cells(near[a], 1 - b)
            small_c[3 * a + b : 3 * a + b + 1, :] = jnp.sum(
                tap_sum(moved, mid), axis=0, keepdims=True
            )
    small_c[10:11, :] = jnp.sum(mid.reshape(-1, 128), axis=0, keepdims=True)
    pair = mid + depthwise_coarse(ext, above, below, taps_c, flip=True)
    pair = jnp.where(cell_valid(pair.shape, 1), pair, 0.0)
    pair = pair.reshape(bands * COARSE, 128).astype(BF16)
    dc = reduce_back(pair, red_c, conv_c, gain_c, shifts_c, kv_c[...], small_c, kv_c_g)
    for i in range(16):
        part = slice(i * 128, (i + 1) * 128)
        conv_c_g[part, :] = dot(xt[i], dc)
        back = dot(dc, turned_c[:, part]).reshape(bands, 16, 128)
        dxn[:, 16 * i : 16 * i + 16, :] += back

    conv.advance(1, shared_pieces(0, CONV, late_rows))
    before.advance()
    swaps[1].wait()
    grad_ref[here, COARSE:CELLS] = own[:, COARSE:CELLS] + recv[:, COARSE:CELLS].astype(F32)
    vals = val_ref[:, COARSE:CELLS, :]
    ext = grad_ref[:, COARSE:CELLS, :]
    ext = jnp.where(lane >= 64, ext, ext.astype(BF16).astype(F32))
    rows = depthwise_fine(ext, above, below, taps_f, flip=True)
    near = fine_rows(vals, above, below)
    mids = fine_rows(ext, above, below)[1]
    for a in range(3):
        for b in range(3):
            total = jnp.zeros((8, 128), F32)
            for row in range(2):
                even, odd = near[a][row][:, 0], near[a][row][:, 1]
                grad_even, grad_odd = mids[row][:, 0], mids[row][:, 1]
                if b == 0:
                    moved = (roll_cells(odd, 1), even)
                elif b == 1:
                    moved = (even, odd)
                else:
                    moved = (odd, roll_cells(even, -1))
                total = total + tap_sum(moved[0], grad_even) + tap_sum(moved[1], grad_odd)
            small_f[3 * a + b : 3 * a + b + 1, :] = jnp.sum(total, axis=0, keepdims=True)
    small_f[10:11, :] = jnp.sum(ext[1:-1].reshape(-1, 128), axis=0, keepdims=True)
    valid = cell_valid((bands, 16, 128), 1)
    blocks = []
    for row in range(2):
        for column in range(2):
            block = jnp.where(valid, mids[row][:, column] + rows[row][column], 0.0)
            blocks.append(block.astype(BF16).reshape(bands, 1, 16, 128))
    pair = jnp.concatenate(blocks, axis=1).reshape(bands * FINE, 128)
    conv.advance()
    dc = reduce_back(pair, red_f, conv_f, gain_f, shifts_f, kv_f_sw, small_f, kv_f_g)
    for i in range(4):
        part = slice(i * 128, (i + 1) * 128)
        total = None
        for row in range(2):
            for column in range(2):
                cells = dc.reshape(bands, 4, 16, 128)[:, 2 * row + column].reshape(bands * 16, 128)
                product = dot(xt[fine_slot(i, row, column)], cells)
                total = product if total is None else total + product
        conv_f_g[part, :] = total
        back = dot(dc, turned_f[:, part]).reshape(bands, 4, 16, 128)
        for row in range(2):
            for column in range(2):
                slot = 16 * fine_slot(i, row, column)
                dxn[:, slot : slot + 16, :] += back[:, 2 * row + column]

    front_g[...] = jnp.zeros(front_g.shape, F32)
    sums = jnp.zeros((8, 128), F32)
    along = jnp.zeros((8, 128), F32)
    for band in range(bands):
        grad = dxn[band]
        sums = sums + fold_rows(grad)
        along = along + fold_rows(grad * hat_ref[band].astype(F32))
    front_g[0:1, :] = jnp.sum(along, axis=0, keepdims=True)
    front_g[1:2, :] = jnp.sum(sums, axis=0, keepdims=True)

    small_phase(0)
    rest.advance(1, shared_pieces(4 * CONV, REST, later_rows))
    conv.advance()
    before.advance()
    place = from_slots()

    def one_band(band):
        at = slice(band * BAND, (band + 1) * BAND)
        grad = dxn[band]
        high = grad.astype(BF16)
        low = (grad - high.astype(F32)).astype(BF16)
        grad = dot(place, jnp.concatenate([high, low], axis=1))
        grad = grad[:, :128] + grad[:, 128:]
        hat, inverse = norm_hat(tok[at, :].astype(F32))
        tok_grad[at, :] = dx1[at, :] + norm_back(grad * gains[0:1, :], hat, inverse)

    done, total = 0, len(rest.left) + 1 + len(gather.left)
    for number in range(1, total + 1):
        while done < bands and done * total < number * bands:
            one_band(done)
            done += 1
        if rest.left:
            rest.advance()
            conv.advance()
            before.advance()
        elif number + len(gather.left) == total:
            conv.advance(len(conv.left))
            before.advance(len(before.left))
            gather.begin([conv.finish(), rest.finish(), before.finish()])
        else:
            gather.advance()
        if number <= len(order):
            small_phase(number)


def shared_rows(start, count):
    done = 0
    while done < count:
        group = 0 if start + done < 4 * CONV else 1
        if group == 0:
            quarter, row = divmod(start + done, CONV)
            size = min(count - done, CONV - row)
        else:
            quarter, row = divmod(start + done - 4 * CONV, REST)
            size = min(count - done, REST - row)
        yield group, quarter % 2, quarter // 2, row, done, size
        done += size


def unpack_kernel(
    levels,     joint, little, tok_grad,
    tok_grad_out, gains, shifts, query, conv_c, gain_c, shifts_c, kv_c, taps_c, conv_f, gain_f, shifts_f, kv_f,
    taps_f, proj, hidden, fc1, depth, fc2,
):
    side = lax.axis_index("heads")
    half = query.shape[0]
    pieces, wide = joint.shape[2], fc2.shape[0]
    widths = [group_size(levels, part) // pieces for part in (CONV, REST, SPLIT)]
    first, second = widths[0], widths[0] + widths[1]
    spans = (slice(0, first), slice(first, second), slice(second, second + widths[2]))

    def quarter_rows(group, core, h):
        return joint[core, h, :, spans[group], :].reshape(-1, 128)

    tok_grad_out[...] = tok_grad[...]

    def rows_of(start, count):
        pieces = [
            quarter_rows(group, core, h)[at : at + size].astype(F32)
            for group, core, h, at, _, size in shared_rows(start, count)
        ]
        return pieces[0] if len(pieces) == 1 else jnp.concatenate(pieces, axis=0)

    start = 0
    for ref in (conv_c, conv_f, kv_c):
        count = ref.shape[0]
        for group, core, h, at, offset, size in shared_rows(start, count):
            ref[offset : offset + size, :] = quarter_rows(group, core, h)[at : at + size].astype(F32)
        start += count
    kv_f[...] = swap_lanes(rows_of(start, 128))
    both = rows_of(start + 128, 128)
    query[...] = jnp.where(side == 0, both[:, :half], both[:, half:]).T
    proj[...] = rows_of(start + 256, 128)
    small = little[...]
    coarse, fine, front, mid = small[0:16], small[16:32], small[32:40], small[40:48]
    taps_c[...] = coarse[0:9, half:]
    taps_f[...] = fine[0:9, :half]
    gain_c[...] = coarse[11:12]
    gain_f[...] = fine[11:12]
    shifts_c[0:1, :] = coarse[13:14]
    shifts_c[1:2, :] = coarse[12:13]
    shifts_c[2:3, :] = jnp.concatenate([coarse[9:10, half:], coarse[10:11, half:]], axis=1)
    shifts_f[0:1, :] = fine[13:14]
    shifts_f[1:2, :] = fine[12:13]
    shifts_f[2:3, :] = jnp.concatenate([fine[9:10, :half], fine[10:11, :half]], axis=1)
    gains[0:1, :] = front[0:1]
    gains[1:2, :] = mid[0:1]
    shifts[0:1, :] = front[1:2]
    shifts[1:2, :] = mid[2:3]
    shifts[2:3, :] = mid[1:2]
    shifts[3:4, :] = mid[3:4]
    for core in range(2):
        split = quarter_rows(2, core, side)
        for i in range(2):
            lanes = slice(core * STEP + i * 128, core * STEP + i * 128 + 128)
            fc1[:, lanes] = split[i * 128 : i * 128 + 128].astype(F32)
            block = split[512 + 16 * i : 528 + 16 * i].astype(F32)
            depth[:, lanes] = block[0:9]
            hidden[:, lanes] = block[9:11]
        fc2[core * STEP : core * STEP + STEP, :] = split[256:512].astype(F32)


SMEM = pl.BlockSpec(memory_space=pltpu.SMEM)
VMEM = pl.BlockSpec(memory_space=pltpu.VMEM)
HBM = pl.BlockSpec(memory_space=pl.ANY)


def shape(dims, kind=F32):
    return jax.ShapeDtypeStruct(dims, kind)


def params(limit=56):
    return pltpu.CompilerParams(vmem_limit_bytes=limit * MIB)


def sending(number, limit=56):
    return pltpu.CompilerParams(
        vmem_limit_bytes=limit * MIB, collective_id=number, has_side_effects=True
    )


def per_device(
    size, tokens, image_bands, cotangent, front_gains, front_shifts, query_w, coarse_conv,
    coarse_gain, coarse_shifts, coarse_kv, coarse_taps, fine_conv, fine_gain, fine_shifts, fine_kv,
    fine_taps, proj_w, hidden_shifts, fc1_w, depth_taps, fc2_w,
):
    count = tokens.shape[0]
    rows = count // W
    bands = count // BAND
    total = 2 * bands
    halo = 2 * W
    half = coarse_kv.shape[1] // 2
    mine = fc1_w.shape[1]
    hidden = 2 * mine
    gain_c, gain_f = coarse_gain[None], fine_gain[None]
    semaphores = pltpu.SemaphoreType.DMA
    levels = size.bit_length() - 1
    query_t = query_w.T

    (
        table, meta, xn, hat, red_c, red_f, slab, other, query_o,
    ) = pl.pallas_call(
        front_kernel,
        out_shape=(
            shape((3, 32), jnp.int32),
            shape((3, total, 8, 128)),
            shape((bands, SLOTS, 128), BF16),
            shape((bands, SLOTS, 128), BF16),
            shape((bands * COARSE, 128)),
            shape((bands * FINE, 128)),
            shape((bands, CELLS, 128)),
            shape((bands, CELLS, 128), BF16),
            shape(query_t.shape, BF16),
        ),
        in_specs=[SMEM] + [VMEM] * 12,
        out_specs=[SMEM] + [VMEM] * 8,
        scratch_shapes=[pltpu.VMEM((bands, CELLS, 128), BF16), semaphores((8,)), semaphores((8,))],
        compiler_params=sending(1),
        name="front",
    )(
        image_bands, tokens, front_gains, front_shifts, coarse_conv, gain_c, coarse_shifts,
        coarse_kv, fine_conv, gain_f, fine_shifts, fine_kv,
        query_t,
    )

    each = 4 if bands % 4 == 0 else 2
    some_bands = pl.BlockSpec((each * BAND, 128), lambda i: (i, 0))
    some_slots = pl.BlockSpec((each, SLOTS, 128), lambda i: (i, 0, 0))
    two_slots = pl.BlockSpec((2, SLOTS, 128), lambda i: (i, 0, 0))
    (
        x1, xm, heads_out, out_t, lse, key_c, key_f, val_c, val_f, fc1_o, fc2_o, depth_o, hidden_o,
        cot_o,
    ) = pl.pallas_call(
        attend_kernel,
        grid=(bands // each,),
        out_shape=(
            shape((count, 128)),
            shape((count, 128), BF16),
            shape((count, 128), BF16),
            shape((bands, 128, SLOTS)),
            shape((bands, 8, SLOTS)),
            shape((total, COARSE, 128), BF16),
            shape((total, PACKED, 128)),
            shape((total, COARSE, 128), BF16),
            shape((total, PACKED, 128)),
            shape(fc1_w.shape, BF16),
            shape(fc2_w.shape, BF16),
            shape(depth_taps.shape),
            shape(hidden_shifts.shape),
            shape((halo, 128), BF16),
        ),
        in_specs=[SMEM] + [VMEM] * 7 + [some_slots, some_bands] + [VMEM] * 5 + [HBM] * 5,
        out_specs=[
            some_bands,
            some_bands,
            some_bands,
            pl.BlockSpec((each, 128, SLOTS), lambda i: (i, 0, 0)),
            pl.BlockSpec((each, 8, SLOTS), lambda i: (i, 0, 0)),
        ]
        + [VMEM] * 4
        + [HBM] * 5,
        scratch_shapes=[
            pltpu.VMEM((total + 2, CELLS, 128), F32),
            pltpu.VMEM((128, 128), BF16),
            pltpu.VMEM((BAND, SLOTS), BF16),
            semaphores((5,)),
            semaphores((5,)),
        ],
        compiler_params=sending(4),
        name="attend",
    )(
        table, slab, other, meta, coarse_taps, fine_taps, coarse_shifts, fine_shifts, xn, tokens,
        query_t, query_o, proj_w, front_gains, front_shifts, fc1_w, fc2_w, depth_taps,
        hidden_shifts, cotangent,
    )

    extra = 64
    output, dx1, out_grad, split_g, mid_g = pl.pallas_call(
        hidden_kernel,
        out_shape=(
            shape((count, 128), BF16),
            shape((count, 128)),
            shape((bands, SLOTS, 128), BF16),
            shape((2, 2, SPLIT, 128)),
            shape((136, 128)),
        ),
        in_specs=[SMEM, HBM] + [VMEM] * 3 + [HBM] + [VMEM] * 11,
        out_specs=[VMEM] * 5,
        scratch_shapes=[
            pltpu.VMEM((count + 2 * halo, 128), BF16),
            pltpu.VMEM((halo, 128), BF16),
            pltpu.VMEM((8, rows + 4, W, 128), F32),
            pltpu.VMEM((count + extra, WIDE), BF16),
            pltpu.VMEM((KEPT, count), BF16),
            pltpu.VMEM((WIDE, hidden), BF16),
            pltpu.VMEM((hidden, TAPS * 128), BF16),
            pltpu.VMEM((16, hidden), F32),
            pltpu.VMEM((16, hidden), F32),
            pltpu.VMEM((128, hidden), BF16),
            pltpu.VMEM((128, hidden), BF16),
            pltpu.VMEM((count + extra, 128), BF16),
            pltpu.VMEM((128, count), BF16),
            pltpu.VMEM((count, hidden), BF16),
            pltpu.VMEM((count + extra, hidden), BF16),
            pltpu.VMEM((KEPT, SPAN), F32),
            pltpu.VMEM((count, 128), F32),
            pltpu.VMEM((count, 128), F32),
            pltpu.VMEM((count, 128), F32),
            pltpu.VMEM((count, 128), BF16),
            semaphores(()),
            semaphores(()),
            semaphores((2,)),
        ],
        compiler_params=sending(2, 63),
        name="hidden",
    )(
        table, x1, xm, cotangent, cot_o, heads_out, fc1_w, fc1_o, fc2_w, fc2_o, depth_taps, depth_o,
        hidden_shifts, hidden_o, front_gains, front_shifts, proj_w,
    )

    dq, grad_own, grad_send, output = pl.pallas_call(
        attend_back_kernel,
        grid=(bands // 2,),
        out_shape=(
            shape((bands, SLOTS, 128), BF16),
            shape((bands + 1, CELLS, 128)),
            shape((bands + 1, CELLS, 128), BF16),
            shape((count, 128), BF16),
        ),
        in_specs=[SMEM]
        + [VMEM] * 4
        + [
            two_slots,
            VMEM,
            VMEM,
            two_slots,
            pl.BlockSpec((2, 128, SLOTS), lambda i: (i, 0, 0)),
            pl.BlockSpec((2, 8, SLOTS), lambda i: (i, 0, 0)),
            pl.BlockSpec((2 * BAND, 128), lambda i: (i, 0)),
        ],
        out_specs=[two_slots, VMEM, VMEM, pl.BlockSpec((2 * BAND, 128), lambda i: (i, 0))],
        scratch_shapes=[
            pltpu.VMEM((total, COARSE, 128), F32),
            pltpu.VMEM((total, FINE, 128), F32),
            pltpu.VMEM((128, 128), BF16),
            pltpu.VMEM((2, 64, MAX_BANDS * COARSE), BF16),
            pltpu.VMEM((2, 2, 64, HALVES[0][1] * PACKED), BF16),
            pltpu.VMEM((2, MAX_BANDS * PACKED, 128), BF16),
            pltpu.VMEM((2, MAX_BANDS * PACKED, 128), BF16),
            pltpu.SMEM((2,), jnp.int32),
        ],
        compiler_params=params(),
        name="attend_back",
    )(table, key_c, key_f, val_c, val_f, xn, query_t, query_o, out_grad, out_t, lse, output)

    peers = sum(2 ** len(dims) - 1 for dims in stages(levels, True))
    links = group_links(levels, False) + 3 * group_links(levels, True) + len(stages(levels, True)) + 1
    early_rows, late_rows, later_rows = (group_size(levels, part) for part in (SPLIT, CONV, REST))
    pieces = 2 ** (levels - 1)
    joint_rows = (early_rows + late_rows + later_rows) // pieces
    tokens_grad, joint, little = pl.pallas_call(
        functools.partial(tail_kernel, levels),
        out_shape=(
            shape((count, 128)),
            shape((2, 2, pieces, joint_rows, 128), BF16),
            shape((SMALL, 128)),
        ),
        in_specs=[HBM] * 3 + [VMEM, HBM] + [VMEM] * 2 + [HBM] * 3 + [VMEM] * 2 + [HBM] * 2
        + [VMEM] + ([HBM] * 2 + [VMEM] * 4) * 2,
        out_specs=[VMEM] * 3,
        scratch_shapes=[
            pltpu.VMEM((4 * QUARTER, 128), F32),
            pltpu.VMEM((len(stages(levels, True)), SMALL, 128), F32),
            pltpu.VMEM((peers, SMALL, 128), F32),
            semaphores((2, peers)),
            pltpu.VMEM((bands + 1, CELLS, 128), BF16),
            pltpu.VMEM((bands + 2, CELLS, 128), F32),
            pltpu.VMEM((bands + 2, CELLS, 128), F32),
            pltpu.VMEM((bands, SLOTS, 128), F32),
            semaphores((2,)),
            semaphores((2,)),
            semaphores((links,)),
            semaphores((links,)),
            pltpu.VMEM((128, coarse_conv.shape[0]), BF16),
            pltpu.VMEM((128, fine_conv.shape[0]), BF16),
            pltpu.VMEM((count, 128), F32),
            pltpu.VMEM((count, 128), BF16),
            pltpu.VMEM((bands, SLOTS, 128), BF16),
            pltpu.VMEM(grad_own.shape, F32),
            pltpu.VMEM(split_g.shape, F32),
            pltpu.VMEM(slab.shape, F32),
            pltpu.VMEM(xn.shape, BF16),
            pltpu.VMEM(dq.shape, BF16),
            pltpu.VMEM(red_c.shape, F32),
            pltpu.VMEM(coarse_conv.shape, BF16),
            pltpu.VMEM(red_f.shape, F32),
            pltpu.VMEM(fine_conv.shape, BF16),
            pltpu.VMEM((16, 128, bands * 16), BF16),
            semaphores((12,)),
        ]
        + group_scratch(levels, False, early_rows)
        + group_scratch(levels, True, late_rows)
        + group_scratch(levels, True, later_rows),
        compiler_params=sending(0),
        name="tail",
    )(
        grad_own, grad_send, split_g, mid_g, slab, other, meta, xn, hat, dq, query_t, query_o, dx1,
        tokens, front_gains,
        red_c, coarse_conv, gain_c, coarse_shifts, coarse_kv, coarse_taps,
        red_f, fine_conv, gain_f, fine_shifts, fine_kv, fine_taps,
    )
    grads = pl.pallas_call(
        functools.partial(unpack_kernel, levels),
        out_shape=(
            shape((count, 128)),
            shape((2, 128)),
            shape((4, 128)),
            shape((half, 128)),
            shape(coarse_conv.shape),
            shape((1, 128)),
            shape((3, 128)),
            shape((128, 128)),
            shape((9, half)),
            shape(fine_conv.shape),
            shape((1, 128)),
            shape((3, 128)),
            shape((128, 128)),
            shape((9, half)),
            shape((128, 128)),
            shape((2, mine)),
            shape((128, mine)),
            shape((9, mine)),
            shape((mine, 128)),
        ),
        in_specs=[VMEM] * 3,
        out_specs=[VMEM] * 19,
        compiler_params=params(),
        name="unpack",
    )(joint, little, tokens_grad)
    grads = [output] + list(grads)
    grads[4] = grads[4].T
    for at in (6, 11):
        grads[at] = grads[at].reshape(128)
    return tuple(grads)


def solution(mesh):
    tokens = P(("batch", "heads"), None)
    columns = P(None, "heads")
    return jax.shard_map(
        functools.partial(per_device, mesh.shape["batch"]),
        mesh=mesh,
        in_specs=(tokens, P("batch", None), tokens, P(), P(), columns)
        + (P(),) * 11
        + (columns, columns, columns, P("heads", None)),
        out_specs=(tokens, tokens, P(), P(), columns)
        + (P(),) * 11
        + (columns, columns, columns, P("heads", None)),
        check_vma=False,
    )
```

```python
import functools

import jax
import jax.numpy as jnp
from jax import lax
from jax.experimental import pallas as pl
from jax.experimental.pallas import tpu as pltpu
from jax.sharding import PartitionSpec as P

W = 56
BAND = 4 * W
SLOTS = 256
COARSE = 16
FINE = 64
CELLS = COARSE + FINE
MAX_BANDS = 14
EPS = 1e-06
F32 = jnp.float32
BF16 = jnp.bfloat16
SCALE = 32**-0.5
LOG2E = 1.4426950408889634
ROOT = 0.7071067811865476
EXP_SCALE = SCALE * LOG2E
BIG = -1e9
MIB = 1024 * 1024
STEP = 256
SPAN = 512
MESH = pl.DeviceIdType.MESH
TAPS = 9
KEPT = TAPS * 128 + 16
WIDE = (TAPS + 1) * 128
QUARTER = 768
CONV = 512
REST = QUARTER - CONV
SMALL = 48
SPLIT = 544


def dot(left, right):
    return jnp.dot(left, right, preferred_element_type=F32)


def dot_t(left, right):
    return lax.dot_general(left, right, (((1,), (1,)), ((), ())), preferred_element_type=F32)


def dot_in(left, right):
    return lax.dot_general(left, right, (((0,), (0,)), ((), ())), preferred_element_type=F32)


def gauss(values):
    return 0.5 + 0.5 * lax.erf(values * ROOT), jnp.exp2(values * values * (-0.5 * LOG2E))


def gelu_slope(values, cdf, bell):
    return cdf + values * bell * 0.3989422804014327


def fold_rows(values):
    wide = jnp.sum(values.reshape(-1, 64, 128), axis=0)
    return jnp.sum(wide.reshape(8, 8, 128), axis=0)


def norm_hat(values):
    centred = values - jnp.mean(values, axis=-1, keepdims=True)
    inverse = lax.rsqrt(jnp.mean(centred * centred, axis=-1, keepdims=True) + EPS)
    return centred * inverse, inverse


def norm_back(grad_scaled, hat, inverse):
    centre = jnp.mean(grad_scaled, axis=-1, keepdims=True)
    along = jnp.mean(grad_scaled * hat, axis=-1, keepdims=True)
    return inverse * (grad_scaled - centre - hat * along)


def slot_map(slot, token):
    a, b, c = slot >> 6, (slot >> 4) & 3, slot & 15
    hit = (token == a * W + 4 * c + b) & (c < 14)
    return jnp.where(hit, 1.0, 0.0).astype(BF16)


def to_slots():
    shape = (SLOTS, BAND)
    return slot_map(
        lax.broadcasted_iota(jnp.int32, shape, 0), lax.broadcasted_iota(jnp.int32, shape, 1)
    )


def from_slots():
    shape = (BAND, SLOTS)
    return slot_map(
        lax.broadcasted_iota(jnp.int32, shape, 1), lax.broadcasted_iota(jnp.int32, shape, 0)
    )


def cell_valid(shape, axis):
    return (lax.broadcasted_iota(jnp.int32, shape, axis) & 15) < 14


def roll_cells(values, step):
    lead = values.shape[:-2]
    flat = values.reshape(-1, values.shape[-1])
    flat = pltpu.roll(flat, step % flat.shape[0], 0)
    return flat.reshape(lead + values.shape[-2:])


def by_band(values, mask):
    count = values.shape[0]
    wide = values.reshape(count, -1, 8, 128) * mask.reshape(count, 1, 8, 128)
    return wide.reshape(values.shape)


def row_taps(taps, flip):
    order = [8 - i for i in range(9)] if flip else list(range(9))
    return [taps[i : i + 1, :] for i in order]


def depthwise_coarse(ext, above, below, taps, flip=False):
    t = row_taps(taps, flip)
    up, mid, down = by_band(ext[:-2], above), ext[1:-1], by_band(ext[2:], below)
    left, centre, right = (up * t[b] + mid * t[3 + b] + down * t[6 + b] for b in range(3))
    return centre + roll_cells(left, 1) + roll_cells(right, -1)


def fine_rows(ext, above, below):
    bands = ext.shape[0] - 2
    grid = ext.reshape(bands + 2, 2, 2, 16, 128)
    first, second = grid[:, 0], grid[:, 1]
    up = (by_band(second[:-2], above), first[1:-1])
    mid = (first[1:-1], second[1:-1])
    down = (second[1:-1], by_band(first[2:], below))
    return up, mid, down


def depthwise_fine(ext, above, below, taps, flip=False):
    t = row_taps(taps, flip)
    ups, mids, downs = fine_rows(ext, above, below)
    rows = []
    for up, mid, down in zip(ups, mids, downs):
        left, centre, right = (up * t[b] + mid * t[3 + b] + down * t[6 + b] for b in range(3))
        even = centre[:, 0] + roll_cells(left[:, 1], 1) + right[:, 1]
        odd = centre[:, 1] + left[:, 0] + roll_cells(right[:, 0], -1)
        rows.append((even, odd))
    return rows


def greet(*peers):
    barrier = pltpu.get_barrier_semaphore()
    for peer in peers:
        pl.semaphore_signal(barrier, inc=1, device_id=peer, device_id_type=MESH)


def met(count):
    pl.semaphore_wait(pltpu.get_barrier_semaphore(), count)


def fetch(pairs, sems):
    loads = [pltpu.make_async_copy(source, target, sems.at[i]) for i, (source, target) in enumerate(pairs)]
    for load in loads:
        load.start()
    return loads


def link(source, target, send_sem, recv_sem, peer):
    return pltpu.make_async_remote_copy(
        src_ref=source,
        dst_ref=target,
        send_sem=send_sem,
        recv_sem=recv_sem,
        device_id=peer,
        device_id_type=MESH,
    )


def remote(source, target, send_sem, recv_sem, peer):
    made = link(source, target, send_sem, recv_sem, peer)
    made.start()
    return made


def across():
    return (lax.axis_index("batch"), 1 - lax.axis_index("heads"))


def swap_lanes(values):
    half = values.shape[1] // 2
    return jnp.concatenate([values[:, half:], values[:, :half]], axis=1)


def keep_lanes(values, upper):
    lane = lax.broadcasted_iota(jnp.int32, values.shape, 1)
    return jnp.where((lane >= 64) if upper else (lane < 64), values, 0.0)


def pad_taps(taps, upper):
    gap = jnp.zeros(taps.shape, F32)
    return jnp.concatenate([gap, taps] if upper else [taps, gap], axis=1)


def band_tables(heights, table, meta, total):
    count = heights.shape[1]
    number = jnp.int32(0)
    start = jnp.int32(0)
    end = heights[0, 0]
    last = jnp.int32(-2)
    images, sames = [], []
    for band in range(total):
        passed = band >= end
        number = jnp.where(passed, number + 1, number)
        start = jnp.where(passed, end, start)
        grown = heights[0, jnp.minimum(number, count - 1)]
        grown = jnp.where(number < count, grown, 0)
        end = jnp.where(passed, end + grown, end)
        image = jnp.where(band < end, number, -1)
        same = jnp.where(image == last, 1, 0)
        last = image
        table[0, band] = image
        table[1, band] = jnp.minimum(start, total - MAX_BANDS)
        table[2, band] = same
        images.append(image)
        sames.append(same)
    for band in range(total, table.shape[1]):
        for row in range(3):
            table[row, band] = jnp.int32(0)
    sames.append(jnp.int32(0))
    for band in range(total):
        for row, value in enumerate((sames[band], sames[band + 1], images[band])):
            meta[row, band] = jnp.full((8, 128), value.astype(F32), F32)


def front_kernel(
    heights, tok, gains, shifts, conv_c, gain_c, shifts_c, kv_c, conv_f, gain_f, shifts_f, kv_f,
    query_t,
    table, meta, xn_out, hat_out, inv_out, red_c, red_f, slab, other, query_o,
    send, send_sems, recv_sems,
):
    bands = xn_out.shape[0]
    peer = across()
    greet(peer)
    copies = []

    def give(source, target):
        at = len(copies)
        copies.append(remote(source, target, send_sems.at[at], recv_sems.at[at], peer))

    place = to_slots()

    def norm_bands(first, count):
        rows = slice(first * BAND, (first + count) * BAND)
        hat, inverse = norm_hat(tok[rows, :].astype(F32))
        inv_out[rows, :] = jnp.broadcast_to(inverse, hat.shape)
        normed = (hat * gains[0:1, :] + shifts[0:1, :]).astype(BF16)
        sides = jnp.concatenate([normed, hat.astype(BF16)], axis=1)
        for band in range(count):
            both = dot(place, sides[band * BAND : (band + 1) * BAND]).astype(BF16)
            xn_out[first + band] = both[:, :128]
            hat_out[first + band] = both[:, 128:]

    def reduce(patches, conv, gain, shift, kv, out, at):
        red = dot(patches, conv) + shift[0:1, :]
        out[at : at + red.shape[0], :] = red
        hat, _ = norm_hat(red)
        normed = hat * gain[...] + shift[1:2, :]
        cdf, _ = gauss(normed)
        return dot((normed * cdf).astype(BF16), kv)

    kv_f_sw = swap_lanes(kv_f[...])
    part = bands // 2
    for first in (0, part):
        norm_bands(first, part)
        grid = xn_out[first : first + part].reshape(part, 16, 16, 128)
        patches = jnp.concatenate([fine_patch(grid, i) for i in range(4)], axis=1)
        pair = reduce(patches, conv_f[...], gain_f, shifts_f, kv_f_sw, red_f, first * FINE)
        pair = pair + keep_lanes(shifts_f[2:3, :], False)
        pair = jnp.where(cell_valid(pair.shape, 0), pair, 0.0).reshape(part, FINE, 128)
        slab[first : first + part, COARSE:CELLS, :] = pair
        send[first : first + part, COARSE:CELLS, :] = pair.astype(BF16)
        here = (pl.ds(first, part), pl.ds(COARSE, FINE))
        if first == 0:
            met(1)
        give(send.at[here], other.at[here])
        if first == 0:
            give(query_t, query_o)
    grid = xn_out[...].reshape(bands, 16, 16, 128)
    patches = jnp.concatenate([grid[:, i].reshape(bands * 16, 128) for i in range(16)], axis=1)
    pair = reduce(patches, conv_c[...], gain_c, shifts_c, kv_c[...], red_c, 0)
    pair = pair + keep_lanes(swap_lanes(shifts_c[2:3, :]), True)
    pair = jnp.where(cell_valid(pair.shape, 0), pair, 0.0).reshape(bands, COARSE, 128)
    slab[:, 0:COARSE, :] = pair
    send[:, 0:COARSE, :] = pair.astype(BF16)
    here = pl.ds(0, COARSE)
    give(send.at[:, here], other.at[:, here])
    band_tables(heights, table, meta, 2 * bands)
    for made in copies:
        made.wait()


def fine_slot(part, row, column):
    return (2 * row + (part >> 1)) * 4 + 2 * column + (part & 1)


def fine_patch(grid, part):
    bands = grid.shape[0]
    blocks = [
        grid[:, fine_slot(part, row, column)].reshape(bands, 1, 16, 128)
        for row in range(2)
        for column in range(2)
    ]
    return jnp.concatenate(blocks, axis=1).reshape(bands * FINE, 128)


def head_lanes(values, head):
    lane = lax.broadcasted_iota(jnp.int32, values.shape, 1)
    return jnp.where((lane >> 5) == head, values, jnp.zeros((), BF16))


def head_rows(values, head):
    row = lax.broadcasted_iota(jnp.int32, values.shape, 0)
    return jnp.where((row >> 5) == head, values, jnp.zeros((), BF16))


def score_rows(query_t, head, image, fine):
    row = lax.broadcasted_iota(jnp.int32, query_t.shape, 0)
    tag = row if fine else row - 64
    fill = jnp.where((tag >= 0) & (tag <= NOBODY) & (tag != image), BIG, 0.0).astype(BF16)
    return jnp.where((row >> 5) == head, query_t, fill)


def with_offset(rows, at, offset):
    start = at // 16 * 16
    block = rows[start : start + 16]
    row = lax.broadcasted_iota(jnp.int32, block.shape, 0)
    for i in range(3):
        term = offset.astype(BF16)
        block = jnp.where(row == at - start + i, term, block)
        offset = offset - term.astype(F32)
    parts = [rows[:start]] if start else []
    return jnp.concatenate(parts + [block, rows[start + 16 :]], axis=0)


def full_query(query_t, query_o, side):
    own, other = query_t[...].astype(F32), query_o[...].astype(F32)
    return jnp.where(
        side == 0,
        jnp.concatenate([own, other], axis=0),
        jnp.concatenate([other, own], axis=0),
    )


def window(ref, first):
    part = ref[pl.ds(first, MAX_BANDS)]
    return part.reshape(-1, 128).astype(BF16)


PACKED = 56
CHUNKS = ((0, 224), (224, 224), (448, 224), (672, 112))
HALVES = ((0, 8), (8, 6))
NOBODY = 32
ONES = 40


def tree_max(values):
    count = values.shape[0]
    while count % 16 == 0:
        count //= 2
        values = jnp.maximum(values[:count], values[count:])
    return jnp.max(values, axis=0, keepdims=True)


def attend_kernel(
    table, slab, other, meta, taps_c, taps_f, shifts_c, shifts_f, xn, tok, query_t, query_o, proj_w,
    gains, shifts, fc1, fc2, depth, hidden, cot,
    x1_out, xm_out, o_out, ot_out, lse_out, key_c, key_f, val_c, val_f, fc1_o, fc2_o, depth_o,
    hidden_o, cot_o,
    grid_ref, query_ref, place_ref, send_sems, recv_sems,
):
    step = pl.program_id(0)
    bands = slab.shape[0]
    total = 2 * bands
    side = lax.axis_index("heads")
    peer = across()
    halo = 2 * W
    edge = pl.multiple_of((1 - side) * (cot.shape[0] - halo), 16)
    swaps = [
        link(source, target, send_sems.at[i], recv_sems.at[i], peer)
        for i, (source, target) in enumerate(
            (
                (cot.at[pl.ds(edge, halo)], cot_o),
                (depth, depth_o),
                (hidden, hidden_o),
                (fc1, fc1_o),
                (fc2, fc2_o),
            )
        )
    ]

    @pl.when(step == 0)
    def _():
        greet(peer)
        place_ref[...] = from_slots()
        query_ref[...] = full_query(query_t, query_o, side).T.astype(BF16)
        grid_ref[0] = jnp.zeros((CELLS, 128), F32)
        grid_ref[total + 1] = jnp.zeros((CELLS, 128), F32)
        grid_ref[pl.ds(1 + side * bands, bands)] = slab[...]
        grid_ref[pl.ds(1 + (1 - side) * bands, bands)] = other[...].astype(F32)
        above, below, image = meta[0], meta[1], meta[2]
        lane = lax.broadcasted_iota(jnp.int32, (total, 16, 128), 2).astype(F32)
        valid = cell_valid((total, 16, 128), 1)
        wide = jnp.broadcast_to(image.reshape(total, 1, 8, 128), (total, 2, 8, 128))
        wide = wide.reshape(total, 16, 128)
        mark = jnp.where(valid & (wide >= 0.0), wide, float(NOBODY))

        ext = grid_ref[:, 0:COARSE, :]
        own = ext[1:-1]
        local = keep_lanes(shifts_c[2:3, :], True)
        mixed = own + depthwise_coarse(ext, above, below, pad_taps(taps_c[...], True)) + local
        val_c[...] = jnp.where(lane < 3.0, 1.0, mixed).astype(BF16)
        place = lane - 64.0
        one = (place >= ONES) & (place < ONES + 3)
        tag = jnp.where((place == mark) | one, 1.0, 0.0)
        keys = jnp.where(lane < 64.0, own, tag)
        key_c[...] = keys.astype(BF16)

        ext = grid_ref[:, COARSE:CELLS, :]
        local = keep_lanes(swap_lanes(shifts_f[2:3, :]), False)
        rows = depthwise_fine(ext, above, below, pad_taps(taps_f[...], False))
        tag = jnp.where((lane == mark) | ((lane >= ONES) & (lane < ONES + 3)), 1.0, 0.0)
        one = (lane >= 64.0) & (lane < 67.0)
        for row in range(2):
            for column in range(2):
                at = (2 * row + column) * 16
                own = ext[1:-1, at : at + 16, :]
                mixed = own + rows[row][column] + local
                cell = (2 * row + column) * 14
                val_f[:, cell : cell + 14, :] = jnp.where(one, 1.0, mixed)[:, 0:14]
                keys = jnp.where(lane >= 64.0, own.astype(BF16).astype(F32), tag)
                key_f[:, cell : cell + 14, :] = keys[:, 0:14]
        met(1)
        for swap in swaps:
            swap.start()

    each = xn.shape[0]
    images = [table[0, side * bands + each * step + i] for i in range(each)]
    firsts = [table[1, side * bands + each * step + i] for i in range(each)]
    queries = [
        dot(xn[i], query_ref[...]).astype(BF16).astype(F32).T.astype(BF16) for i in range(each)
    ]
    turned, windows = {}, {}

    def score(unit):
        i, head, part = unit
        fine = head >= 2
        start, size = CHUNKS[part]
        rows = slice(start, start + size)
        if not head & 1:
            if part == 0:
                windows[i, fine] = [
                    window(ref, firsts[i]) for ref in ((key_f, val_f) if fine else (key_c, val_c))
                ]
            turned[i, fine, part] = windows[i, fine][1][rows].T
        keys = windows[i, fine][0][rows]
        return dot(keys, score_rows(queries[i], head, images[i], fine))

    outs = [[None] * 4 for _ in range(each)]
    mixed = {}
    lse_out[...] = jnp.zeros(lse_out.shape, F32)

    def mix(unit, scores):
        i, head, part = unit
        fine = head >= 2
        top = tree_max(scores) * EXP_SCALE
        expo = jnp.exp2(scores * EXP_SCALE - top).astype(BF16)
        row = 32 * (head & 1) + (0 if fine else 64)
        vals = turned[i, fine, part][row : row + 32]
        left = jnp.concatenate([vals, jnp.ones((16, CHUNKS[part][1]), BF16)], axis=0)
        done = mixed.setdefault((i, head), [])
        done.append((top, dot(left, expo)))
        if len(done) < (4 if fine else 1):
            return
        top = functools.reduce(jnp.maximum, [part_top for part_top, _ in done])
        total = None
        for part_top, value in done:
            value = value * jnp.exp2(part_top - top)
            total = value if total is None else total + value
        sums = total[32:33]
        lse_out[i, head : head + 1, :] = top + jnp.log2(sums)
        outs[i][head] = total[0:32] * (1.0 / sums)

    waiting = []
    for i in range(each):
        for head, parts in ((2, 4), (0, 1), (3, 4), (1, 1)):
            for part in range(parts):
                waiting.append(((i, head, part), score((i, head, part))))
                if len(waiting) > 6:
                    mix(*waiting.pop(0))
    for unit, scores in waiting:
        mix(unit, scores)
    place = place_ref[...]
    joined = []
    for i in range(each):
        live = jnp.where(images[i] >= 0, 1.0, 0.0)
        out_t = jnp.concatenate(outs[i], axis=0) * live
        ot_out[i] = out_t
        joined.append(dot(place, out_t.T.astype(BF16)).astype(BF16))
    heads_out = jnp.concatenate(joined, axis=0)
    o_out[...] = heads_out
    middle = tok[...].astype(F32) + dot(heads_out, proj_w[...]) + shifts[1:2, :]
    x1_out[...] = middle
    hat, _ = norm_hat(middle)
    xm_out[...] = (hat * gains[1:2, :] + shifts[2:3, :]).astype(BF16)

    @pl.when(step == pl.num_programs(0) - 1)
    def _():
        for swap in swaps:
            swap.wait()


def shift_right(values):
    column = lax.broadcasted_iota(jnp.int32, values.shape, 0)
    return jnp.where(column == 0, 0.0, pltpu.roll(values, 1, 0))


def shift_left(values):
    column = lax.broadcasted_iota(jnp.int32, values.shape, 0)
    return jnp.where(column == W - 1, 0.0, pltpu.roll(values, W - 1, 0))


def mask_lanes():
    lane = lax.broadcasted_iota(jnp.int32, (W, 128), 1)
    column = lax.broadcasted_iota(jnp.int32, (W, 128), 0)
    tap = jnp.where(lane < 32, lane & 15, 15)
    parts = []
    for a in range(3):
        hit = tap == 3 * a + 1
        hit = hit | ((tap == 3 * a) & (column > 0)) | ((tap == 3 * a + 2) & (column < W - 1))
        if a == 1:
            hit = hit | (tap == TAPS)
        parts.append(jnp.where(hit, 1.0, 0.0))
    return parts


def hidden_kernel(
    table, x1_in, xm, cot, cot_o, heads_in, fc1, fc1_o, fc2, fc2_o, depth, depth_o, hidden, hidden_o,
    gains, shifts, proj_w,
    out, dx1_out, do_out, split_g, mid_g,
    xm_ext, halo_ref, moved, wide, wide_t, weights, weights_t, taps, bias, base_ref, fc2_t, dy, dy_t, act, du,
    sums, dxm, out_acc, x1, heads_out, send_sem, recv_sem, load_sems,
):
    side = lax.axis_index("heads")
    peer = across()
    tokens = x1.shape[0]
    rows = tokens // W
    bands = tokens // BAND
    halo = 2 * W
    extra = wide.shape[0] - tokens
    mine = fc1.shape[1]
    width = 2 * mine
    halo_at = pl.multiple_of((1 - side) * (halo + tokens), 16)
    halo_row = 1 + (1 - side) * (rows + 1)
    greet(peer)
    loads = fetch(((x1_in, x1), (heads_in, heads_out)), load_sems)
    edge = pl.multiple_of((1 - side) * (tokens - halo), 16)
    swap = link(xm.at[pl.ds(edge, halo)], halo_ref, send_sem, recv_sem, peer)

    def live_band(band):
        return jnp.where(table[0, band] >= 0, 1.0, 0.0)

    def neighbour(row):
        place = side * rows - 2 + row
        band = jnp.maximum(place, 0) >> 2
        up = jnp.where((place & 3) == 0, table[2, band], 1)
        down = jnp.where((place & 3) == 3, table[2, band + 1], 1)
        return up.astype(F32), down.astype(F32)

    xm_ext[0:halo, :] = jnp.zeros((halo, 128), BF16)
    xm_ext[halo + tokens : tokens + 2 * halo, :] = jnp.zeros((halo, 128), BF16)
    xm_ext[halo : halo + tokens, :] = xm[...]
    for band in range(bands):
        at = slice(band * BAND, (band + 1) * BAND)
        dy[at, :] = (cot[at, :].astype(F32) * live_band(side * bands + band)).astype(BF16)
    tail = cot_o[...].astype(F32)
    tail = jnp.where(side == 0, tail[:W], tail[W:]) * live_band((1 - side) * bands + side * (bands - 1))
    tail = jnp.concatenate([tail, jnp.zeros((extra - W, 128), F32)], axis=0)
    dy[tokens : tokens + extra, :] = tail.astype(BF16)

    taps[...] = jnp.zeros(taps.shape, F32)
    bias[...] = jnp.zeros(bias.shape, F32)
    for part, (taps_ref, shift_ref, fc1_ref, fc2_ref) in enumerate(
        ((depth, hidden, fc1, fc2), (depth_o, hidden_o, fc1_o, fc2_o))
    ):
        lanes = slice(part * mine, part * mine + mine)
        taps[0:TAPS, lanes] = taps_ref[...]
        taps[TAPS : TAPS + 1, lanes] = shift_ref[0:1, :]
        bias[0:TAPS, lanes] = taps_ref[...] * shift_ref[0:1, :]
        bias[TAPS : TAPS + 1, lanes] = shift_ref[0:1, :] + shift_ref[1:2, :]
        fc2_t[:, lanes] = fc2_ref[...].T
        base_ref[:, lanes] = fc1_ref[...]
        base = fc1_ref[...].astype(F32)
        for k in range(TAPS):
            factor = taps_ref[k : k + 1, :] + (1.0 if k == 4 else 0.0)
            weights[k * 128 : k * 128 + 128, lanes] = (base * (factor * ROOT)).astype(BF16)
    scaled = bias[...] * ROOT
    high = scaled.astype(BF16)
    weights[TAPS * 128 : TAPS * 128 + 16, :] = high
    weights[TAPS * 128 + 16 : TAPS * 128 + 32, :] = (scaled - high.astype(F32)).astype(BF16)
    weights[TAPS * 128 + 32 : WIDE, :] = jnp.zeros((96, width), BF16)

    met(1)
    swap.start()

    def move_rows(pair, carry):
        both = xm_ext[pl.ds(pl.multiple_of(pair * halo, 16), halo), :].astype(F32)
        for i in range(2):
            row = both[W * i : W * i + W]
            moved[0, 2 * pair + i] = shift_right(row)
            moved[1, 2 * pair + i] = row
            moved[2, 2 * pair + i] = shift_left(row)
        return carry

    lax.fori_loop(1, rows // 2 + 1, move_rows, 0, unroll=2)
    swap.wait()
    xm_ext[pl.ds(halo_at, halo), :] = halo_ref[...]
    move_rows(0, 0)
    move_rows(rows // 2 + 1, 0)

    masks = mask_lanes()

    def gather_row(row, block):
        up, down = neighbour(row)
        if block == TAPS:
            return masks[0] * up + masks[1] + masks[2] * down
        a, b = divmod(block, 3)
        values = moved[b, row + a - 1]
        return values if a == 1 else values * (up if a == 0 else down)

    inner = masks[0] + masks[1] + masks[2]

    def gather_band(band, carry):
        row = 2 + 4 * band
        up, _ = neighbour(row)
        _, down = neighbour(row + 3)
        for block in range(TAPS + 1):
            if block == TAPS:
                first = masks[0] * up + masks[1] + masks[2]
                last = masks[0] + masks[1] + masks[2] * down
                parts = [first, inner, inner, last]
            else:
                a, b = divmod(block, 3)
                parts = [moved[b, row + i + a - 1] for i in range(4)]
                if a == 0:
                    parts[0] = parts[0] * up
                elif a == 2:
                    parts[3] = parts[3] * down
            both = jnp.concatenate(parts, axis=0).astype(BF16)
            wide[pl.ds(pl.multiple_of(band * BAND, 16), BAND), block * 128 : block * 128 + 128] = both
        return carry

    lax.fori_loop(0, bands, gather_band, 0)
    for block in range(TAPS + 1):
        lanes = slice(block * 128, block * 128 + 128)
        tail = jnp.concatenate([gather_row(halo_row, block), jnp.zeros((extra - W, 128), F32)], axis=0)
        wide[tokens : tokens + extra, lanes] = tail.astype(BF16)

    def fc2_part(n):
        ref, at = (fc2, n * SPAN) if n * SPAN < mine else (fc2_o, n * SPAN - mine)
        return ref[at : at + SPAN, :]

    def one_block(at, own):
        total = None
        coming = dot(wide[at, :], weights[:, 0:SPAN])
        for n in range(width // SPAN):
            lanes = slice(n * SPAN, n * SPAN + SPAN)
            spread = coming
            if (n + 1) * SPAN < width:
                coming = dot(wide[at, :], weights[:, (n + 1) * SPAN : (n + 2) * SPAN])
            grad = dot(dy[at, :], fc2_t[:, lanes])
            bell = jnp.exp2(spread * spread * -LOG2E)
            share = 1.0 + lax.erf(spread)
            du[at, lanes] = (grad * (share + spread * bell * 1.1283791670955126)).astype(BF16)
            if own:
                active = (spread * share).astype(BF16)
                act[at, lanes] = active
                part = dot(active, fc2_part(n))
                total = part if total is None else total + part
        return total

    size = 896

    def own_block(block, carry):
        at = pl.ds(pl.multiple_of(block * size, 128), size)
        for part in range(TAPS + 1):
            kept = min(128, KEPT - part * 128)
            turned = wide[at, part * 128 : part * 128 + 128].T
            wide_t[part * 128 : part * 128 + kept, at] = turned[0:kept]
        dy_t[:, at] = dy[at, :].T
        out_acc[at, :] = one_block(at, True) * ROOT
        return carry

    lax.fori_loop(0, tokens // size, own_block, 0)
    one_block(slice(tokens, tokens + extra), False)

    def fold(half):
        lanes = pl.ds(pl.multiple_of(half * SPAN, SPAN), SPAN)
        base = base_ref[:, lanes].astype(F32)
        grad = sums[4 * 128 : 5 * 128, :]
        marks = sums[TAPS * 128 : KEPT, :]
        mean = marks[TAPS : TAPS + 1]
        bias_g = mean
        rows_g = []
        factors = taps[:, lanes]
        for k in range(TAPS):
            part = sums[k * 128 : k * 128 + 128, :]
            mark = marks[k : k + 1]
            factor = factors[k : k + 1]
            grad = grad + part * factor
            bias_g = bias_g + mark * factor
            rows_g.append(jnp.sum(part * base, axis=0, keepdims=True) + mark * factors[TAPS : TAPS + 1])
        rows_g = jnp.concatenate(rows_g + [bias_g, mean, jnp.zeros((5, SPAN), F32)], axis=0)
        for i in range(SPAN // 128):
            core, row = divmod(i, STEP // 128)
            piece = slice(i * 128, i * 128 + 128)
            split_g[half, core, row * 128 : row * 128 + 128, :] = grad[:, piece] * 0.5
            split_g[half, core, 512 + 16 * row : 528 + 16 * row, :] = rows_g[:, piece] * 0.5

    def gradients(half, carry):
        lanes = pl.ds(pl.multiple_of(half * SPAN, SPAN), SPAN)
        for part in (slice(0, 592), slice(592, KEPT)):
            sums[part, :] = dot(wide_t[part, :], du[0:tokens, lanes])
        turned = dot(dy_t[...], act[:, lanes]).T * ROOT
        for core in range(2):
            split_g[half, core, 256:512, :] = turned[core * STEP : core * STEP + STEP]
        for k in range(TAPS):
            weights_t[lanes, k * 128 : k * 128 + 128] = weights[k * 128 : k * 128 + 128, lanes].T
        fold(half)
        return carry

    lax.fori_loop(0, width // SPAN, gradients, 0)

    groups = ((4, 1, 7, 0), (3, 6, 2, 5), (8,))

    def collect_row(group, base, row):
        total = [None] * 3
        for i, k in enumerate(group):
            a, b = divmod(k, 3)
            source = row + 3 - a
            part = moved[base + i, source]
            if a != 1:
                up, down = neighbour(source)
                part = part * (up if a == 0 else down)
            total[b] = part if total[b] is None else total[b] + part
        if total[0] is not None:
            total[0] = shift_left(total[0])
        if total[2] is not None:
            total[2] = shift_right(total[2])
        total = functools.reduce(jnp.add, [part for part in total if part is not None])
        at = pl.ds(pl.multiple_of(row * W, 8), W)
        if group[0] == 4:
            dxm[at, :] = total
        else:
            dxm[at, :] += total

    for number, group in enumerate(groups):
        base = 4 * (number & 1)
        for i in range(len(group)):
            moved[base + i, 1] = jnp.zeros((W, 128), F32)
            moved[base + i, rows + 2] = jnp.zeros((W, 128), F32)

        def back(at):
            parts = [weights_t[:, k * 128 : k * 128 + 128] for k in group]
            return dot(du[at, :], jnp.concatenate(parts, axis=1))

        tail = back(slice(tokens, tokens + extra))
        for i in range(len(group)):
            moved[base + i, halo_row] = tail[0:W, i * 128 : i * 128 + 128]

        def back_block(block, carry):
            result = back(pl.ds(pl.multiple_of(block * 4 * BAND, 16), 4 * BAND))
            for i in range(len(group)):
                moved[base + i, pl.ds(2 + 16 * block, 16)] = result[
                    :, i * 128 : i * 128 + 128
                ].reshape(16, W, 128)
            if number:
                for i in range(16):
                    collect_row(groups[number - 1], 4 - base, 16 * block + i)
            return carry

        lax.fori_loop(0, bands // 4, back_block, 0)

    def last_rows(row, carry):
        collect_row(groups[-1], 4 * ((len(groups) - 1) & 1), row)
        return carry

    lax.fori_loop(0, rows, last_rows, 0, unroll=4)

    mid_g[...] = jnp.zeros(mid_g.shape, F32)
    for load in loads:
        load.wait()
    place = to_slots()
    proj = proj_w[...].astype(F32)
    proj_sw = jnp.concatenate([proj[64:], proj[:64]], axis=0).T.astype(BF16)

    def fold_up(values):
        return jnp.sum(jnp.sum(values.reshape(-1, 64, 128), axis=0).reshape(8, 8, 128), axis=0)

    def two_bands(block, carry):
        at = pl.ds(pl.multiple_of(block * 2 * BAND, 16), 2 * BAND)
        middle = x1[at, :]
        result = middle + out_acc[at, :] + shifts[3:4, :]
        hat, inverse = norm_hat(middle)
        grad = dxm[at, :] * ROOT
        grad_y = dy[at, :].astype(F32)
        dx1 = grad_y + norm_back(grad * gains[1:2, :], hat, inverse)
        dx1_out[at, :] = dx1
        dz = dx1.astype(BF16)
        mid_g[8:136, :] += dot_in(heads_out[at, :], dz)
        do = dot(dz, proj_sw)
        for i in range(2):
            band = 2 * block + i
            live = live_band(side * bands + band)
            part = slice(i * BAND, (i + 1) * BAND)
            here = pl.ds(pl.multiple_of(band * BAND, 16), BAND)
            out[here, :] = (result[part] * live).astype(BF16)
            do_out[band] = dot(place, (do[part] * live).astype(BF16)).astype(BF16)
        terms = (grad * hat, grad, dz.astype(F32), grad_y)
        return tuple(total + fold_up(term) for total, term in zip(carry, terms))

    zero = jnp.zeros((8, 128), F32)
    totals = lax.fori_loop(0, bands // 2, two_bands, (zero,) * 4)
    for i in range(4):
        mid_g[i : i + 1, :] = jnp.sum(totals[i], axis=0, keepdims=True)


def stages(levels, shared):
    rest = list(range(2, levels))
    pairs = [rest[i : i + 2] for i in range(0, len(rest), 2)]
    return [[0], ["x", 1]] + pairs if shared else [[0], [1]] + pairs + [["x"]]


def group_size(levels, rows):
    unit = 16 * 2 ** (levels - 1)
    return -(-rows // unit) * unit


def stage_shapes(levels, shared, rows):
    halves, shapes = 2, [(1, 2, rows, 128)]
    for dims in stages(levels, shared)[1:]:
        if "x" in dims:
            halves = 1
        rows >>= sum(1 for dim in dims if dim != "x")
        shapes.append((2 ** len(dims) - 1, halves, rows, 128))
    return shapes


def group_scratch(levels, shared, rows):
    buffers = [pltpu.VMEM(part, BF16) for part in stage_shapes(levels, shared, rows)]
    return [pltpu.VMEM((2, rows, 128), F32)] + buffers + buffers


def group_links(levels, shared):
    return sum(2 ** len(dims) - 1 for dims in stages(levels, shared))


def everyone(levels):
    batch, side = lax.axis_index("batch"), lax.axis_index("heads")
    peers = []
    for dims in stages(levels, True):
        for flips in range(1, 2 ** len(dims)):
            peers.append(flipped(batch, side, dims, flips))
    return peers


def flipped(batch, side, dims, flips):
    for i, dim in enumerate(dims):
        if flips >> i & 1:
            if dim == "x":
                side = 1 - side
            else:
                batch = batch + (1 - 2 * ((batch // 2**dim) % 2)) * 2**dim
    return batch, side


class Group:
    def __init__(self, levels, shared, buffers, sems, base):
        self.stages = stages(levels, shared)
        count = len(self.stages)
        self.cur, self.sends, self.recvs = buffers[0], buffers[1 : 1 + count], buffers[1 + count :]
        self.sems, self.base = sems, base
        self.batch, self.side = lax.axis_index("batch"), lax.axis_index("heads")
        self.core = self.batch % 2
        at, rows = 0, self.cur.shape[1]
        self.kept, self.given = [(at, rows)], [None]
        for dims in self.stages[1:]:
            bits = [dim for dim in dims if dim != "x"]
            starts = []
            for flips in range(2 ** len(dims)):
                batch, _ = flipped(self.batch, self.side, dims, flips)
                start = at
                for i, bit in enumerate(bits):
                    start = start + ((batch // 2**bit) % 2) * (rows >> (i + 1))
                starts.append(pl.multiple_of(start, 16))
            rows >>= len(bits)
            at = starts[0]
            self.kept.append((at, rows))
            self.given.append(starts)
        self.left = list(range(count))

    def link(self, stage, flips):
        number = self.base + sum(2 ** len(part) - 1 for part in self.stages[:stage]) + flips - 1
        peer = flipped(self.batch, self.side, self.stages[stage], flips)
        source, target = self.sends[stage].at[flips - 1], self.recvs[stage].at[flips - 1]
        return link(source, target, self.sems[0].at[number], self.sems[1].at[number], peer)

    def wait(self, stage):
        for flips in range(1, 2 ** len(self.stages[stage])):
            self.link(stage, flips).wait()

    def add(self, stage):
        at, rows = self.kept[stage]
        here, recv = pl.ds(at, rows), self.recvs[stage]
        if recv.shape[1] == 2:
            total = self.cur[:, here, :]
            for i in range(recv.shape[0]):
                total = total + recv[i].astype(F32)
            self.cur[:, here, :] = total
            return
        total = self.cur[self.side, here, :]
        for i in range(recv.shape[0]):
            total = total + recv[i, 0].astype(F32)
        self.cur[self.side, here, :] = total

    def advance(self, count=1, pieces=None):
        for number in self.left[:count]:
            self.phase(number, pieces)
        del self.left[:count]

    def phase(self, number, pieces):
        count = len(self.stages)
        if number == 0:
            for half in range(2):
                for row, value in pieces(half, 1 - self.core):
                    self.sends[0][0, half, row : row + value.shape[0], :] = value.astype(BF16)
            self.link(0, 1).start()
            for half in range(2):
                for row, value in pieces(half, self.core):
                    self.cur[half, row : row + value.shape[0], :] = value
        else:
            self.wait(number - 1)
            self.add(number - 1)
            dims = self.stages[number]
            _, rows = self.kept[number]
            for flips in range(1, 2 ** len(dims)):
                crossing = "x" in dims and flips >> dims.index("x") & 1
                here = pl.ds(self.given[number][flips], rows)
                if self.sends[number].shape[1] == 2:
                    self.sends[number][flips - 1] = self.cur[:, here, :].astype(BF16)
                else:
                    half = 1 - self.side if crossing else self.side
                    self.sends[number][flips - 1, 0] = self.cur[half, here, :].astype(BF16)
                self.link(number, flips).start()

    def finish(self):
        self.wait(len(self.stages) - 1)
        self.add(len(self.stages) - 1)
        at, rows = self.kept[-1]
        return self.cur[self.side, pl.ds(at, rows), :].astype(BF16)


class Gather:
    def __init__(self, levels, out, shared, sems, base):
        self.stages, self.out, self.shared = stages(levels, True), out, shared
        self.sems, self.base = sems, base
        self.batch, self.side = lax.axis_index("batch"), lax.axis_index("heads")
        self.core = self.batch % 2
        at, count = 0, out.shape[2]
        self.kept = [(at, count)]
        for dims in self.stages[1:]:
            for bit in dims:
                if bit != "x":
                    count //= 2
                    at = at + ((self.batch // 2**bit) % 2) * count
            self.kept.append((at, count))
        self.left = list(range(len(self.stages)))

    def links(self, stage):
        dims = self.stages[stage]
        at, count = self.kept[stage]
        number = self.base + sum(2 ** len(part) for part in self.stages[:stage])
        mine = self.out.at[self.core, self.side, pl.ds(at, count)]
        for flips in range(1, 2 ** len(dims)):
            part = mine
            if "x" in dims and flips >> dims.index("x") & 1:
                part = self.out.at[self.core, self.side, pl.ds(at, count), pl.ds(0, self.shared)]
            yield self.made(part, number, flipped(self.batch, self.side, dims, flips))
            number += 1
        if stage == 0:
            part = self.out.at[self.core, 1 - self.side, :, pl.ds(0, self.shared)]
            yield self.made(part, number, flipped(self.batch, self.side, dims, 1))

    def made(self, part, number, peer):
        return link(part, part, self.sems[0].at[number], self.sems[1].at[number], peer)

    def begin(self, pieces):
        at, _ = self.kept[-1]
        row = 0
        for piece in pieces:
            self.out[self.core, self.side, at, row : row + piece.shape[0], :] = piece
            row += piece.shape[0]
        for made in self.links(len(self.stages) - 1):
            made.start()

    def advance(self):
        stage = len(self.left) - 1
        for made in self.links(stage):
            made.wait()
        if stage:
            for made in self.links(stage - 1):
                made.start()
        del self.left[-1]


def attend_back_kernel(
    table, key_c, key_f, val_c, val_f, xn, query_t, query_o, do_ref, ot_ref, lse, output,
    dq_out, own_out, send_out, output_out,
    acc_c, acc_f, query_ref, turned_c, turned_f, keys_ref, vals_ref, kept,
):
    step = pl.program_id(0)
    each = xn.shape[0]
    bands = each * pl.num_programs(0)
    side = lax.axis_index("heads")

    @pl.when(step == 0)
    def _():
        acc_c[...] = jnp.zeros(acc_c.shape, F32)
        acc_f[...] = jnp.zeros(acc_f.shape, F32)
        query_ref[...] = full_query(query_t, query_o, side).T.astype(BF16)

    output_out[...] = output[...]
    firsts = [table[1, side * bands + each * step + i] for i in range(each)]
    for i in range(each):

        @pl.when((step == 0) | (kept[i] != firsts[i]))
        def _():
            kept[i] = firsts[i]
            keys = window(key_f, firsts[i])
            keys_ref[i] = keys
            vals_ref[i] = window(val_f, firsts[i])
            for part, (start, count) in enumerate(HALVES):
                rows = slice(start * PACKED, (start + count) * PACKED)
                turned_f[i, part, :, 0 : count * PACKED] = keys[rows].T[64:128]
            turned_c[i] = window(key_c, firsts[i]).T[0:64]

    queries, query_rows, grads_t, grads_low = [], [], [], []
    for i in range(each):
        query = dot(xn[i], query_ref[...]).astype(BF16)
        queries.append(query)
        query_rows.append(query.astype(F32).T.astype(BF16))
        grads_t.append(do_ref[i].astype(F32).T)
        grads_low.append(grads_t[i].astype(BF16))
    dq = [[None] * 4 for _ in range(each)]

    def products(unit):
        i, head, part = unit
        fine = head >= 2
        image = table[0, side * bands + each * step + i]
        start, count = HALVES[part]
        if fine:
            rows = slice(start * PACKED, (start + count) * PACKED)
            keys, vals = keys_ref[i, rows], vals_ref[i, rows]
        else:
            keys, vals = window(key_c, firsts[i]), window(val_c, firsts[i])
        swapped = (head + 2) & 3
        delta = jnp.sum(
            ot_ref[i, 32 * head : 32 * head + 32]
            * grads_t[i][32 * swapped : 32 * swapped + 32],
            axis=0,
            keepdims=True,
        )
        offset = lse[i, head : head + 1, :] * (-1.0 / EXP_SCALE)
        left = score_rows(query_rows[i], head, image, fine)
        left = with_offset(left, ONES + (0 if fine else 64), offset)
        right = with_offset(head_rows(grads_low[i], swapped), 64 if fine else 0, -delta)
        return dot(keys, left), dot(vals, right)

    held = {}

    def back(unit, score, prob_grad):
        i, head, part = unit
        fine = head >= 2
        swapped = (head + 2) & 3
        prob = jnp.exp2(score * EXP_SCALE)
        score_grad = (prob * prob_grad).astype(BF16)
        row = 32 * (head & 1)
        start, count = HALVES[part]
        turned = turned_c[i, row : row + 32]
        if fine:
            turned = turned_f[i, part, row : row + 32, 0 : count * PACKED]
        grad = dot(turned, score_grad)
        dq[i][head] = grad if part == 0 else dq[i][head] + grad
        pair = held.setdefault((i, fine, part), ([], []))
        pair[0].extend([score_grad, prob.astype(BF16)])
        pair[1].extend([head_lanes(queries[i], head), head_lanes(do_ref[i], swapped)])
        if head & 1:
            both = dot(jnp.concatenate(pair[0], axis=1), jnp.concatenate(pair[1], axis=0))
            if fine:
                at = pl.ds(firsts[i] + start, count)
                acc_f[at, 0:PACKED, :] += both.reshape(count, PACKED, 128)
            else:
                acc_c[pl.ds(firsts[i], MAX_BANDS)] += both.reshape(MAX_BANDS, COARSE, 128)

    waiting = []
    for i in range(each):
        for head, parts in ((2, 2), (3, 2), (0, 1), (1, 1)):
            for part in range(parts):
                waiting.append(((i, head, part), *products((i, head, part))))
                if len(waiting) > 3:
                    back(*waiting.pop(0))
    for unit in waiting:
        back(*unit)
    for i in range(each):
        dq_out[i] = (jnp.concatenate(dq[i], axis=0).T * SCALE).astype(BF16)

    @pl.when(step == pl.num_programs(0) - 1)
    def _():
        span = bands + 1
        lane = lax.broadcasted_iota(jnp.int32, (1, 128), 1)
        scale_c = jnp.where(lane < 64, SCALE, 1.0)
        scale_f = jnp.where(lane < 64, 1.0, SCALE)
        for dest, at, kind in (
            (own_out, side * (bands - 1), F32),
            (send_out, (1 - side) * (bands - 1), BF16),
        ):
            dest[:, 0:COARSE, :] = (acc_c[pl.ds(at, span)] * scale_c).astype(kind)
            for cell in range(4):
                part = acc_f[pl.ds(at, span), 14 * cell : 14 * cell + 16, :] * scale_f
                part = jnp.where(cell_valid(part.shape, 1), part, 0.0)
                row = COARSE + 16 * cell
                dest[:, row : row + 16, :] = part.astype(kind)


def tail_kernel(
    levels, own_in, given, split_in, mid_g, slab_in, other, meta, xn_in, hat_in, dq_in, query_t,
    query_o, dx1_in, inv_in, gains,
    red_c_in, conv_c_in, gain_c, shifts_c, kv_c, taps_c_ref,
    red_f_in, conv_f_in, gain_f, shifts_f, kv_f, taps_f_ref,
    tok_grad, joint, little,
    pack, small, small_in, small_sems, recv, grad_ref, val_ref, dxn, send_sem, recv_sem, send_sems, recv_sems, turned_c, turned_f,
    dx1, inv, hat_ref, own, split_g, slab, xn, dq, red_c, conv_c, red_f, conv_f, xt, load_sems,
    *buffers,
):
    bands = xn.shape[0]
    side = lax.axis_index("heads")
    greet(*everyone(levels))
    early_pairs = (
        (split_in, split_g), (dq_in, dq), (xn_in, xn), (own_in, own), (slab_in, slab),
        (conv_c_in, conv_c), (conv_f_in, conv_f),
    )
    loads = fetch(early_pairs, load_sems)
    met(len(everyone(levels)))
    swaps = [
        remote(given.at[:, here], recv.at[:, here], send_sem.at[i], recv_sem.at[i], across())
        for i, here in enumerate((pl.ds(0, COARSE), pl.ds(COARSE, FINE)))
    ]
    late_pairs = (
        (red_c_in, red_c), (red_f_in, red_f), (hat_in, hat_ref), (inv_in, inv), (dx1_in, dx1),
    )
    loads += fetch(late_pairs, load_sems.at[pl.ds(len(early_pairs), len(late_pairs))])
    sems = (send_sems, recv_sems)
    split_count, shared_count = (1 + 2 * len(stages(levels, shared)) for shared in (False, True))
    before = Group(levels, False, buffers[:split_count], sems, 0)
    base = group_links(levels, False)
    buffers = buffers[split_count:]
    conv = Group(levels, True, buffers[:shared_count], sems, base)
    base += group_links(levels, True)
    rest = Group(levels, True, buffers[shared_count:], sems, base)
    base += group_links(levels, True)
    early_rows, late_rows, later_rows = (group.cur.shape[1] for group in (before, conv, rest))
    gather = Gather(levels, joint, (late_rows + later_rows) // joint.shape[2], sems, base)

    def split_pieces(half, which):
        yield 0, split_g[(half + side) % 2, which]
        if early_rows > SPLIT:
            yield SPLIT, jnp.zeros((early_rows - SPLIT, 128), F32)

    def shared_pieces(first, used, rows):
        def pieces(half, which):
            at = pl.multiple_of(first + used * (2 * half + which), 16)
            yield 0, pack[pl.ds(at, used), :]
            if rows > used:
                yield used, jnp.zeros((rows - used, 128), F32)

        return pieces

    batch, order = lax.axis_index("batch"), stages(levels, True)

    def small_links(stage):
        before = sum(2 ** len(dims) - 1 for dims in order[:stage])
        for flips in range(1, 2 ** len(order[stage])):
            at = before + flips - 1
            yield at, link(
                small.at[stage], small_in.at[at], small_sems.at[0, at], small_sems.at[1, at],
                flipped(batch, side, order[stage], flips),
            )

    def small_phase(stage):
        if stage:
            total = small[stage - 1]
            for at, made in small_links(stage - 1):
                made.wait()
                total = total + small_in[at]
            if stage == len(order):
                little[...] = total
                return
            small[stage] = total
        for _, made in small_links(stage):
            made.start()

    for load in loads[:7]:
        load.wait()
    before.advance(1, split_pieces)

    start = 0
    parts = []
    for count in (conv_c.shape[0], conv_f.shape[0], 128, 128, 128, 128):
        parts.append(pack.at[start : start + count])
        start += count
    conv_c_g, conv_f_g, kv_c_g, kv_f_g, query_g, proj_g = parts
    small_c, small_f, front_g = small.at[0, 0:16], small.at[0, 16:32], small.at[0, 32:40]
    small[0, 40:48, :] = mid_g[0:8, :]
    proj_g[...] = mid_g[8:136, :]
    taps_c, taps_f = pad_taps(taps_c_ref[...], True), pad_taps(taps_f_ref[...], False)
    kv_f_sw = swap_lanes(kv_f[...])

    val_ref[0] = jnp.zeros((CELLS, 128), F32)
    val_ref[bands + 1] = jnp.zeros((CELLS, 128), F32)
    val_ref[1 : bands + 1] = slab[...]
    val_ref[pl.ds((1 - side) * (bands + 1), 1)] = other[
        pl.ds(side * (bands - 1), 1)
    ].astype(F32)
    at = pl.ds(side * bands, bands)
    above, below = meta[0, at], meta[1, at]
    grid = xn[...].reshape(bands, 16, 16, 128)
    slot_grads = dq[...].reshape(bands, 16, 16, 128)
    total = None
    for i in range(16):
        turned = grid[:, i].reshape(bands * 16, 128).T
        xt[i] = turned
        part = dot(turned, slot_grads[:, i].reshape(bands * 16, 128))
        total = part if total is None else total + part
    query_g[...] = total
    full = full_query(query_t, query_o, side).astype(BF16)
    dxn[...] = dot(dq[...].reshape(-1, 128), full).reshape(bands, SLOTS, 128)
    grad_ref[0] = jnp.zeros((CELLS, 128), F32)
    grad_ref[bands + 1] = jnp.zeros((CELLS, 128), F32)
    turned_c[...] = conv_c[...].T
    turned_f[...] = conv_f[...].T
    before.advance()
    swaps[0].wait()
    here = pl.ds(1 - side, bands + 1)
    for load in loads[7:]:
        load.wait()
    grad_ref[here, 0:COARSE] = own[:, 0:COARSE] + recv[:, 0:COARSE].astype(F32)
    lane = lax.broadcasted_iota(jnp.int32, (1, 1, 128), 2)

    def tap_sum(values, grads):
        return fold_rows(values * grads)

    def reduce_back(pair, red, conv, gain, shifts, kv, small, kv_g):
        hat, inverse = norm_hat(red[...])
        normed = hat * gain[...] + shifts[1:2, :]
        cdf, bell = gauss(normed)
        active = (normed * cdf).astype(BF16)
        kv_g[...] = dot_in(active, pair)
        small[9:10, :] = jnp.sum(pair.astype(F32), axis=0, keepdims=True)
        grad = dot_t(pair, kv) * gelu_slope(normed, cdf, bell)
        small[11:12, :] = jnp.sum(grad * hat, axis=0, keepdims=True)
        small[12:13, :] = jnp.sum(grad, axis=0, keepdims=True)
        dc = norm_back(grad * gain[...], hat, inverse).astype(BF16)
        small[13:14, :] = jnp.sum(dc.astype(F32), axis=0, keepdims=True)
        return dc

    small_c[...] = jnp.zeros(small_c.shape, F32)
    small_f[...] = jnp.zeros(small_f.shape, F32)

    vals = val_ref[:, 0:COARSE, :]
    ext = grad_ref[:, 0:COARSE, :]
    ext = jnp.where(lane < 64, ext, ext.astype(BF16).astype(F32))
    mid = ext[1:-1]
    near = (by_band(vals[:-2], above), vals[1:-1], by_band(vals[2:], below))
    for a in range(3):
        for b in range(3):
            moved = near[a] if b == 1 else roll_cells(near[a], 1 - b)
            small_c[3 * a + b : 3 * a + b + 1, :] = jnp.sum(
                tap_sum(moved, mid), axis=0, keepdims=True
            )
    small_c[10:11, :] = jnp.sum(mid.reshape(-1, 128), axis=0, keepdims=True)
    pair = mid + depthwise_coarse(ext, above, below, taps_c, flip=True)
    pair = jnp.where(cell_valid(pair.shape, 1), pair, 0.0)
    pair = pair.reshape(bands * COARSE, 128).astype(BF16)
    dc = reduce_back(pair, red_c, conv_c, gain_c, shifts_c, kv_c[...], small_c, kv_c_g)
    for i in range(16):
        part = slice(i * 128, (i + 1) * 128)
        conv_c_g[part, :] = dot(xt[i], dc)
        back = dot(dc, turned_c[:, part]).reshape(bands, 16, 128)
        dxn[:, 16 * i : 16 * i + 16, :] += back

    conv.advance(1, shared_pieces(0, CONV, late_rows))
    before.advance()
    swaps[1].wait()
    grad_ref[here, COARSE:CELLS] = own[:, COARSE:CELLS] + recv[:, COARSE:CELLS].astype(F32)
    vals = val_ref[:, COARSE:CELLS, :]
    ext = grad_ref[:, COARSE:CELLS, :]
    ext = jnp.where(lane >= 64, ext, ext.astype(BF16).astype(F32))
    rows = depthwise_fine(ext, above, below, taps_f, flip=True)
    near = fine_rows(vals, above, below)
    mids = fine_rows(ext, above, below)[1]
    for a in range(3):
        for b in range(3):
            total = jnp.zeros((8, 128), F32)
            for row in range(2):
                even, odd = near[a][row][:, 0], near[a][row][:, 1]
                grad_even, grad_odd = mids[row][:, 0], mids[row][:, 1]
                if b == 0:
                    moved = (roll_cells(odd, 1), even)
                elif b == 1:
                    moved = (even, odd)
                else:
                    moved = (odd, roll_cells(even, -1))
                total = total + tap_sum(moved[0], grad_even) + tap_sum(moved[1], grad_odd)
            small_f[3 * a + b : 3 * a + b + 1, :] = jnp.sum(total, axis=0, keepdims=True)
    small_f[10:11, :] = jnp.sum(ext[1:-1].reshape(-1, 128), axis=0, keepdims=True)
    valid = cell_valid((bands, 16, 128), 1)
    blocks = []
    for row in range(2):
        for column in range(2):
            block = jnp.where(valid, mids[row][:, column] + rows[row][column], 0.0)
            blocks.append(block.astype(BF16).reshape(bands, 1, 16, 128))
    pair = jnp.concatenate(blocks, axis=1).reshape(bands * FINE, 128)
    conv.advance()
    dc = reduce_back(pair, red_f, conv_f, gain_f, shifts_f, kv_f_sw, small_f, kv_f_g)
    for i in range(4):
        part = slice(i * 128, (i + 1) * 128)
        total = None
        for row in range(2):
            for column in range(2):
                cells = dc.reshape(bands, 4, 16, 128)[:, 2 * row + column].reshape(bands * 16, 128)
                product = dot(xt[fine_slot(i, row, column)], cells)
                total = product if total is None else total + product
        conv_f_g[part, :] = total
        back = dot(dc, turned_f[:, part]).reshape(bands, 4, 16, 128)
        for row in range(2):
            for column in range(2):
                slot = 16 * fine_slot(i, row, column)
                dxn[:, slot : slot + 16, :] += back[:, 2 * row + column]

    front_g[...] = jnp.zeros(front_g.shape, F32)
    sums = jnp.zeros((8, 128), F32)
    along = jnp.zeros((8, 128), F32)
    for band in range(bands):
        grad = dxn[band]
        sums = sums + fold_rows(grad)
        along = along + fold_rows(grad * hat_ref[band].astype(F32))
    front_g[0:1, :] = jnp.sum(along, axis=0, keepdims=True)
    front_g[1:2, :] = jnp.sum(sums, axis=0, keepdims=True)

    small_phase(0)
    rest.advance(1, shared_pieces(4 * CONV, REST, later_rows))
    conv.advance()
    before.advance()
    place = from_slots()

    def one_band(band):
        at = slice(band * BAND, (band + 1) * BAND)
        back = norm_back(dxn[band] * gains[0:1, :], hat_ref[band].astype(F32), 1.0)
        tok_grad[at, :] = dx1[at, :] + dot(place, back.astype(BF16)) * inv[at, :]

    done, total = 0, len(rest.left) + 1 + len(gather.left)
    for number in range(1, total + 1):
        while done < bands and done * total < number * bands:
            one_band(done)
            done += 1
        if rest.left:
            rest.advance()
            conv.advance()
            before.advance()
        elif number + len(gather.left) == total:
            conv.advance(len(conv.left))
            before.advance(len(before.left))
            gather.begin([conv.finish(), rest.finish(), before.finish()])
        else:
            gather.advance()
        if number <= len(order):
            small_phase(number)


def shared_rows(start, count):
    done = 0
    while done < count:
        group = 0 if start + done < 4 * CONV else 1
        if group == 0:
            quarter, row = divmod(start + done, CONV)
            size = min(count - done, CONV - row)
        else:
            quarter, row = divmod(start + done - 4 * CONV, REST)
            size = min(count - done, REST - row)
        yield group, quarter % 2, quarter // 2, row, done, size
        done += size


def unpack_kernel(
    levels,     joint, little, tok_grad,
    tok_grad_out, gains, shifts, query, conv_c, gain_c, shifts_c, kv_c, taps_c, conv_f, gain_f, shifts_f, kv_f,
    taps_f, proj, hidden, fc1, depth, fc2,
):
    side = lax.axis_index("heads")
    half = query.shape[0]
    pieces, wide = joint.shape[2], fc2.shape[0]
    widths = [group_size(levels, part) // pieces for part in (CONV, REST, SPLIT)]
    first, second = widths[0], widths[0] + widths[1]
    spans = (slice(0, first), slice(first, second), slice(second, second + widths[2]))

    def quarter_rows(group, core, h):
        return joint[core, h, :, spans[group], :].reshape(-1, 128)

    tok_grad_out[...] = tok_grad[...]

    def rows_of(start, count):
        pieces = [
            quarter_rows(group, core, h)[at : at + size].astype(F32)
            for group, core, h, at, _, size in shared_rows(start, count)
        ]
        return pieces[0] if len(pieces) == 1 else jnp.concatenate(pieces, axis=0)

    start = 0
    for ref in (conv_c, conv_f, kv_c):
        count = ref.shape[0]
        for group, core, h, at, offset, size in shared_rows(start, count):
            ref[offset : offset + size, :] = quarter_rows(group, core, h)[at : at + size].astype(F32)
        start += count
    kv_f[...] = swap_lanes(rows_of(start, 128))
    both = rows_of(start + 128, 128)
    query[...] = jnp.where(side == 0, both[:, :half], both[:, half:]).T
    proj[...] = rows_of(start + 256, 128)
    small = little[...]
    coarse, fine, front, mid = small[0:16], small[16:32], small[32:40], small[40:48]
    taps_c[...] = coarse[0:9, half:]
    taps_f[...] = fine[0:9, :half]
    gain_c[...] = coarse[11:12]
    gain_f[...] = fine[11:12]
    shifts_c[0:1, :] = coarse[13:14]
    shifts_c[1:2, :] = coarse[12:13]
    shifts_c[2:3, :] = jnp.concatenate([coarse[9:10, half:], coarse[10:11, half:]], axis=1)
    shifts_f[0:1, :] = fine[13:14]
    shifts_f[1:2, :] = fine[12:13]
    shifts_f[2:3, :] = jnp.concatenate([fine[9:10, :half], fine[10:11, :half]], axis=1)
    gains[0:1, :] = front[0:1]
    gains[1:2, :] = mid[0:1]
    shifts[0:1, :] = front[1:2]
    shifts[1:2, :] = mid[2:3]
    shifts[2:3, :] = mid[1:2]
    shifts[3:4, :] = mid[3:4]
    for core in range(2):
        split = quarter_rows(2, core, side)
        for i in range(2):
            lanes = slice(core * STEP + i * 128, core * STEP + i * 128 + 128)
            fc1[:, lanes] = split[i * 128 : i * 128 + 128].astype(F32)
            block = split[512 + 16 * i : 528 + 16 * i].astype(F32)
            depth[:, lanes] = block[0:9]
            hidden[:, lanes] = block[9:11]
        fc2[core * STEP : core * STEP + STEP, :] = split[256:512].astype(F32)


SMEM = pl.BlockSpec(memory_space=pltpu.SMEM)
VMEM = pl.BlockSpec(memory_space=pltpu.VMEM)
HBM = pl.BlockSpec(memory_space=pl.ANY)


def shape(dims, kind=F32):
    return jax.ShapeDtypeStruct(dims, kind)


def params(limit=56):
    return pltpu.CompilerParams(vmem_limit_bytes=limit * MIB)


def sending(number, limit=56):
    return pltpu.CompilerParams(
        vmem_limit_bytes=limit * MIB, collective_id=number, has_side_effects=True
    )


def per_device(
    size, tokens, image_bands, cotangent, front_gains, front_shifts, query_w, coarse_conv,
    coarse_gain, coarse_shifts, coarse_kv, coarse_taps, fine_conv, fine_gain, fine_shifts, fine_kv,
    fine_taps, proj_w, hidden_shifts, fc1_w, depth_taps, fc2_w,
):
    count = tokens.shape[0]
    rows = count // W
    bands = count // BAND
    total = 2 * bands
    halo = 2 * W
    half = coarse_kv.shape[1] // 2
    mine = fc1_w.shape[1]
    hidden = 2 * mine
    gain_c, gain_f = coarse_gain[None], fine_gain[None]
    semaphores = pltpu.SemaphoreType.DMA
    levels = size.bit_length() - 1
    query_t = query_w.T

    (
        table, meta, xn, hat, inverse, red_c, red_f, slab, other, query_o,
    ) = pl.pallas_call(
        front_kernel,
        out_shape=(
            shape((3, 32), jnp.int32),
            shape((3, total, 8, 128)),
            shape((bands, SLOTS, 128), BF16),
            shape((bands, SLOTS, 128), BF16),
            shape((count, 128)),
            shape((bands * COARSE, 128)),
            shape((bands * FINE, 128)),
            shape((bands, CELLS, 128)),
            shape((bands, CELLS, 128), BF16),
            shape(query_t.shape, BF16),
        ),
        in_specs=[SMEM] + [VMEM] * 12,
        out_specs=[SMEM] + [VMEM] * 9,
        scratch_shapes=[pltpu.VMEM((bands, CELLS, 128), BF16), semaphores((8,)), semaphores((8,))],
        compiler_params=sending(1),
        name="front",
    )(
        image_bands, tokens, front_gains, front_shifts, coarse_conv, gain_c, coarse_shifts,
        coarse_kv, fine_conv, gain_f, fine_shifts, fine_kv,
        query_t,
    )

    each = 4 if bands % 4 == 0 else 2
    some_bands = pl.BlockSpec((each * BAND, 128), lambda i: (i, 0))
    some_slots = pl.BlockSpec((each, SLOTS, 128), lambda i: (i, 0, 0))
    two_slots = pl.BlockSpec((2, SLOTS, 128), lambda i: (i, 0, 0))
    (
        x1, xm, heads_out, out_t, lse, key_c, key_f, val_c, val_f, fc1_o, fc2_o, depth_o, hidden_o,
        cot_o,
    ) = pl.pallas_call(
        attend_kernel,
        grid=(bands // each,),
        out_shape=(
            shape((count, 128)),
            shape((count, 128), BF16),
            shape((count, 128), BF16),
            shape((bands, 128, SLOTS)),
            shape((bands, 8, SLOTS)),
            shape((total, COARSE, 128), BF16),
            shape((total, PACKED, 128)),
            shape((total, COARSE, 128), BF16),
            shape((total, PACKED, 128)),
            shape(fc1_w.shape, BF16),
            shape(fc2_w.shape, BF16),
            shape(depth_taps.shape),
            shape(hidden_shifts.shape),
            shape((halo, 128), BF16),
        ),
        in_specs=[SMEM] + [VMEM] * 7 + [some_slots, some_bands] + [VMEM] * 5 + [HBM] * 5,
        out_specs=[
            some_bands,
            some_bands,
            some_bands,
            pl.BlockSpec((each, 128, SLOTS), lambda i: (i, 0, 0)),
            pl.BlockSpec((each, 8, SLOTS), lambda i: (i, 0, 0)),
        ]
        + [VMEM] * 4
        + [HBM] * 5,
        scratch_shapes=[
            pltpu.VMEM((total + 2, CELLS, 128), F32),
            pltpu.VMEM((128, 128), BF16),
            pltpu.VMEM((BAND, SLOTS), BF16),
            semaphores((5,)),
            semaphores((5,)),
        ],
        compiler_params=sending(4),
        name="attend",
    )(
        table, slab, other, meta, coarse_taps, fine_taps, coarse_shifts, fine_shifts, xn, tokens,
        query_t, query_o, proj_w, front_gains, front_shifts, fc1_w, fc2_w, depth_taps,
        hidden_shifts, cotangent,
    )

    extra = 64
    output, dx1, out_grad, split_g, mid_g = pl.pallas_call(
        hidden_kernel,
        out_shape=(
            shape((count, 128), BF16),
            shape((count, 128)),
            shape((bands, SLOTS, 128), BF16),
            shape((2, 2, SPLIT, 128)),
            shape((136, 128)),
        ),
        in_specs=[SMEM, HBM] + [VMEM] * 3 + [HBM] + [VMEM] * 11,
        out_specs=[VMEM] * 5,
        scratch_shapes=[
            pltpu.VMEM((count + 2 * halo, 128), BF16),
            pltpu.VMEM((halo, 128), BF16),
            pltpu.VMEM((8, rows + 4, W, 128), F32),
            pltpu.VMEM((count + extra, WIDE), BF16),
            pltpu.VMEM((KEPT, count), BF16),
            pltpu.VMEM((WIDE, hidden), BF16),
            pltpu.VMEM((hidden, TAPS * 128), BF16),
            pltpu.VMEM((16, hidden), F32),
            pltpu.VMEM((16, hidden), F32),
            pltpu.VMEM((128, hidden), BF16),
            pltpu.VMEM((128, hidden), BF16),
            pltpu.VMEM((count + extra, 128), BF16),
            pltpu.VMEM((128, count), BF16),
            pltpu.VMEM((count, hidden), BF16),
            pltpu.VMEM((count + extra, hidden), BF16),
            pltpu.VMEM((KEPT, SPAN), F32),
            pltpu.VMEM((count, 128), F32),
            pltpu.VMEM((count, 128), F32),
            pltpu.VMEM((count, 128), F32),
            pltpu.VMEM((count, 128), BF16),
            semaphores(()),
            semaphores(()),
            semaphores((2,)),
        ],
        compiler_params=sending(2, 63),
        name="hidden",
    )(
        table, x1, xm, cotangent, cot_o, heads_out, fc1_w, fc1_o, fc2_w, fc2_o, depth_taps, depth_o,
        hidden_shifts, hidden_o, front_gains, front_shifts, proj_w,
    )

    dq, grad_own, grad_send, output = pl.pallas_call(
        attend_back_kernel,
        grid=(bands // 2,),
        out_shape=(
            shape((bands, SLOTS, 128), BF16),
            shape((bands + 1, CELLS, 128)),
            shape((bands + 1, CELLS, 128), BF16),
            shape((count, 128), BF16),
        ),
        in_specs=[SMEM]
        + [VMEM] * 4
        + [
            two_slots,
            VMEM,
            VMEM,
            two_slots,
            pl.BlockSpec((2, 128, SLOTS), lambda i: (i, 0, 0)),
            pl.BlockSpec((2, 8, SLOTS), lambda i: (i, 0, 0)),
            pl.BlockSpec((2 * BAND, 128), lambda i: (i, 0)),
        ],
        out_specs=[two_slots, VMEM, VMEM, pl.BlockSpec((2 * BAND, 128), lambda i: (i, 0))],
        scratch_shapes=[
            pltpu.VMEM((total, COARSE, 128), F32),
            pltpu.VMEM((total, FINE, 128), F32),
            pltpu.VMEM((128, 128), BF16),
            pltpu.VMEM((2, 64, MAX_BANDS * COARSE), BF16),
            pltpu.VMEM((2, 2, 64, HALVES[0][1] * PACKED), BF16),
            pltpu.VMEM((2, MAX_BANDS * PACKED, 128), BF16),
            pltpu.VMEM((2, MAX_BANDS * PACKED, 128), BF16),
            pltpu.SMEM((2,), jnp.int32),
        ],
        compiler_params=params(),
        name="attend_back",
    )(table, key_c, key_f, val_c, val_f, xn, query_t, query_o, out_grad, out_t, lse, output)

    peers = sum(2 ** len(dims) - 1 for dims in stages(levels, True))
    links = group_links(levels, False) + 3 * group_links(levels, True) + len(stages(levels, True)) + 1
    early_rows, late_rows, later_rows = (group_size(levels, part) for part in (SPLIT, CONV, REST))
    pieces = 2 ** (levels - 1)
    joint_rows = (early_rows + late_rows + later_rows) // pieces
    tokens_grad, joint, little = pl.pallas_call(
        functools.partial(tail_kernel, levels),
        out_shape=(
            shape((count, 128)),
            shape((2, 2, pieces, joint_rows, 128), BF16),
            shape((SMALL, 128)),
        ),
        in_specs=[HBM] * 3 + [VMEM, HBM] + [VMEM] * 2 + [HBM] * 3 + [VMEM] * 2 + [HBM] * 2
        + [VMEM] + ([HBM] * 2 + [VMEM] * 4) * 2,
        out_specs=[VMEM] * 3,
        scratch_shapes=[
            pltpu.VMEM((4 * QUARTER, 128), F32),
            pltpu.VMEM((len(stages(levels, True)), SMALL, 128), F32),
            pltpu.VMEM((peers, SMALL, 128), F32),
            semaphores((2, peers)),
            pltpu.VMEM((bands + 1, CELLS, 128), BF16),
            pltpu.VMEM((bands + 2, CELLS, 128), F32),
            pltpu.VMEM((bands + 2, CELLS, 128), F32),
            pltpu.VMEM((bands, SLOTS, 128), F32),
            semaphores((2,)),
            semaphores((2,)),
            semaphores((links,)),
            semaphores((links,)),
            pltpu.VMEM((128, coarse_conv.shape[0]), BF16),
            pltpu.VMEM((128, fine_conv.shape[0]), BF16),
            pltpu.VMEM((count, 128), F32),
            pltpu.VMEM((count, 128), F32),
            pltpu.VMEM((bands, SLOTS, 128), BF16),
            pltpu.VMEM(grad_own.shape, F32),
            pltpu.VMEM(split_g.shape, F32),
            pltpu.VMEM(slab.shape, F32),
            pltpu.VMEM(xn.shape, BF16),
            pltpu.VMEM(dq.shape, BF16),
            pltpu.VMEM(red_c.shape, F32),
            pltpu.VMEM(coarse_conv.shape, BF16),
            pltpu.VMEM(red_f.shape, F32),
            pltpu.VMEM(fine_conv.shape, BF16),
            pltpu.VMEM((16, 128, bands * 16), BF16),
            semaphores((12,)),
        ]
        + group_scratch(levels, False, early_rows)
        + group_scratch(levels, True, late_rows)
        + group_scratch(levels, True, later_rows),
        compiler_params=sending(0),
        name="tail",
    )(
        grad_own, grad_send, split_g, mid_g, slab, other, meta, xn, hat, dq, query_t, query_o, dx1,
        inverse, front_gains,
        red_c, coarse_conv, gain_c, coarse_shifts, coarse_kv, coarse_taps,
        red_f, fine_conv, gain_f, fine_shifts, fine_kv, fine_taps,
    )
    grads = pl.pallas_call(
        functools.partial(unpack_kernel, levels),
        out_shape=(
            shape((count, 128)),
            shape((2, 128)),
            shape((4, 128)),
            shape((half, 128)),
            shape(coarse_conv.shape),
            shape((1, 128)),
            shape((3, 128)),
            shape((128, 128)),
            shape((9, half)),
            shape(fine_conv.shape),
            shape((1, 128)),
            shape((3, 128)),
            shape((128, 128)),
            shape((9, half)),
            shape((128, 128)),
            shape((2, mine)),
            shape((128, mine)),
            shape((9, mine)),
            shape((mine, 128)),
        ),
        in_specs=[VMEM] * 3,
        out_specs=[VMEM] * 19,
        compiler_params=params(),
        name="unpack",
    )(joint, little, tokens_grad)
    grads = [output] + list(grads)
    grads[4] = grads[4].T
    for at in (6, 11):
        grads[at] = grads[at].reshape(128)
    return tuple(grads)


def solution(mesh):
    tokens = P(("batch", "heads"), None)
    columns = P(None, "heads")
    return jax.shard_map(
        functools.partial(per_device, mesh.shape["batch"]),
        mesh=mesh,
        in_specs=(tokens, P("batch", None), tokens, P(), P(), columns)
        + (P(),) * 11
        + (columns, columns, columns, P("heads", None)),
        out_specs=(tokens, tokens, P(), P(), columns)
        + (P(),) * 11
        + (columns, columns, columns, P("heads", None)),
        check_vma=False,
    )
```

```python
import functools

import jax
import jax.numpy as jnp
from jax import lax
from jax.experimental import pallas as pl
from jax.experimental.pallas import tpu as pltpu
from jax.sharding import PartitionSpec as P

W = 56
BAND = 4 * W
SLOTS = 256
COARSE = 16
FINE = 64
CELLS = COARSE + FINE
MAX_BANDS = 14
EPS = 1e-06
F32 = jnp.float32
BF16 = jnp.bfloat16
SCALE = 32**-0.5
LOG2E = 1.4426950408889634
ROOT = 0.7071067811865476
EXP_SCALE = SCALE * LOG2E
BIG = -1e9
MIB = 1024 * 1024
STEP = 256
SPAN = 512
MESH = pl.DeviceIdType.MESH
TAPS = 9
KEPT = TAPS * 128 + 16
WIDE = (TAPS + 1) * 128
QUARTER = 768
CONV = 512
REST = QUARTER - CONV
SMALL = 48
SPLIT = 544


def dot(left, right):
    return jnp.dot(left, right, preferred_element_type=F32)


def dot_t(left, right):
    return lax.dot_general(left, right, (((1,), (1,)), ((), ())), preferred_element_type=F32)


def dot_in(left, right):
    return lax.dot_general(left, right, (((0,), (0,)), ((), ())), preferred_element_type=F32)


def gauss(values):
    return 0.5 + 0.5 * lax.erf(values * ROOT), jnp.exp2(values * values * (-0.5 * LOG2E))


def gelu_slope(values, cdf, bell):
    return cdf + values * bell * 0.3989422804014327


def fold_rows(values):
    wide = jnp.sum(values.reshape(-1, 64, 128), axis=0)
    return jnp.sum(wide.reshape(8, 8, 128), axis=0)


def norm_hat(values):
    centred = values - jnp.mean(values, axis=-1, keepdims=True)
    inverse = lax.rsqrt(jnp.mean(centred * centred, axis=-1, keepdims=True) + EPS)
    return centred * inverse, inverse


def norm_back(grad_scaled, hat, inverse):
    centre = jnp.mean(grad_scaled, axis=-1, keepdims=True)
    along = jnp.mean(grad_scaled * hat, axis=-1, keepdims=True)
    return inverse * (grad_scaled - centre - hat * along)


def slot_map(slot, token):
    a, b, c = slot >> 6, (slot >> 4) & 3, slot & 15
    hit = (token == a * W + 4 * c + b) & (c < 14)
    return jnp.where(hit, 1.0, 0.0).astype(BF16)


def to_slots():
    shape = (SLOTS, BAND)
    return slot_map(
        lax.broadcasted_iota(jnp.int32, shape, 0), lax.broadcasted_iota(jnp.int32, shape, 1)
    )


def from_slots():
    shape = (BAND, SLOTS)
    return slot_map(
        lax.broadcasted_iota(jnp.int32, shape, 1), lax.broadcasted_iota(jnp.int32, shape, 0)
    )


def cell_valid(shape, axis):
    return (lax.broadcasted_iota(jnp.int32, shape, axis) & 15) < 14


def roll_cells(values, step):
    lead = values.shape[:-2]
    flat = values.reshape(-1, values.shape[-1])
    flat = pltpu.roll(flat, step % flat.shape[0], 0)
    return flat.reshape(lead + values.shape[-2:])


def by_band(values, mask):
    count = values.shape[0]
    wide = values.reshape(count, -1, 8, 128) * mask.reshape(count, 1, 8, 128)
    return wide.reshape(values.shape)


def row_taps(taps, flip):
    order = [8 - i for i in range(9)] if flip else list(range(9))
    return [taps[i : i + 1, :] for i in order]


def depthwise_coarse(ext, above, below, taps, flip=False):
    t = row_taps(taps, flip)
    up, mid, down = by_band(ext[:-2], above), ext[1:-1], by_band(ext[2:], below)
    left, centre, right = (up * t[b] + mid * t[3 + b] + down * t[6 + b] for b in range(3))
    return centre + roll_cells(left, 1) + roll_cells(right, -1)


def fine_rows(ext, above, below):
    bands = ext.shape[0] - 2
    grid = ext.reshape(bands + 2, 2, 2, 16, 128)
    first, second = grid[:, 0], grid[:, 1]
    up = (by_band(second[:-2], above), first[1:-1])
    mid = (first[1:-1], second[1:-1])
    down = (second[1:-1], by_band(first[2:], below))
    return up, mid, down


def depthwise_fine(ext, above, below, taps, flip=False):
    t = row_taps(taps, flip)
    ups, mids, downs = fine_rows(ext, above, below)
    rows = []
    for up, mid, down in zip(ups, mids, downs):
        left, centre, right = (up * t[b] + mid * t[3 + b] + down * t[6 + b] for b in range(3))
        even = centre[:, 0] + roll_cells(left[:, 1], 1) + right[:, 1]
        odd = centre[:, 1] + left[:, 0] + roll_cells(right[:, 0], -1)
        rows.append((even, odd))
    return rows


def greet(*peers):
    barrier = pltpu.get_barrier_semaphore()
    for peer in peers:
        pl.semaphore_signal(barrier, inc=1, device_id=peer, device_id_type=MESH)


def met(count):
    pl.semaphore_wait(pltpu.get_barrier_semaphore(), count)


def fetch(pairs, sems):
    loads = [pltpu.make_async_copy(source, target, sems.at[i]) for i, (source, target) in enumerate(pairs)]
    for load in loads:
        load.start()
    return loads


def link(source, target, send_sem, recv_sem, peer):
    return pltpu.make_async_remote_copy(
        src_ref=source,
        dst_ref=target,
        send_sem=send_sem,
        recv_sem=recv_sem,
        device_id=peer,
        device_id_type=MESH,
    )


def remote(source, target, send_sem, recv_sem, peer):
    made = link(source, target, send_sem, recv_sem, peer)
    made.start()
    return made


def across():
    return (lax.axis_index("batch"), 1 - lax.axis_index("heads"))


def swap_lanes(values):
    half = values.shape[1] // 2
    return jnp.concatenate([values[:, half:], values[:, :half]], axis=1)


def keep_lanes(values, upper):
    lane = lax.broadcasted_iota(jnp.int32, values.shape, 1)
    return jnp.where((lane >= 64) if upper else (lane < 64), values, 0.0)


def pad_taps(taps, upper):
    gap = jnp.zeros(taps.shape, F32)
    return jnp.concatenate([gap, taps] if upper else [taps, gap], axis=1)


def band_tables(heights, table, meta, total):
    count = heights.shape[1]
    number = jnp.int32(0)
    start = jnp.int32(0)
    end = heights[0, 0]
    last = jnp.int32(-2)
    images, sames = [], []
    for band in range(total):
        passed = band >= end
        number = jnp.where(passed, number + 1, number)
        start = jnp.where(passed, end, start)
        grown = heights[0, jnp.minimum(number, count - 1)]
        grown = jnp.where(number < count, grown, 0)
        end = jnp.where(passed, end + grown, end)
        image = jnp.where(band < end, number, -1)
        same = jnp.where(image == last, 1, 0)
        last = image
        table[0, band] = image
        table[1, band] = jnp.minimum(start, total - MAX_BANDS)
        table[2, band] = same
        images.append(image)
        sames.append(same)
    for band in range(total, table.shape[1]):
        for row in range(3):
            table[row, band] = jnp.int32(0)
    sames.append(jnp.int32(0))
    for band in range(total):
        for row, value in enumerate((sames[band], sames[band + 1], images[band])):
            meta[row, band] = jnp.full((8, 128), value.astype(F32), F32)


def front_kernel(
    heights, tok, gains, shifts, conv_c, gain_c, shifts_c, kv_c, conv_f, gain_f, shifts_f, kv_f,
    query_t,
    table, meta, xn_out, hat_out, inv_out, red_c, red_f, slab, other, query_o,
    send, send_sems, recv_sems,
):
    bands = xn_out.shape[0]
    peer = across()
    greet(peer)
    copies = []

    def give(source, target):
        at = len(copies)
        copies.append(remote(source, target, send_sems.at[at], recv_sems.at[at], peer))

    place = to_slots()

    def norm_bands(first, count):
        rows = slice(first * BAND, (first + count) * BAND)
        hat, inverse = norm_hat(tok[rows, :].astype(F32))
        inv_out[rows, :] = jnp.broadcast_to(inverse, hat.shape)
        normed = (hat * gains[0:1, :] + shifts[0:1, :]).astype(BF16)
        sides = jnp.concatenate([normed, hat.astype(BF16)], axis=1)
        for band in range(count):
            both = dot(place, sides[band * BAND : (band + 1) * BAND]).astype(BF16)
            xn_out[first + band] = both[:, :128]
            hat_out[first + band] = both[:, 128:]

    def reduce(patches, conv, gain, shift, kv, out, at):
        red = dot(patches, conv) + shift[0:1, :]
        out[at : at + red.shape[0], :] = red
        hat, _ = norm_hat(red)
        normed = hat * gain[...] + shift[1:2, :]
        cdf, _ = gauss(normed)
        return dot((normed * cdf).astype(BF16), kv)

    kv_f_sw = swap_lanes(kv_f[...])
    part = bands // 2
    for first in (0, part):
        norm_bands(first, part)
        grid = xn_out[first : first + part].reshape(part, 16, 16, 128)
        patches = jnp.concatenate([fine_patch(grid, i) for i in range(4)], axis=1)
        pair = reduce(patches, conv_f[...], gain_f, shifts_f, kv_f_sw, red_f, first * FINE)
        pair = pair + keep_lanes(shifts_f[2:3, :], False)
        pair = jnp.where(cell_valid(pair.shape, 0), pair, 0.0).reshape(part, FINE, 128)
        slab[first : first + part, COARSE:CELLS, :] = pair
        send[first : first + part, COARSE:CELLS, :] = pair.astype(BF16)
        here = (pl.ds(first, part), pl.ds(COARSE, FINE))
        if first == 0:
            met(1)
        give(send.at[here], other.at[here])
        if first == 0:
            give(query_t, query_o)
    grid = xn_out[...].reshape(bands, 16, 16, 128)
    patches = jnp.concatenate([grid[:, i].reshape(bands * 16, 128) for i in range(16)], axis=1)
    pair = reduce(patches, conv_c[...], gain_c, shifts_c, kv_c[...], red_c, 0)
    pair = pair + keep_lanes(swap_lanes(shifts_c[2:3, :]), True)
    pair = jnp.where(cell_valid(pair.shape, 0), pair, 0.0).reshape(bands, COARSE, 128)
    slab[:, 0:COARSE, :] = pair
    send[:, 0:COARSE, :] = pair.astype(BF16)
    here = pl.ds(0, COARSE)
    give(send.at[:, here], other.at[:, here])
    band_tables(heights, table, meta, 2 * bands)
    for made in copies:
        made.wait()


def fine_slot(part, row, column):
    return (2 * row + (part >> 1)) * 4 + 2 * column + (part & 1)


def fine_patch(grid, part):
    bands = grid.shape[0]
    blocks = [
        grid[:, fine_slot(part, row, column)].reshape(bands, 1, 16, 128)
        for row in range(2)
        for column in range(2)
    ]
    return jnp.concatenate(blocks, axis=1).reshape(bands * FINE, 128)


def head_lanes(values, head):
    lane = lax.broadcasted_iota(jnp.int32, values.shape, 1)
    return jnp.where((lane >> 5) == head, values, jnp.zeros((), BF16))


def head_rows(values, head):
    row = lax.broadcasted_iota(jnp.int32, values.shape, 0)
    return jnp.where((row >> 5) == head, values, jnp.zeros((), BF16))


def score_rows(query_t, head, image, fine):
    row = lax.broadcasted_iota(jnp.int32, query_t.shape, 0)
    tag = row if fine else row - 64
    fill = jnp.where((tag >= 0) & (tag <= NOBODY) & (tag != image), BIG, 0.0).astype(BF16)
    return jnp.where((row >> 5) == head, query_t, fill)


def with_offset(rows, at, offset):
    start = at // 16 * 16
    block = rows[start : start + 16]
    row = lax.broadcasted_iota(jnp.int32, block.shape, 0)
    for i in range(3):
        term = offset.astype(BF16)
        block = jnp.where(row == at - start + i, term, block)
        offset = offset - term.astype(F32)
    parts = [rows[:start]] if start else []
    return jnp.concatenate(parts + [block, rows[start + 16 :]], axis=0)


def full_query(query_t, query_o, side):
    own, other = query_t[...].astype(F32), query_o[...].astype(F32)
    return jnp.where(
        side == 0,
        jnp.concatenate([own, other], axis=0),
        jnp.concatenate([other, own], axis=0),
    )


def window(ref, first):
    part = ref[pl.ds(first, MAX_BANDS)]
    return part.reshape(-1, 128).astype(BF16)


PACKED = 56
CHUNKS = ((0, 224), (224, 224), (448, 224), (672, 112))
HALVES = ((0, 8), (8, 6))
NOBODY = 32
ONES = 40


def tree_max(values):
    count = values.shape[0]
    while count % 16 == 0:
        count //= 2
        values = jnp.maximum(values[:count], values[count:])
    return jnp.max(values, axis=0, keepdims=True)


def attend_kernel(
    table, slab, other, meta, taps_c, taps_f, shifts_c, shifts_f, xn, tok, query_t, query_o, proj_w,
    gains, shifts, fc1, fc2, depth, hidden, cot,
    x1_out, xm_out, o_out, ot_out, lse_out, key_c, key_f, val_c, val_f, fc1_o, fc2_o, depth_o,
    hidden_o, cot_o,
    grid_ref, query_ref, place_ref, send_sems, recv_sems,
):
    step = pl.program_id(0)
    bands = slab.shape[0]
    total = 2 * bands
    side = lax.axis_index("heads")
    peer = across()
    halo = 2 * W
    edge = pl.multiple_of((1 - side) * (cot.shape[0] - halo), 16)
    swaps = [
        link(source, target, send_sems.at[i], recv_sems.at[i], peer)
        for i, (source, target) in enumerate(
            (
                (cot.at[pl.ds(edge, halo)], cot_o),
                (depth, depth_o),
                (hidden, hidden_o),
                (fc1, fc1_o),
                (fc2, fc2_o),
            )
        )
    ]

    @pl.when(step == 0)
    def _():
        greet(peer)
        place_ref[...] = from_slots()
        query_ref[...] = full_query(query_t, query_o, side).T.astype(BF16)
        grid_ref[0] = jnp.zeros((CELLS, 128), F32)
        grid_ref[total + 1] = jnp.zeros((CELLS, 128), F32)
        grid_ref[pl.ds(1 + side * bands, bands)] = slab[...]
        grid_ref[pl.ds(1 + (1 - side) * bands, bands)] = other[...].astype(F32)
        above, below, image = meta[0], meta[1], meta[2]
        lane = lax.broadcasted_iota(jnp.int32, (total, 16, 128), 2).astype(F32)
        valid = cell_valid((total, 16, 128), 1)
        wide = jnp.broadcast_to(image.reshape(total, 1, 8, 128), (total, 2, 8, 128))
        wide = wide.reshape(total, 16, 128)
        mark = jnp.where(valid & (wide >= 0.0), wide, float(NOBODY))

        ext = grid_ref[:, 0:COARSE, :]
        own = ext[1:-1]
        local = keep_lanes(shifts_c[2:3, :], True)
        mixed = own + depthwise_coarse(ext, above, below, pad_taps(taps_c[...], True)) + local
        val_c[...] = jnp.where(lane < 3.0, 1.0, mixed).astype(BF16)
        place = lane - 64.0
        one = (place >= ONES) & (place < ONES + 3)
        tag = jnp.where((place == mark) | one, 1.0, 0.0)
        keys = jnp.where(lane < 64.0, own, tag)
        key_c[...] = keys.astype(BF16)

        ext = grid_ref[:, COARSE:CELLS, :]
        local = keep_lanes(swap_lanes(shifts_f[2:3, :]), False)
        rows = depthwise_fine(ext, above, below, pad_taps(taps_f[...], False))
        tag = jnp.where((lane == mark) | ((lane >= ONES) & (lane < ONES + 3)), 1.0, 0.0)
        one = (lane >= 64.0) & (lane < 67.0)
        for row in range(2):
            for column in range(2):
                at = (2 * row + column) * 16
                own = ext[1:-1, at : at + 16, :]
                mixed = own + rows[row][column] + local
                cell = (2 * row + column) * 14
                val_f[:, cell : cell + 14, :] = jnp.where(one, 1.0, mixed)[:, 0:14]
                keys = jnp.where(lane >= 64.0, own.astype(BF16).astype(F32), tag)
                key_f[:, cell : cell + 14, :] = keys[:, 0:14]
        met(1)
        for swap in swaps:
            swap.start()

    each = xn.shape[0]
    images = [table[0, side * bands + each * step + i] for i in range(each)]
    firsts = [table[1, side * bands + each * step + i] for i in range(each)]
    queries = [
        dot(xn[i], query_ref[...]).astype(BF16).astype(F32).T.astype(BF16) for i in range(each)
    ]
    turned, windows = {}, {}

    def score(unit):
        i, head, part = unit
        fine = head >= 2
        start, size = CHUNKS[part]
        rows = slice(start, start + size)
        if not head & 1:
            if part == 0:
                windows[i, fine] = [
                    window(ref, firsts[i]) for ref in ((key_f, val_f) if fine else (key_c, val_c))
                ]
            turned[i, fine, part] = windows[i, fine][1][rows].T
        keys = windows[i, fine][0][rows]
        return dot(keys, score_rows(queries[i], head, images[i], fine))

    outs = [[None] * 4 for _ in range(each)]
    mixed = {}
    lse_out[...] = jnp.zeros(lse_out.shape, F32)

    def mix(unit, scores):
        i, head, part = unit
        fine = head >= 2
        top = tree_max(scores) * EXP_SCALE
        expo = jnp.exp2(scores * EXP_SCALE - top).astype(BF16)
        row = 32 * (head & 1) + (0 if fine else 64)
        vals = turned[i, fine, part][row : row + 32]
        left = jnp.concatenate([vals, jnp.ones((16, CHUNKS[part][1]), BF16)], axis=0)
        done = mixed.setdefault((i, head), [])
        done.append((top, dot(left, expo)))
        if len(done) < (4 if fine else 1):
            return
        top = functools.reduce(jnp.maximum, [part_top for part_top, _ in done])
        total = None
        for part_top, value in done:
            value = value * jnp.exp2(part_top - top)
            total = value if total is None else total + value
        sums = total[32:33]
        lse_out[i, head : head + 1, :] = top + jnp.log2(sums)
        outs[i][head] = total[0:32] * (1.0 / sums)

    waiting = []
    for i in range(each):
        for head, parts in ((2, 4), (0, 1), (3, 4), (1, 1)):
            for part in range(parts):
                waiting.append(((i, head, part), score((i, head, part))))
                if len(waiting) > 6:
                    mix(*waiting.pop(0))
    for unit, scores in waiting:
        mix(unit, scores)
    place = place_ref[...]
    joined = []
    for i in range(each):
        live = jnp.where(images[i] >= 0, 1.0, 0.0)
        out_t = jnp.concatenate(outs[i], axis=0) * live
        ot_out[i] = out_t
        joined.append(dot(place, out_t.T.astype(BF16)).astype(BF16))
    heads_out = jnp.concatenate(joined, axis=0)
    o_out[...] = heads_out
    middle = tok[...].astype(F32) + dot(heads_out, proj_w[...]) + shifts[1:2, :]
    x1_out[...] = middle
    hat, _ = norm_hat(middle)
    xm_out[...] = (hat * gains[1:2, :] + shifts[2:3, :]).astype(BF16)

    @pl.when(step == pl.num_programs(0) - 1)
    def _():
        for swap in swaps:
            swap.wait()


def shift_right(values):
    column = lax.broadcasted_iota(jnp.int32, values.shape, 0)
    return jnp.where(column == 0, 0.0, pltpu.roll(values, 1, 0))


def shift_left(values):
    column = lax.broadcasted_iota(jnp.int32, values.shape, 0)
    return jnp.where(column == W - 1, 0.0, pltpu.roll(values, W - 1, 0))


def mask_lanes():
    lane = lax.broadcasted_iota(jnp.int32, (W, 128), 1)
    column = lax.broadcasted_iota(jnp.int32, (W, 128), 0)
    tap = jnp.where(lane < 32, lane & 15, 15)
    parts = []
    for a in range(3):
        hit = tap == 3 * a + 1
        hit = hit | ((tap == 3 * a) & (column > 0)) | ((tap == 3 * a + 2) & (column < W - 1))
        if a == 1:
            hit = hit | (tap == TAPS)
        parts.append(jnp.where(hit, 1.0, 0.0))
    return parts


def hidden_kernel(
    table, x1_in, xm, cot, cot_o, heads_in, fc1, fc1_o, fc2, fc2_o, depth, depth_o, hidden, hidden_o,
    gains, shifts, proj_w,
    out, dx1_out, do_out, split_g, mid_g,
    xm_ext, halo_ref, moved, wide, wide_t, weights, weights_t, taps, bias, base_ref, fc2_t, dy, dy_t, act, du,
    sums, dxm, out_acc, x1, heads_out, send_sem, recv_sem, load_sems,
):
    side = lax.axis_index("heads")
    peer = across()
    tokens = x1.shape[0]
    rows = tokens // W
    bands = tokens // BAND
    halo = 2 * W
    extra = wide.shape[0] - tokens
    mine = fc1.shape[1]
    width = 2 * mine
    halo_at = pl.multiple_of((1 - side) * (halo + tokens), 16)
    halo_row = 1 + (1 - side) * (rows + 1)
    greet(peer)
    loads = fetch(((x1_in, x1), (heads_in, heads_out)), load_sems)
    edge = pl.multiple_of((1 - side) * (tokens - halo), 16)
    swap = link(xm.at[pl.ds(edge, halo)], halo_ref, send_sem, recv_sem, peer)

    def live_band(band):
        return jnp.where(table[0, band] >= 0, 1.0, 0.0)

    def neighbour(row):
        place = side * rows - 2 + row
        band = jnp.maximum(place, 0) >> 2
        up = jnp.where((place & 3) == 0, table[2, band], 1)
        down = jnp.where((place & 3) == 3, table[2, band + 1], 1)
        return up.astype(F32), down.astype(F32)

    xm_ext[0:halo, :] = jnp.zeros((halo, 128), BF16)
    xm_ext[halo + tokens : tokens + 2 * halo, :] = jnp.zeros((halo, 128), BF16)
    xm_ext[halo : halo + tokens, :] = xm[...]
    for band in range(bands):
        at = slice(band * BAND, (band + 1) * BAND)
        dy[at, :] = (cot[at, :].astype(F32) * live_band(side * bands + band)).astype(BF16)
    tail = cot_o[...].astype(F32)
    tail = jnp.where(side == 0, tail[:W], tail[W:]) * live_band((1 - side) * bands + side * (bands - 1))
    tail = jnp.concatenate([tail, jnp.zeros((extra - W, 128), F32)], axis=0)
    dy[tokens : tokens + extra, :] = tail.astype(BF16)

    taps[...] = jnp.zeros(taps.shape, F32)
    bias[...] = jnp.zeros(bias.shape, F32)
    for part, (taps_ref, shift_ref, fc1_ref, fc2_ref) in enumerate(
        ((depth, hidden, fc1, fc2), (depth_o, hidden_o, fc1_o, fc2_o))
    ):
        lanes = slice(part * mine, part * mine + mine)
        taps[0:TAPS, lanes] = taps_ref[...]
        taps[TAPS : TAPS + 1, lanes] = shift_ref[0:1, :]
        bias[0:TAPS, lanes] = taps_ref[...] * shift_ref[0:1, :]
        bias[TAPS : TAPS + 1, lanes] = shift_ref[0:1, :] + shift_ref[1:2, :]
        fc2_t[:, lanes] = fc2_ref[...].T
        base_ref[:, lanes] = fc1_ref[...]
        base = fc1_ref[...].astype(F32)
        for k in range(TAPS):
            factor = taps_ref[k : k + 1, :] + (1.0 if k == 4 else 0.0)
            weights[k * 128 : k * 128 + 128, lanes] = (base * (factor * ROOT)).astype(BF16)
    scaled = bias[...] * ROOT
    high = scaled.astype(BF16)
    weights[TAPS * 128 : TAPS * 128 + 16, :] = high
    weights[TAPS * 128 + 16 : TAPS * 128 + 32, :] = (scaled - high.astype(F32)).astype(BF16)
    weights[TAPS * 128 + 32 : WIDE, :] = jnp.zeros((96, width), BF16)

    met(1)
    swap.start()

    def move_rows(pair, carry):
        both = xm_ext[pl.ds(pl.multiple_of(pair * halo, 16), halo), :].astype(F32)
        for i in range(2):
            row = both[W * i : W * i + W]
            moved[0, 2 * pair + i] = shift_right(row)
            moved[1, 2 * pair + i] = row
            moved[2, 2 * pair + i] = shift_left(row)
        return carry

    lax.fori_loop(1, rows // 2 + 1, move_rows, 0, unroll=2)
    swap.wait()
    xm_ext[pl.ds(halo_at, halo), :] = halo_ref[...]
    move_rows(0, 0)
    move_rows(rows // 2 + 1, 0)

    masks = mask_lanes()

    def gather_row(row, block):
        up, down = neighbour(row)
        if block == TAPS:
            return masks[0] * up + masks[1] + masks[2] * down
        a, b = divmod(block, 3)
        values = moved[b, row + a - 1]
        return values if a == 1 else values * (up if a == 0 else down)

    inner = masks[0] + masks[1] + masks[2]

    def gather_band(band, carry):
        row = 2 + 4 * band
        up, _ = neighbour(row)
        _, down = neighbour(row + 3)
        for block in range(TAPS + 1):
            if block == TAPS:
                first = masks[0] * up + masks[1] + masks[2]
                last = masks[0] + masks[1] + masks[2] * down
                parts = [first, inner, inner, last]
            else:
                a, b = divmod(block, 3)
                parts = [moved[b, row + i + a - 1] for i in range(4)]
                if a == 0:
                    parts[0] = parts[0] * up
                elif a == 2:
                    parts[3] = parts[3] * down
            both = jnp.concatenate(parts, axis=0).astype(BF16)
            wide[pl.ds(pl.multiple_of(band * BAND, 16), BAND), block * 128 : block * 128 + 128] = both
        return carry

    lax.fori_loop(0, bands, gather_band, 0)
    for block in range(TAPS + 1):
        lanes = slice(block * 128, block * 128 + 128)
        tail = jnp.concatenate([gather_row(halo_row, block), jnp.zeros((extra - W, 128), F32)], axis=0)
        wide[tokens : tokens + extra, lanes] = tail.astype(BF16)

    def fc2_part(n):
        ref, at = (fc2, n * SPAN) if n * SPAN < mine else (fc2_o, n * SPAN - mine)
        return ref[at : at + SPAN, :]

    def one_block(at, own):
        total = None
        coming = dot(wide[at, :], weights[:, 0:SPAN])
        for n in range(width // SPAN):
            lanes = slice(n * SPAN, n * SPAN + SPAN)
            spread = coming
            if (n + 1) * SPAN < width:
                coming = dot(wide[at, :], weights[:, (n + 1) * SPAN : (n + 2) * SPAN])
            grad = dot(dy[at, :], fc2_t[:, lanes])
            bell = jnp.exp2(spread * spread * -LOG2E)
            share = 1.0 + lax.erf(spread)
            du[at, lanes] = (grad * (share + spread * bell * 1.1283791670955126)).astype(BF16)
            if own:
                active = (spread * share).astype(BF16)
                act[at, lanes] = active
                part = dot(active, fc2_part(n))
                total = part if total is None else total + part
        return total

    size = 896

    def own_block(block, carry):
        at = pl.ds(pl.multiple_of(block * size, 128), size)
        for part in range(TAPS + 1):
            kept = min(128, KEPT - part * 128)
            turned = wide[at, part * 128 : part * 128 + 128].T
            wide_t[part * 128 : part * 128 + kept, at] = turned[0:kept]
        dy_t[:, at] = dy[at, :].T
        out_acc[at, :] = one_block(at, True) * ROOT
        return carry

    lax.fori_loop(0, tokens // size, own_block, 0)
    one_block(slice(tokens, tokens + extra), False)

    def fold(half):
        lanes = pl.ds(pl.multiple_of(half * SPAN, SPAN), SPAN)
        base = base_ref[:, lanes].astype(F32)
        grad = sums[4 * 128 : 5 * 128, :]
        marks = sums[TAPS * 128 : KEPT, :]
        mean = marks[TAPS : TAPS + 1]
        bias_g = mean
        rows_g = []
        factors = taps[:, lanes]
        for k in range(TAPS):
            part = sums[k * 128 : k * 128 + 128, :]
            mark = marks[k : k + 1]
            factor = factors[k : k + 1]
            grad = grad + part * factor
            bias_g = bias_g + mark * factor
            rows_g.append(jnp.sum(part * base, axis=0, keepdims=True) + mark * factors[TAPS : TAPS + 1])
        rows_g = jnp.concatenate(rows_g + [bias_g, mean, jnp.zeros((5, SPAN), F32)], axis=0)
        for i in range(SPAN // 128):
            core, row = divmod(i, STEP // 128)
            piece = slice(i * 128, i * 128 + 128)
            split_g[half, core, row * 128 : row * 128 + 128, :] = grad[:, piece] * 0.5
            split_g[half, core, 512 + 16 * row : 528 + 16 * row, :] = rows_g[:, piece] * 0.5

    def gradients(half, carry):
        lanes = pl.ds(pl.multiple_of(half * SPAN, SPAN), SPAN)
        for part in (slice(0, 592), slice(592, KEPT)):
            sums[part, :] = dot(wide_t[part, :], du[0:tokens, lanes])
        turned = dot(dy_t[...], act[:, lanes]).T * ROOT
        for core in range(2):
            split_g[half, core, 256:512, :] = turned[core * STEP : core * STEP + STEP]
        for k in range(TAPS):
            weights_t[lanes, k * 128 : k * 128 + 128] = weights[k * 128 : k * 128 + 128, lanes].T
        fold(half)
        return carry

    lax.fori_loop(0, width // SPAN, gradients, 0)

    groups = ((4, 1, 7, 0), (3, 6, 2, 5), (8,))

    def collect_row(group, base, row):
        total = [None] * 3
        for i, k in enumerate(group):
            a, b = divmod(k, 3)
            source = row + 3 - a
            part = moved[base + i, source]
            if a != 1:
                up, down = neighbour(source)
                part = part * (up if a == 0 else down)
            total[b] = part if total[b] is None else total[b] + part
        if total[0] is not None:
            total[0] = shift_left(total[0])
        if total[2] is not None:
            total[2] = shift_right(total[2])
        total = functools.reduce(jnp.add, [part for part in total if part is not None])
        at = pl.ds(pl.multiple_of(row * W, 8), W)
        if group[0] == 4:
            dxm[at, :] = total
        else:
            dxm[at, :] += total

    for number, group in enumerate(groups):
        base = 4 * (number & 1)
        for i in range(len(group)):
            moved[base + i, 1] = jnp.zeros((W, 128), F32)
            moved[base + i, rows + 2] = jnp.zeros((W, 128), F32)

        def back(at):
            parts = [weights_t[:, k * 128 : k * 128 + 128] for k in group]
            return dot(du[at, :], jnp.concatenate(parts, axis=1))

        tail = back(slice(tokens, tokens + extra))
        for i in range(len(group)):
            moved[base + i, halo_row] = tail[0:W, i * 128 : i * 128 + 128]

        def back_block(block, carry):
            result = back(pl.ds(pl.multiple_of(block * 4 * BAND, 16), 4 * BAND))
            for i in range(len(group)):
                moved[base + i, pl.ds(2 + 16 * block, 16)] = result[
                    :, i * 128 : i * 128 + 128
                ].reshape(16, W, 128)
            if number:
                for i in range(16):
                    collect_row(groups[number - 1], 4 - base, 16 * block + i)
            return carry

        lax.fori_loop(0, bands // 4, back_block, 0)

    def last_rows(row, carry):
        collect_row(groups[-1], 4 * ((len(groups) - 1) & 1), row)
        return carry

    lax.fori_loop(0, rows, last_rows, 0, unroll=4)

    mid_g[...] = jnp.zeros(mid_g.shape, F32)
    for load in loads:
        load.wait()
    place = to_slots()
    proj = proj_w[...].astype(F32)
    proj_sw = jnp.concatenate([proj[64:], proj[:64]], axis=0).T.astype(BF16)

    def fold_up(values):
        return jnp.sum(jnp.sum(values.reshape(-1, 64, 128), axis=0).reshape(8, 8, 128), axis=0)

    def two_bands(block, carry):
        at = pl.ds(pl.multiple_of(block * 2 * BAND, 16), 2 * BAND)
        middle = x1[at, :]
        result = middle + out_acc[at, :] + shifts[3:4, :]
        hat, inverse = norm_hat(middle)
        grad = dxm[at, :] * ROOT
        grad_y = dy[at, :].astype(F32)
        dx1 = grad_y + norm_back(grad * gains[1:2, :], hat, inverse)
        dx1_out[at, :] = dx1
        dz = dx1.astype(BF16)
        mid_g[8:136, :] += dot_in(heads_out[at, :], dz)
        do = dot(dz, proj_sw)
        for i in range(2):
            band = 2 * block + i
            live = live_band(side * bands + band)
            part = slice(i * BAND, (i + 1) * BAND)
            here = pl.ds(pl.multiple_of(band * BAND, 16), BAND)
            out[here, :] = (result[part] * live).astype(BF16)
            do_out[band] = dot(place, (do[part] * live).astype(BF16)).astype(BF16)
        terms = (grad * hat, grad, dz.astype(F32), grad_y)
        return tuple(total + fold_up(term) for total, term in zip(carry, terms))

    zero = jnp.zeros((8, 128), F32)
    totals = lax.fori_loop(0, bands // 2, two_bands, (zero,) * 4)
    for i in range(4):
        mid_g[i : i + 1, :] = jnp.sum(totals[i], axis=0, keepdims=True)


def stages(levels, shared):
    rest = list(range(2, levels))
    pairs = [rest[i : i + 2] for i in range(0, len(rest), 2)]
    return [[0], ["x", 1]] + pairs if shared else [[0], [1]] + pairs + [["x"]]


def group_size(levels, rows):
    unit = 16 * 2 ** (levels - 1)
    return -(-rows // unit) * unit


def stage_shapes(levels, shared, rows):
    halves, shapes = 2, [(1, 2, rows, 128)]
    for dims in stages(levels, shared)[1:]:
        if "x" in dims:
            halves = 1
        rows >>= sum(1 for dim in dims if dim != "x")
        shapes.append((2 ** len(dims) - 1, halves, rows, 128))
    return shapes


def group_scratch(levels, shared, rows):
    buffers = [pltpu.VMEM(part, BF16) for part in stage_shapes(levels, shared, rows)]
    return [pltpu.VMEM((2, rows, 128), F32)] + buffers + buffers


def group_links(levels, shared):
    return sum(2 ** len(dims) - 1 for dims in stages(levels, shared))


def everyone(levels):
    batch, side = lax.axis_index("batch"), lax.axis_index("heads")
    peers = []
    for dims in stages(levels, True):
        for flips in range(1, 2 ** len(dims)):
            peers.append(flipped(batch, side, dims, flips))
    return peers


def flipped(batch, side, dims, flips):
    for i, dim in enumerate(dims):
        if flips >> i & 1:
            if dim == "x":
                side = 1 - side
            else:
                batch = batch + (1 - 2 * ((batch // 2**dim) % 2)) * 2**dim
    return batch, side


class Group:
    def __init__(self, levels, shared, buffers, sems, base):
        self.stages = stages(levels, shared)
        count = len(self.stages)
        self.cur, self.sends, self.recvs = buffers[0], buffers[1 : 1 + count], buffers[1 + count :]
        self.sems, self.base = sems, base
        self.batch, self.side = lax.axis_index("batch"), lax.axis_index("heads")
        self.core = self.batch % 2
        at, rows = 0, self.cur.shape[1]
        self.kept, self.given = [(at, rows)], [None]
        for dims in self.stages[1:]:
            bits = [dim for dim in dims if dim != "x"]
            starts = []
            for flips in range(2 ** len(dims)):
                batch, _ = flipped(self.batch, self.side, dims, flips)
                start = at
                for i, bit in enumerate(bits):
                    start = start + ((batch // 2**bit) % 2) * (rows >> (i + 1))
                starts.append(pl.multiple_of(start, 16))
            rows >>= len(bits)
            at = starts[0]
            self.kept.append((at, rows))
            self.given.append(starts)
        self.left = list(range(count))

    def link(self, stage, flips):
        number = self.base + sum(2 ** len(part) - 1 for part in self.stages[:stage]) + flips - 1
        peer = flipped(self.batch, self.side, self.stages[stage], flips)
        source, target = self.sends[stage].at[flips - 1], self.recvs[stage].at[flips - 1]
        return link(source, target, self.sems[0].at[number], self.sems[1].at[number], peer)

    def wait(self, stage):
        for flips in range(1, 2 ** len(self.stages[stage])):
            self.link(stage, flips).wait()

    def add(self, stage):
        at, rows = self.kept[stage]
        here, recv = pl.ds(at, rows), self.recvs[stage]
        if recv.shape[1] == 2:
            total = self.cur[:, here, :]
            for i in range(recv.shape[0]):
                total = total + recv[i].astype(F32)
            self.cur[:, here, :] = total
            return
        total = self.cur[self.side, here, :]
        for i in range(recv.shape[0]):
            total = total + recv[i, 0].astype(F32)
        self.cur[self.side, here, :] = total

    def advance(self, count=1, pieces=None):
        for number in self.left[:count]:
            self.phase(number, pieces)
        del self.left[:count]

    def phase(self, number, pieces):
        count = len(self.stages)
        if number == 0:
            for half in range(2):
                for row, value in pieces(half, 1 - self.core):
                    self.sends[0][0, half, row : row + value.shape[0], :] = value.astype(BF16)
            self.link(0, 1).start()
            for half in range(2):
                for row, value in pieces(half, self.core):
                    self.cur[half, row : row + value.shape[0], :] = value
        else:
            self.wait(number - 1)
            self.add(number - 1)
            dims = self.stages[number]
            _, rows = self.kept[number]
            for flips in range(1, 2 ** len(dims)):
                crossing = "x" in dims and flips >> dims.index("x") & 1
                here = pl.ds(self.given[number][flips], rows)
                if self.sends[number].shape[1] == 2:
                    self.sends[number][flips - 1] = self.cur[:, here, :].astype(BF16)
                else:
                    half = 1 - self.side if crossing else self.side
                    self.sends[number][flips - 1, 0] = self.cur[half, here, :].astype(BF16)
                self.link(number, flips).start()

    def finish(self):
        self.wait(len(self.stages) - 1)
        self.add(len(self.stages) - 1)
        at, rows = self.kept[-1]
        return self.cur[self.side, pl.ds(at, rows), :].astype(BF16)


class Gather:
    def __init__(self, levels, out, shared, sems, base):
        self.stages, self.out, self.shared = stages(levels, True), out, shared
        self.sems, self.base = sems, base
        self.batch, self.side = lax.axis_index("batch"), lax.axis_index("heads")
        self.core = self.batch % 2
        at, count = 0, out.shape[2]
        self.kept = [(at, count)]
        for dims in self.stages[1:]:
            for bit in dims:
                if bit != "x":
                    count //= 2
                    at = at + ((self.batch // 2**bit) % 2) * count
            self.kept.append((at, count))
        self.left = list(range(len(self.stages)))

    def links(self, stage):
        dims = self.stages[stage]
        at, count = self.kept[stage]
        number = self.base + sum(2 ** len(part) for part in self.stages[:stage])
        mine = self.out.at[self.core, self.side, pl.ds(at, count)]
        for flips in range(1, 2 ** len(dims)):
            part = mine
            if "x" in dims and flips >> dims.index("x") & 1:
                if not self.shared:
                    continue
                part = self.out.at[self.core, self.side, pl.ds(at, count), pl.ds(0, self.shared)]
            yield self.made(part, number, flipped(self.batch, self.side, dims, flips))
            number += 1
        if stage == 0 and self.shared:
            part = self.out.at[self.core, 1 - self.side, :, pl.ds(0, self.shared)]
            yield self.made(part, number, flipped(self.batch, self.side, dims, 1))

    def made(self, part, number, peer):
        return link(part, part, self.sems[0].at[number], self.sems[1].at[number], peer)

    def begin(self, pieces):
        at, _ = self.kept[-1]
        row = 0
        for piece in pieces:
            self.out[self.core, self.side, at, row : row + piece.shape[0], :] = piece
            row += piece.shape[0]
        for made in self.links(len(self.stages) - 1):
            made.start()

    def advance(self):
        stage = len(self.left) - 1
        for made in self.links(stage):
            made.wait()
        if stage:
            for made in self.links(stage - 1):
                made.start()
        del self.left[-1]


def attend_back_kernel(
    table, key_c, key_f, val_c, val_f, xn, query_t, query_o, do_ref, ot_ref, lse, output,
    dq_out, own_out, send_out, output_out,
    acc_c, acc_f, query_ref, turned_c, turned_f, keys_ref, vals_ref, kept,
):
    step = pl.program_id(0)
    each = xn.shape[0]
    bands = each * pl.num_programs(0)
    side = lax.axis_index("heads")

    @pl.when(step == 0)
    def _():
        acc_c[...] = jnp.zeros(acc_c.shape, F32)
        acc_f[...] = jnp.zeros(acc_f.shape, F32)
        query_ref[...] = full_query(query_t, query_o, side).T.astype(BF16)

    output_out[...] = output[...]
    firsts = [table[1, side * bands + each * step + i] for i in range(each)]
    for i in range(each):

        @pl.when((step == 0) | (kept[i] != firsts[i]))
        def _():
            kept[i] = firsts[i]
            keys = window(key_f, firsts[i])
            keys_ref[i] = keys
            vals_ref[i] = window(val_f, firsts[i])
            for part, (start, count) in enumerate(HALVES):
                rows = slice(start * PACKED, (start + count) * PACKED)
                turned_f[i, part, :, 0 : count * PACKED] = keys[rows].T[64:128]
            turned_c[i] = window(key_c, firsts[i]).T[0:64]

    queries, query_rows, grads_t, grads_low = [], [], [], []
    for i in range(each):
        query = dot(xn[i], query_ref[...]).astype(BF16)
        queries.append(query)
        query_rows.append(query.astype(F32).T.astype(BF16))
        grads_t.append(do_ref[i].astype(F32).T)
        grads_low.append(grads_t[i].astype(BF16))
    dq = [[None] * 4 for _ in range(each)]

    def products(unit):
        i, head, part = unit
        fine = head >= 2
        image = table[0, side * bands + each * step + i]
        start, count = HALVES[part]
        if fine:
            rows = slice(start * PACKED, (start + count) * PACKED)
            keys, vals = keys_ref[i, rows], vals_ref[i, rows]
        else:
            keys, vals = window(key_c, firsts[i]), window(val_c, firsts[i])
        swapped = (head + 2) & 3
        delta = jnp.sum(
            ot_ref[i, 32 * head : 32 * head + 32]
            * grads_t[i][32 * swapped : 32 * swapped + 32],
            axis=0,
            keepdims=True,
        )
        offset = lse[i, head : head + 1, :] * (-1.0 / EXP_SCALE)
        left = score_rows(query_rows[i], head, image, fine)
        left = with_offset(left, ONES + (0 if fine else 64), offset)
        right = with_offset(head_rows(grads_low[i], swapped), 64 if fine else 0, -delta)
        return dot(keys, left), dot(vals, right)

    held = {}

    def back(unit, score, prob_grad):
        i, head, part = unit
        fine = head >= 2
        swapped = (head + 2) & 3
        prob = jnp.exp2(score * EXP_SCALE)
        score_grad = (prob * prob_grad).astype(BF16)
        row = 32 * (head & 1)
        start, count = HALVES[part]
        turned = turned_c[i, row : row + 32]
        if fine:
            turned = turned_f[i, part, row : row + 32, 0 : count * PACKED]
        grad = dot(turned, score_grad)
        dq[i][head] = grad if part == 0 else dq[i][head] + grad
        pair = held.setdefault((i, fine, part), ([], []))
        pair[0].extend([score_grad, prob.astype(BF16)])
        pair[1].extend([head_lanes(queries[i], head), head_lanes(do_ref[i], swapped)])
        if head & 1:
            both = dot(jnp.concatenate(pair[0], axis=1), jnp.concatenate(pair[1], axis=0))
            if fine:
                at = pl.ds(firsts[i] + start, count)
                acc_f[at, 0:PACKED, :] += both.reshape(count, PACKED, 128)
            else:
                acc_c[pl.ds(firsts[i], MAX_BANDS)] += both.reshape(MAX_BANDS, COARSE, 128)

    waiting = []
    for i in range(each):
        for head, parts in ((2, 2), (3, 2), (0, 1), (1, 1)):
            for part in range(parts):
                waiting.append(((i, head, part), *products((i, head, part))))
                if len(waiting) > 3:
                    back(*waiting.pop(0))
    for unit in waiting:
        back(*unit)
    for i in range(each):
        dq_out[i] = (jnp.concatenate(dq[i], axis=0).T * SCALE).astype(BF16)

    @pl.when(step == pl.num_programs(0) - 1)
    def _():
        span = bands + 1
        lane = lax.broadcasted_iota(jnp.int32, (1, 128), 1)
        scale_c = jnp.where(lane < 64, SCALE, 1.0)
        scale_f = jnp.where(lane < 64, 1.0, SCALE)
        for dest, at, kind in (
            (own_out, side * (bands - 1), F32),
            (send_out, (1 - side) * (bands - 1), BF16),
        ):
            dest[:, 0:COARSE, :] = (acc_c[pl.ds(at, span)] * scale_c).astype(kind)
            for cell in range(4):
                part = acc_f[pl.ds(at, span), 14 * cell : 14 * cell + 16, :] * scale_f
                part = jnp.where(cell_valid(part.shape, 1), part, 0.0)
                row = COARSE + 16 * cell
                dest[:, row : row + 16, :] = part.astype(kind)


def tail_kernel(
    levels, own_in, given, split_in, mid_g, slab_in, other, meta, xn_in, hat_in, dq_in, query_t,
    query_o, dx1_in, inv_in, gains,
    red_c_in, conv_c_in, gain_c, shifts_c, kv_c, taps_c_ref,
    red_f_in, conv_f_in, gain_f, shifts_f, kv_f, taps_f_ref,
    tok_grad, early, joint, little,
    pack, small, small_in, small_sems, recv, grad_ref, val_ref, dxn, send_sem, recv_sem, send_sems, recv_sems, turned_c, turned_f,
    dx1, inv, hat_ref, own, split_g, slab, xn, dq, red_c, conv_c, red_f, conv_f, xt, load_sems,
    *buffers,
):
    bands = xn.shape[0]
    side = lax.axis_index("heads")
    greet(*everyone(levels))
    early_pairs = (
        (split_in, split_g), (dq_in, dq), (xn_in, xn), (own_in, own), (slab_in, slab),
        (conv_c_in, conv_c), (conv_f_in, conv_f),
    )
    loads = fetch(early_pairs, load_sems)
    met(len(everyone(levels)))
    swaps = [
        remote(given.at[:, here], recv.at[:, here], send_sem.at[i], recv_sem.at[i], across())
        for i, here in enumerate((pl.ds(0, COARSE), pl.ds(COARSE, FINE)))
    ]
    late_pairs = (
        (red_c_in, red_c), (red_f_in, red_f), (hat_in, hat_ref), (inv_in, inv), (dx1_in, dx1),
    )
    loads += fetch(late_pairs, load_sems.at[pl.ds(len(early_pairs), len(late_pairs))])
    sems = (send_sems, recv_sems)
    split_count, shared_count = (1 + 2 * len(stages(levels, shared)) for shared in (False, True))
    before = Group(levels, False, buffers[:split_count], sems, 0)
    base = group_links(levels, False)
    buffers = buffers[split_count:]
    conv = Group(levels, True, buffers[:shared_count], sems, base)
    base += group_links(levels, True)
    rest = Group(levels, True, buffers[shared_count:], sems, base)
    base += group_links(levels, True)
    early_rows, late_rows, later_rows = (group.cur.shape[1] for group in (before, conv, rest))
    gather = Gather(levels, joint, joint.shape[3], sems, base)
    base += group_links(levels, True) + len(stages(levels, True))
    gather_split = Gather(levels, early, 0, sems, base)

    def split_pieces(half, which):
        yield 0, split_g[(half + side) % 2, which]
        if early_rows > SPLIT:
            yield SPLIT, jnp.zeros((early_rows - SPLIT, 128), F32)

    def shared_pieces(first, used, rows):
        def pieces(half, which):
            at = pl.multiple_of(first + used * (2 * half + which), 16)
            yield 0, pack[pl.ds(at, used), :]
            if rows > used:
                yield used, jnp.zeros((rows - used, 128), F32)

        return pieces

    batch, order = lax.axis_index("batch"), stages(levels, True)

    def small_links(stage):
        before = sum(2 ** len(dims) - 1 for dims in order[:stage])
        for flips in range(1, 2 ** len(order[stage])):
            at = before + flips - 1
            yield at, link(
                small.at[stage], small_in.at[at], small_sems.at[0, at], small_sems.at[1, at],
                flipped(batch, side, order[stage], flips),
            )

    def small_phase(stage):
        if stage:
            total = small[stage - 1]
            for at, made in small_links(stage - 1):
                made.wait()
                total = total + small_in[at]
            if stage == len(order):
                little[...] = total
                return
            small[stage] = total
        for _, made in small_links(stage):
            made.start()

    for load in loads[:7]:
        load.wait()
    before.advance(1, split_pieces)

    start = 0
    parts = []
    for count in (conv_c.shape[0], conv_f.shape[0], 128, 128, 128, 128):
        parts.append(pack.at[start : start + count])
        start += count
    conv_c_g, conv_f_g, kv_c_g, kv_f_g, query_g, proj_g = parts
    small_c, small_f, front_g = small.at[0, 0:16], small.at[0, 16:32], small.at[0, 32:40]
    small[0, 40:48, :] = mid_g[0:8, :]
    proj_g[...] = mid_g[8:136, :]
    taps_c, taps_f = pad_taps(taps_c_ref[...], True), pad_taps(taps_f_ref[...], False)
    kv_f_sw = swap_lanes(kv_f[...])

    val_ref[0] = jnp.zeros((CELLS, 128), F32)
    val_ref[bands + 1] = jnp.zeros((CELLS, 128), F32)
    val_ref[1 : bands + 1] = slab[...]
    val_ref[pl.ds((1 - side) * (bands + 1), 1)] = other[
        pl.ds(side * (bands - 1), 1)
    ].astype(F32)
    at = pl.ds(side * bands, bands)
    above, below = meta[0, at], meta[1, at]
    grid = xn[...].reshape(bands, 16, 16, 128)
    slot_grads = dq[...].reshape(bands, 16, 16, 128)
    total = None
    for i in range(16):
        turned = grid[:, i].reshape(bands * 16, 128).T
        xt[i] = turned
        part = dot(turned, slot_grads[:, i].reshape(bands * 16, 128))
        total = part if total is None else total + part
    query_g[...] = total
    full = full_query(query_t, query_o, side).astype(BF16)
    dxn[...] = dot(dq[...].reshape(-1, 128), full).reshape(bands, SLOTS, 128)
    grad_ref[0] = jnp.zeros((CELLS, 128), F32)
    grad_ref[bands + 1] = jnp.zeros((CELLS, 128), F32)
    turned_c[...] = conv_c[...].T
    turned_f[...] = conv_f[...].T
    before.advance()
    swaps[0].wait()
    here = pl.ds(1 - side, bands + 1)
    for load in loads[7:]:
        load.wait()
    grad_ref[here, 0:COARSE] = own[:, 0:COARSE] + recv[:, 0:COARSE].astype(F32)
    lane = lax.broadcasted_iota(jnp.int32, (1, 1, 128), 2)

    def tap_sum(values, grads):
        return fold_rows(values * grads)

    def reduce_back(pair, red, conv, gain, shifts, kv, small, kv_g):
        hat, inverse = norm_hat(red[...])
        normed = hat * gain[...] + shifts[1:2, :]
        cdf, bell = gauss(normed)
        active = (normed * cdf).astype(BF16)
        kv_g[...] = dot_in(active, pair)
        small[9:10, :] = jnp.sum(pair.astype(F32), axis=0, keepdims=True)
        grad = dot_t(pair, kv) * gelu_slope(normed, cdf, bell)
        small[11:12, :] = jnp.sum(grad * hat, axis=0, keepdims=True)
        small[12:13, :] = jnp.sum(grad, axis=0, keepdims=True)
        dc = norm_back(grad * gain[...], hat, inverse).astype(BF16)
        small[13:14, :] = jnp.sum(dc.astype(F32), axis=0, keepdims=True)
        return dc

    small_c[...] = jnp.zeros(small_c.shape, F32)
    small_f[...] = jnp.zeros(small_f.shape, F32)

    vals = val_ref[:, 0:COARSE, :]
    ext = grad_ref[:, 0:COARSE, :]
    ext = jnp.where(lane < 64, ext, ext.astype(BF16).astype(F32))
    mid = ext[1:-1]
    near = (by_band(vals[:-2], above), vals[1:-1], by_band(vals[2:], below))
    for a in range(3):
        for b in range(3):
            moved = near[a] if b == 1 else roll_cells(near[a], 1 - b)
            small_c[3 * a + b : 3 * a + b + 1, :] = jnp.sum(
                tap_sum(moved, mid), axis=0, keepdims=True
            )
    small_c[10:11, :] = jnp.sum(mid.reshape(-1, 128), axis=0, keepdims=True)
    pair = mid + depthwise_coarse(ext, above, below, taps_c, flip=True)
    pair = jnp.where(cell_valid(pair.shape, 1), pair, 0.0)
    pair = pair.reshape(bands * COARSE, 128).astype(BF16)
    dc = reduce_back(pair, red_c, conv_c, gain_c, shifts_c, kv_c[...], small_c, kv_c_g)
    for i in range(16):
        part = slice(i * 128, (i + 1) * 128)
        conv_c_g[part, :] = dot(xt[i], dc)
        back = dot(dc, turned_c[:, part]).reshape(bands, 16, 128)
        dxn[:, 16 * i : 16 * i + 16, :] += back

    conv.advance(1, shared_pieces(0, CONV, late_rows))
    before.advance()
    swaps[1].wait()
    grad_ref[here, COARSE:CELLS] = own[:, COARSE:CELLS] + recv[:, COARSE:CELLS].astype(F32)
    vals = val_ref[:, COARSE:CELLS, :]
    ext = grad_ref[:, COARSE:CELLS, :]
    ext = jnp.where(lane >= 64, ext, ext.astype(BF16).astype(F32))
    rows = depthwise_fine(ext, above, below, taps_f, flip=True)
    near = fine_rows(vals, above, below)
    mids = fine_rows(ext, above, below)[1]
    for a in range(3):
        for b in range(3):
            total = jnp.zeros((8, 128), F32)
            for row in range(2):
                even, odd = near[a][row][:, 0], near[a][row][:, 1]
                grad_even, grad_odd = mids[row][:, 0], mids[row][:, 1]
                if b == 0:
                    moved = (roll_cells(odd, 1), even)
                elif b == 1:
                    moved = (even, odd)
                else:
                    moved = (odd, roll_cells(even, -1))
                total = total + tap_sum(moved[0], grad_even) + tap_sum(moved[1], grad_odd)
            small_f[3 * a + b : 3 * a + b + 1, :] = jnp.sum(total, axis=0, keepdims=True)
    small_f[10:11, :] = jnp.sum(ext[1:-1].reshape(-1, 128), axis=0, keepdims=True)
    valid = cell_valid((bands, 16, 128), 1)
    blocks = []
    for row in range(2):
        for column in range(2):
            block = jnp.where(valid, mids[row][:, column] + rows[row][column], 0.0)
            blocks.append(block.astype(BF16).reshape(bands, 1, 16, 128))
    pair = jnp.concatenate(blocks, axis=1).reshape(bands * FINE, 128)
    conv.advance()
    dc = reduce_back(pair, red_f, conv_f, gain_f, shifts_f, kv_f_sw, small_f, kv_f_g)
    for i in range(4):
        part = slice(i * 128, (i + 1) * 128)
        total = None
        for row in range(2):
            for column in range(2):
                cells = dc.reshape(bands, 4, 16, 128)[:, 2 * row + column].reshape(bands * 16, 128)
                product = dot(xt[fine_slot(i, row, column)], cells)
                total = product if total is None else total + product
        conv_f_g[part, :] = total
        back = dot(dc, turned_f[:, part]).reshape(bands, 4, 16, 128)
        for row in range(2):
            for column in range(2):
                slot = 16 * fine_slot(i, row, column)
                dxn[:, slot : slot + 16, :] += back[:, 2 * row + column]

    front_g[...] = jnp.zeros(front_g.shape, F32)
    sums = jnp.zeros((8, 128), F32)
    along = jnp.zeros((8, 128), F32)
    for band in range(bands):
        grad = dxn[band]
        sums = sums + fold_rows(grad)
        along = along + fold_rows(grad * hat_ref[band].astype(F32))
    front_g[0:1, :] = jnp.sum(along, axis=0, keepdims=True)
    front_g[1:2, :] = jnp.sum(sums, axis=0, keepdims=True)

    small_phase(0)
    rest.advance(1, shared_pieces(4 * CONV, REST, later_rows))
    conv.advance()
    before.advance()
    place = from_slots()

    def one_band(band):
        at = slice(band * BAND, (band + 1) * BAND)
        back = norm_back(dxn[band] * gains[0:1, :], hat_ref[band].astype(F32), 1.0)
        tok_grad[at, :] = dx1[at, :] + dot(place, back.astype(BF16)) * inv[at, :]

    began = len(before.left) + 1
    done = 0
    total = max(len(rest.left) + 1 + len(gather.left), began + len(gather_split.left))
    for number in range(1, total + 1):
        while done < bands and done * total < number * bands:
            one_band(done)
            done += 1
        if rest.left:
            rest.advance()
            conv.advance()
        elif number + len(gather.left) == total:
            conv.advance(len(conv.left))
            gather.begin([conv.finish(), rest.finish()])
        else:
            gather.advance()
        if before.left:
            before.advance()
        elif number == began:
            gather_split.begin([before.finish()])
        elif gather_split.left:
            gather_split.advance()
        if number <= len(order):
            small_phase(number)


def shared_rows(start, count):
    done = 0
    while done < count:
        group = 0 if start + done < 4 * CONV else 1
        if group == 0:
            quarter, row = divmod(start + done, CONV)
            size = min(count - done, CONV - row)
        else:
            quarter, row = divmod(start + done - 4 * CONV, REST)
            size = min(count - done, REST - row)
        yield group, quarter % 2, quarter // 2, row, done, size
        done += size


def unpack_kernel(
    levels,     early, joint, little, tok_grad,
    tok_grad_out, gains, shifts, query, conv_c, gain_c, shifts_c, kv_c, taps_c, conv_f, gain_f, shifts_f, kv_f,
    taps_f, proj, hidden, fc1, depth, fc2,
):
    tok_grad_out[...] = tok_grad[...]

    @pl.when(pl.program_id(0) == 0)
    def _():
        unpack_grads(
            levels, early, joint, little, gains, shifts, query, conv_c, gain_c, shifts_c, kv_c,
            taps_c, conv_f, gain_f, shifts_f, kv_f, taps_f, proj, hidden, fc1, depth, fc2,
        )


def unpack_grads(
    levels, early, joint, little,
    gains, shifts, query, conv_c, gain_c, shifts_c, kv_c, taps_c, conv_f, gain_f, shifts_f, kv_f,
    taps_f, proj, hidden, fc1, depth, fc2,
):
    side = lax.axis_index("heads")
    half = query.shape[0]
    first = group_size(levels, CONV) // joint.shape[2]
    spans = (slice(0, first), slice(first, joint.shape[3]))

    def quarter_rows(group, core, h):
        ref, rows = (early, slice(None)) if group == 2 else (joint, spans[group])
        return ref[core, h, :, rows, :].reshape(-1, 128)


    def rows_of(start, count):
        pieces = [
            quarter_rows(group, core, h)[at : at + size].astype(F32)
            for group, core, h, at, _, size in shared_rows(start, count)
        ]
        return pieces[0] if len(pieces) == 1 else jnp.concatenate(pieces, axis=0)

    start = 0
    for ref in (conv_c, conv_f, kv_c):
        count = ref.shape[0]
        for group, core, h, at, offset, size in shared_rows(start, count):
            ref[offset : offset + size, :] = quarter_rows(group, core, h)[at : at + size].astype(F32)
        start += count
    kv_f[...] = swap_lanes(rows_of(start, 128))
    both = rows_of(start + 128, 128)
    query[...] = jnp.where(side == 0, both[:, :half], both[:, half:]).T
    proj[...] = rows_of(start + 256, 128)
    small = little[...]
    coarse, fine, front, mid = small[0:16], small[16:32], small[32:40], small[40:48]
    taps_c[...] = coarse[0:9, half:]
    taps_f[...] = fine[0:9, :half]
    gain_c[...] = coarse[11:12]
    gain_f[...] = fine[11:12]
    shifts_c[0:1, :] = coarse[13:14]
    shifts_c[1:2, :] = coarse[12:13]
    shifts_c[2:3, :] = jnp.concatenate([coarse[9:10, half:], coarse[10:11, half:]], axis=1)
    shifts_f[0:1, :] = fine[13:14]
    shifts_f[1:2, :] = fine[12:13]
    shifts_f[2:3, :] = jnp.concatenate([fine[9:10, :half], fine[10:11, :half]], axis=1)
    gains[0:1, :] = front[0:1]
    gains[1:2, :] = mid[0:1]
    shifts[0:1, :] = front[1:2]
    shifts[1:2, :] = mid[2:3]
    shifts[2:3, :] = mid[1:2]
    shifts[3:4, :] = mid[3:4]
    for core in range(2):
        split = quarter_rows(2, core, side)
        for i in range(2):
            lanes = slice(core * STEP + i * 128, core * STEP + i * 128 + 128)
            fc1[:, lanes] = split[i * 128 : i * 128 + 128].astype(F32)
            block = split[512 + 16 * i : 528 + 16 * i].astype(F32)
            depth[:, lanes] = block[0:9]
            hidden[:, lanes] = block[9:11]
        fc2[core * STEP : core * STEP + STEP, :] = split[256:512].astype(F32)


SMEM = pl.BlockSpec(memory_space=pltpu.SMEM)
VMEM = pl.BlockSpec(memory_space=pltpu.VMEM)
HBM = pl.BlockSpec(memory_space=pl.ANY)


def shape(dims, kind=F32):
    return jax.ShapeDtypeStruct(dims, kind)


def params(limit=56):
    return pltpu.CompilerParams(vmem_limit_bytes=limit * MIB)


def sending(number, limit=56):
    return pltpu.CompilerParams(
        vmem_limit_bytes=limit * MIB, collective_id=number, has_side_effects=True
    )


def per_device(
    size, tokens, image_bands, cotangent, front_gains, front_shifts, query_w, coarse_conv,
    coarse_gain, coarse_shifts, coarse_kv, coarse_taps, fine_conv, fine_gain, fine_shifts, fine_kv,
    fine_taps, proj_w, hidden_shifts, fc1_w, depth_taps, fc2_w,
):
    count = tokens.shape[0]
    rows = count // W
    bands = count // BAND
    total = 2 * bands
    halo = 2 * W
    half = coarse_kv.shape[1] // 2
    mine = fc1_w.shape[1]
    hidden = 2 * mine
    gain_c, gain_f = coarse_gain[None], fine_gain[None]
    semaphores = pltpu.SemaphoreType.DMA
    levels = size.bit_length() - 1
    query_t = query_w.T

    (
        table, meta, xn, hat, inverse, red_c, red_f, slab, other, query_o,
    ) = pl.pallas_call(
        front_kernel,
        out_shape=(
            shape((3, 32), jnp.int32),
            shape((3, total, 8, 128)),
            shape((bands, SLOTS, 128), BF16),
            shape((bands, SLOTS, 128), BF16),
            shape((count, 128)),
            shape((bands * COARSE, 128)),
            shape((bands * FINE, 128)),
            shape((bands, CELLS, 128)),
            shape((bands, CELLS, 128), BF16),
            shape(query_t.shape, BF16),
        ),
        in_specs=[SMEM] + [VMEM] * 12,
        out_specs=[SMEM] + [VMEM] * 9,
        scratch_shapes=[pltpu.VMEM((bands, CELLS, 128), BF16), semaphores((8,)), semaphores((8,))],
        compiler_params=sending(1),
        name="front",
    )(
        image_bands, tokens, front_gains, front_shifts, coarse_conv, gain_c, coarse_shifts,
        coarse_kv, fine_conv, gain_f, fine_shifts, fine_kv,
        query_t,
    )

    each = 4 if bands % 4 == 0 else 2
    some_bands = pl.BlockSpec((each * BAND, 128), lambda i: (i, 0))
    some_slots = pl.BlockSpec((each, SLOTS, 128), lambda i: (i, 0, 0))
    two_slots = pl.BlockSpec((2, SLOTS, 128), lambda i: (i, 0, 0))
    (
        x1, xm, heads_out, out_t, lse, key_c, key_f, val_c, val_f, fc1_o, fc2_o, depth_o, hidden_o,
        cot_o,
    ) = pl.pallas_call(
        attend_kernel,
        grid=(bands // each,),
        out_shape=(
            shape((count, 128)),
            shape((count, 128), BF16),
            shape((count, 128), BF16),
            shape((bands, 128, SLOTS)),
            shape((bands, 8, SLOTS)),
            shape((total, COARSE, 128), BF16),
            shape((total, PACKED, 128)),
            shape((total, COARSE, 128), BF16),
            shape((total, PACKED, 128)),
            shape(fc1_w.shape, BF16),
            shape(fc2_w.shape, BF16),
            shape(depth_taps.shape),
            shape(hidden_shifts.shape),
            shape((halo, 128), BF16),
        ),
        in_specs=[SMEM] + [VMEM] * 7 + [some_slots, some_bands] + [VMEM] * 5 + [HBM] * 5,
        out_specs=[
            some_bands,
            some_bands,
            some_bands,
            pl.BlockSpec((each, 128, SLOTS), lambda i: (i, 0, 0)),
            pl.BlockSpec((each, 8, SLOTS), lambda i: (i, 0, 0)),
        ]
        + [VMEM] * 4
        + [HBM] * 5,
        scratch_shapes=[
            pltpu.VMEM((total + 2, CELLS, 128), F32),
            pltpu.VMEM((128, 128), BF16),
            pltpu.VMEM((BAND, SLOTS), BF16),
            semaphores((5,)),
            semaphores((5,)),
        ],
        compiler_params=sending(4),
        name="attend",
    )(
        table, slab, other, meta, coarse_taps, fine_taps, coarse_shifts, fine_shifts, xn, tokens,
        query_t, query_o, proj_w, front_gains, front_shifts, fc1_w, fc2_w, depth_taps,
        hidden_shifts, cotangent,
    )

    extra = 64
    output, dx1, out_grad, split_g, mid_g = pl.pallas_call(
        hidden_kernel,
        out_shape=(
            shape((count, 128), BF16),
            shape((count, 128)),
            shape((bands, SLOTS, 128), BF16),
            shape((2, 2, SPLIT, 128)),
            shape((136, 128)),
        ),
        in_specs=[SMEM, HBM] + [VMEM] * 3 + [HBM] + [VMEM] * 11,
        out_specs=[VMEM] * 5,
        scratch_shapes=[
            pltpu.VMEM((count + 2 * halo, 128), BF16),
            pltpu.VMEM((halo, 128), BF16),
            pltpu.VMEM((8, rows + 4, W, 128), F32),
            pltpu.VMEM((count + extra, WIDE), BF16),
            pltpu.VMEM((KEPT, count), BF16),
            pltpu.VMEM((WIDE, hidden), BF16),
            pltpu.VMEM((hidden, TAPS * 128), BF16),
            pltpu.VMEM((16, hidden), F32),
            pltpu.VMEM((16, hidden), F32),
            pltpu.VMEM((128, hidden), BF16),
            pltpu.VMEM((128, hidden), BF16),
            pltpu.VMEM((count + extra, 128), BF16),
            pltpu.VMEM((128, count), BF16),
            pltpu.VMEM((count, hidden), BF16),
            pltpu.VMEM((count + extra, hidden), BF16),
            pltpu.VMEM((KEPT, SPAN), F32),
            pltpu.VMEM((count, 128), F32),
            pltpu.VMEM((count, 128), F32),
            pltpu.VMEM((count, 128), F32),
            pltpu.VMEM((count, 128), BF16),
            semaphores(()),
            semaphores(()),
            semaphores((2,)),
        ],
        compiler_params=sending(2, 63),
        name="hidden",
    )(
        table, x1, xm, cotangent, cot_o, heads_out, fc1_w, fc1_o, fc2_w, fc2_o, depth_taps, depth_o,
        hidden_shifts, hidden_o, front_gains, front_shifts, proj_w,
    )

    dq, grad_own, grad_send, output = pl.pallas_call(
        attend_back_kernel,
        grid=(bands // 2,),
        out_shape=(
            shape((bands, SLOTS, 128), BF16),
            shape((bands + 1, CELLS, 128)),
            shape((bands + 1, CELLS, 128), BF16),
            shape((count, 128), BF16),
        ),
        in_specs=[SMEM]
        + [VMEM] * 4
        + [
            two_slots,
            VMEM,
            VMEM,
            two_slots,
            pl.BlockSpec((2, 128, SLOTS), lambda i: (i, 0, 0)),
            pl.BlockSpec((2, 8, SLOTS), lambda i: (i, 0, 0)),
            pl.BlockSpec((2 * BAND, 128), lambda i: (i, 0)),
        ],
        out_specs=[two_slots, VMEM, VMEM, pl.BlockSpec((2 * BAND, 128), lambda i: (i, 0))],
        scratch_shapes=[
            pltpu.VMEM((total, COARSE, 128), F32),
            pltpu.VMEM((total, FINE, 128), F32),
            pltpu.VMEM((128, 128), BF16),
            pltpu.VMEM((2, 64, MAX_BANDS * COARSE), BF16),
            pltpu.VMEM((2, 2, 64, HALVES[0][1] * PACKED), BF16),
            pltpu.VMEM((2, MAX_BANDS * PACKED, 128), BF16),
            pltpu.VMEM((2, MAX_BANDS * PACKED, 128), BF16),
            pltpu.SMEM((2,), jnp.int32),
        ],
        compiler_params=params(),
        name="attend_back",
    )(table, key_c, key_f, val_c, val_f, xn, query_t, query_o, out_grad, out_t, lse, output)

    peers = sum(2 ** len(dims) - 1 for dims in stages(levels, True))
    links = group_links(levels, False) + 4 * group_links(levels, True) + 2 * len(stages(levels, True)) + 1
    early_rows, late_rows, later_rows = (group_size(levels, part) for part in (SPLIT, CONV, REST))
    pieces = 2 ** (levels - 1)
    joint_rows = (late_rows + later_rows) // pieces
    tokens_grad, early, joint, little = pl.pallas_call(
        functools.partial(tail_kernel, levels),
        out_shape=(
            shape((count, 128)),
            shape((2, 2, pieces, early_rows // pieces, 128), BF16),
            shape((2, 2, pieces, joint_rows, 128), BF16),
            shape((SMALL, 128)),
        ),
        in_specs=[HBM] * 3 + [VMEM, HBM] + [VMEM] * 2 + [HBM] * 3 + [VMEM] * 2 + [HBM] * 2
        + [VMEM] + ([HBM] * 2 + [VMEM] * 4) * 2,
        out_specs=[VMEM] * 4,
        scratch_shapes=[
            pltpu.VMEM((4 * QUARTER, 128), F32),
            pltpu.VMEM((len(stages(levels, True)), SMALL, 128), F32),
            pltpu.VMEM((peers, SMALL, 128), F32),
            semaphores((2, peers)),
            pltpu.VMEM((bands + 1, CELLS, 128), BF16),
            pltpu.VMEM((bands + 2, CELLS, 128), F32),
            pltpu.VMEM((bands + 2, CELLS, 128), F32),
            pltpu.VMEM((bands, SLOTS, 128), F32),
            semaphores((2,)),
            semaphores((2,)),
            semaphores((links,)),
            semaphores((links,)),
            pltpu.VMEM((128, coarse_conv.shape[0]), BF16),
            pltpu.VMEM((128, fine_conv.shape[0]), BF16),
            pltpu.VMEM((count, 128), F32),
            pltpu.VMEM((count, 128), F32),
            pltpu.VMEM((bands, SLOTS, 128), BF16),
            pltpu.VMEM(grad_own.shape, F32),
            pltpu.VMEM(split_g.shape, F32),
            pltpu.VMEM(slab.shape, F32),
            pltpu.VMEM(xn.shape, BF16),
            pltpu.VMEM(dq.shape, BF16),
            pltpu.VMEM(red_c.shape, F32),
            pltpu.VMEM(coarse_conv.shape, BF16),
            pltpu.VMEM(red_f.shape, F32),
            pltpu.VMEM(fine_conv.shape, BF16),
            pltpu.VMEM((16, 128, bands * 16), BF16),
            semaphores((12,)),
        ]
        + group_scratch(levels, False, early_rows)
        + group_scratch(levels, True, late_rows)
        + group_scratch(levels, True, later_rows),
        compiler_params=sending(0),
        name="tail",
    )(
        grad_own, grad_send, split_g, mid_g, slab, other, meta, xn, hat, dq, query_t, query_o, dx1,
        inverse, front_gains,
        red_c, coarse_conv, gain_c, coarse_shifts, coarse_kv, coarse_taps,
        red_f, fine_conv, gain_f, fine_shifts, fine_kv, fine_taps,
    )
    grads = pl.pallas_call(
        functools.partial(unpack_kernel, levels),
        out_shape=(
            shape((count, 128)),
            shape((2, 128)),
            shape((4, 128)),
            shape((half, 128)),
            shape(coarse_conv.shape),
            shape((1, 128)),
            shape((3, 128)),
            shape((128, 128)),
            shape((9, half)),
            shape(fine_conv.shape),
            shape((1, 128)),
            shape((3, 128)),
            shape((128, 128)),
            shape((9, half)),
            shape((128, 128)),
            shape((2, mine)),
            shape((128, mine)),
            shape((9, mine)),
            shape((mine, 128)),
        ),
        grid=(bands // 2,),
        in_specs=[VMEM] * 3 + [pl.BlockSpec((2 * BAND, 128), lambda i: (i, 0))],
        out_specs=[pl.BlockSpec((2 * BAND, 128), lambda i: (i, 0))] + [VMEM] * 18,
        compiler_params=params(),
        name="unpack",
    )(early, joint, little, tokens_grad)
    grads = [output] + list(grads)
    grads[4] = grads[4].T
    for at in (6, 11):
        grads[at] = grads[at].reshape(128)
    return tuple(grads)


def solution(mesh):
    tokens = P(("batch", "heads"), None)
    columns = P(None, "heads")
    return jax.shard_map(
        functools.partial(per_device, mesh.shape["batch"]),
        mesh=mesh,
        in_specs=(tokens, P("batch", None), tokens, P(), P(), columns)
        + (P(),) * 11
        + (columns, columns, columns, P("heads", None)),
        out_specs=(tokens, tokens, P(), P(), columns)
        + (P(),) * 11
        + (columns, columns, columns, P("heads", None)),
        check_vma=False,
    )
```

```python
import functools

import jax
import jax.numpy as jnp
from jax import lax
from jax.experimental import pallas as pl
from jax.experimental.pallas import tpu as pltpu
from jax.sharding import PartitionSpec as P

W = 56
BAND = 4 * W
SLOTS = 256
COARSE = 16
FINE = 64
CELLS = COARSE + FINE
MAX_BANDS = 14
EPS = 1e-06
F32 = jnp.float32
BF16 = jnp.bfloat16
SCALE = 32**-0.5
LOG2E = 1.4426950408889634
ROOT = 0.7071067811865476
EXP_SCALE = SCALE * LOG2E
BIG = -1e9
MIB = 1024 * 1024
STEP = 256
SPAN = 512
MESH = pl.DeviceIdType.MESH
TAPS = 9
KEPT = TAPS * 128 + 16
WIDE = (TAPS + 1) * 128
QUARTER = 768
CONV = 512
REST = QUARTER - CONV
SMALL = 48
SPLIT = 544


def dot(left, right):
    return jnp.dot(left, right, preferred_element_type=F32)


def dot_t(left, right):
    return lax.dot_general(left, right, (((1,), (1,)), ((), ())), preferred_element_type=F32)


def dot_in(left, right):
    return lax.dot_general(left, right, (((0,), (0,)), ((), ())), preferred_element_type=F32)


def gauss(values):
    return 0.5 + 0.5 * lax.erf(values * ROOT), jnp.exp2(values * values * (-0.5 * LOG2E))


def gelu_slope(values, cdf, bell):
    return cdf + values * bell * 0.3989422804014327


def fold_rows(values):
    wide = jnp.sum(values.reshape(-1, 64, 128), axis=0)
    return jnp.sum(wide.reshape(8, 8, 128), axis=0)


def norm_hat(values):
    centred = values - jnp.mean(values, axis=-1, keepdims=True)
    inverse = lax.rsqrt(jnp.mean(centred * centred, axis=-1, keepdims=True) + EPS)
    return centred * inverse, inverse


def norm_back(grad_scaled, hat, inverse):
    centre = jnp.mean(grad_scaled, axis=-1, keepdims=True)
    along = jnp.mean(grad_scaled * hat, axis=-1, keepdims=True)
    return inverse * (grad_scaled - centre - hat * along)


def slot_map(slot, token):
    a, b, c = slot >> 6, (slot >> 4) & 3, slot & 15
    hit = (token == a * W + 4 * c + b) & (c < 14)
    return jnp.where(hit, 1.0, 0.0).astype(BF16)


def to_slots():
    shape = (SLOTS, BAND)
    return slot_map(
        lax.broadcasted_iota(jnp.int32, shape, 0), lax.broadcasted_iota(jnp.int32, shape, 1)
    )


def from_slots():
    shape = (BAND, SLOTS)
    return slot_map(
        lax.broadcasted_iota(jnp.int32, shape, 1), lax.broadcasted_iota(jnp.int32, shape, 0)
    )


def cell_valid(shape, axis):
    return (lax.broadcasted_iota(jnp.int32, shape, axis) & 15) < 14


def roll_cells(values, step):
    lead = values.shape[:-2]
    flat = values.reshape(-1, values.shape[-1])
    flat = pltpu.roll(flat, step % flat.shape[0], 0)
    return flat.reshape(lead + values.shape[-2:])


def by_band(values, mask):
    count = values.shape[0]
    wide = values.reshape(count, -1, 8, 128) * mask.reshape(count, 1, 8, 128)
    return wide.reshape(values.shape)


def row_taps(taps, flip):
    order = [8 - i for i in range(9)] if flip else list(range(9))
    return [taps[i : i + 1, :] for i in order]


def depthwise_coarse(ext, above, below, taps, flip=False):
    t = row_taps(taps, flip)
    up, mid, down = by_band(ext[:-2], above), ext[1:-1], by_band(ext[2:], below)
    left, centre, right = (up * t[b] + mid * t[3 + b] + down * t[6 + b] for b in range(3))
    return centre + roll_cells(left, 1) + roll_cells(right, -1)


def fine_rows(ext, above, below):
    bands = ext.shape[0] - 2
    grid = ext.reshape(bands + 2, 2, 2, 16, 128)
    first, second = grid[:, 0], grid[:, 1]
    up = (by_band(second[:-2], above), first[1:-1])
    mid = (first[1:-1], second[1:-1])
    down = (second[1:-1], by_band(first[2:], below))
    return up, mid, down


def depthwise_fine(ext, above, below, taps, flip=False):
    t = row_taps(taps, flip)
    ups, mids, downs = fine_rows(ext, above, below)
    rows = []
    for up, mid, down in zip(ups, mids, downs):
        left, centre, right = (up * t[b] + mid * t[3 + b] + down * t[6 + b] for b in range(3))
        even = centre[:, 0] + roll_cells(left[:, 1], 1) + right[:, 1]
        odd = centre[:, 1] + left[:, 0] + roll_cells(right[:, 0], -1)
        rows.append((even, odd))
    return rows


def greet(*peers):
    barrier = pltpu.get_barrier_semaphore()
    for peer in peers:
        pl.semaphore_signal(barrier, inc=1, device_id=peer, device_id_type=MESH)


def met(count):
    pl.semaphore_wait(pltpu.get_barrier_semaphore(), count)


def fetch(pairs, sems):
    loads = [pltpu.make_async_copy(source, target, sems.at[i]) for i, (source, target) in enumerate(pairs)]
    for load in loads:
        load.start()
    return loads


def link(source, target, send_sem, recv_sem, peer):
    return pltpu.make_async_remote_copy(
        src_ref=source,
        dst_ref=target,
        send_sem=send_sem,
        recv_sem=recv_sem,
        device_id=peer,
        device_id_type=MESH,
    )


def remote(source, target, send_sem, recv_sem, peer):
    made = link(source, target, send_sem, recv_sem, peer)
    made.start()
    return made


def across():
    return (lax.axis_index("batch"), 1 - lax.axis_index("heads"))


def swap_lanes(values):
    half = values.shape[1] // 2
    return jnp.concatenate([values[:, half:], values[:, :half]], axis=1)


def keep_lanes(values, upper):
    lane = lax.broadcasted_iota(jnp.int32, values.shape, 1)
    return jnp.where((lane >= 64) if upper else (lane < 64), values, 0.0)


def pad_taps(taps, upper):
    gap = jnp.zeros(taps.shape, F32)
    return jnp.concatenate([gap, taps] if upper else [taps, gap], axis=1)


def band_tables(heights, table, meta, total):
    count = heights.shape[1]
    number = jnp.int32(0)
    start = jnp.int32(0)
    end = heights[0, 0]
    last = jnp.int32(-2)
    images, sames = [], []
    for band in range(total):
        passed = band >= end
        number = jnp.where(passed, number + 1, number)
        start = jnp.where(passed, end, start)
        grown = heights[0, jnp.minimum(number, count - 1)]
        grown = jnp.where(number < count, grown, 0)
        end = jnp.where(passed, end + grown, end)
        image = jnp.where(band < end, number, -1)
        same = jnp.where(image == last, 1, 0)
        last = image
        table[0, band] = image
        table[1, band] = jnp.minimum(start, total - MAX_BANDS)
        table[2, band] = same
        images.append(image)
        sames.append(same)
    for band in range(total, table.shape[1]):
        for row in range(3):
            table[row, band] = jnp.int32(0)
    sames.append(jnp.int32(0))
    for band in range(total):
        for row, value in enumerate((sames[band], sames[band + 1], images[band])):
            meta[row, band] = jnp.full((8, 128), value.astype(F32), F32)


def front_kernel(
    heights, tok, gains, shifts, conv_c, gain_c, shifts_c, kv_c, conv_f, gain_f, shifts_f, kv_f,
    query_t,
    table, meta, xn_out, hat_out, inv_out, red_c, red_f, slab, other, query_o,
    send, send_sems, recv_sems,
):
    bands = xn_out.shape[0]
    peer = across()
    greet(peer)
    copies = []

    def give(source, target):
        at = len(copies)
        copies.append(remote(source, target, send_sems.at[at], recv_sems.at[at], peer))

    place = to_slots()

    def norm_bands(first, count):
        rows = slice(first * BAND, (first + count) * BAND)
        hat, inverse = norm_hat(tok[rows, :].astype(F32))
        inv_out[rows, :] = jnp.broadcast_to(inverse, hat.shape)
        normed = (hat * gains[0:1, :] + shifts[0:1, :]).astype(BF16)
        sides = jnp.concatenate([normed, hat.astype(BF16)], axis=1)
        for band in range(count):
            both = dot(place, sides[band * BAND : (band + 1) * BAND]).astype(BF16)
            xn_out[first + band] = both[:, :128]
            hat_out[first + band] = both[:, 128:]

    def reduce(patches, conv, gain, shift, kv, out, at):
        red = dot(patches, conv) + shift[0:1, :]
        out[at : at + red.shape[0], :] = red
        hat, _ = norm_hat(red)
        normed = hat * gain[...] + shift[1:2, :]
        cdf, _ = gauss(normed)
        return dot((normed * cdf).astype(BF16), kv)

    kv_f_sw = swap_lanes(kv_f[...])
    part = bands // 2
    for first in (0, part):
        norm_bands(first, part)
        grid = xn_out[first : first + part].reshape(part, 16, 16, 128)
        patches = jnp.concatenate([fine_patch(grid, i) for i in range(4)], axis=1)
        pair = reduce(patches, conv_f[...], gain_f, shifts_f, kv_f_sw, red_f, first * FINE)
        pair = pair + keep_lanes(shifts_f[2:3, :], False)
        pair = jnp.where(cell_valid(pair.shape, 0), pair, 0.0).reshape(part, FINE, 128)
        slab[first : first + part, COARSE:CELLS, :] = pair
        send[first : first + part, COARSE:CELLS, :] = pair.astype(BF16)
        here = (pl.ds(first, part), pl.ds(COARSE, FINE))
        if first == 0:
            met(1)
        give(send.at[here], other.at[here])
        if first == 0:
            give(query_t, query_o)
    grid = xn_out[...].reshape(bands, 16, 16, 128)
    patches = jnp.concatenate([grid[:, i].reshape(bands * 16, 128) for i in range(16)], axis=1)
    pair = reduce(patches, conv_c[...], gain_c, shifts_c, kv_c[...], red_c, 0)
    pair = pair + keep_lanes(swap_lanes(shifts_c[2:3, :]), True)
    pair = jnp.where(cell_valid(pair.shape, 0), pair, 0.0).reshape(bands, COARSE, 128)
    slab[:, 0:COARSE, :] = pair
    send[:, 0:COARSE, :] = pair.astype(BF16)
    here = pl.ds(0, COARSE)
    give(send.at[:, here], other.at[:, here])
    band_tables(heights, table, meta, 2 * bands)
    for made in copies:
        made.wait()


def fine_slot(part, row, column):
    return (2 * row + (part >> 1)) * 4 + 2 * column + (part & 1)


def fine_patch(grid, part):
    bands = grid.shape[0]
    blocks = [
        grid[:, fine_slot(part, row, column)].reshape(bands, 1, 16, 128)
        for row in range(2)
        for column in range(2)
    ]
    return jnp.concatenate(blocks, axis=1).reshape(bands * FINE, 128)


def head_lanes(values, head):
    lane = lax.broadcasted_iota(jnp.int32, values.shape, 1)
    return jnp.where((lane >> 5) == head, values, jnp.zeros((), BF16))


def head_rows(values, head):
    row = lax.broadcasted_iota(jnp.int32, values.shape, 0)
    return jnp.where((row >> 5) == head, values, jnp.zeros((), BF16))


def score_rows(query_t, head, image, fine):
    row = lax.broadcasted_iota(jnp.int32, query_t.shape, 0)
    tag = row if fine else row - 64
    fill = jnp.where((tag >= 0) & (tag <= NOBODY) & (tag != image), BIG, 0.0).astype(BF16)
    return jnp.where((row >> 5) == head, query_t, fill)


def with_offset(rows, at, offset):
    start = at // 16 * 16
    block = rows[start : start + 16]
    row = lax.broadcasted_iota(jnp.int32, block.shape, 0)
    for i in range(3):
        term = offset.astype(BF16)
        block = jnp.where(row == at - start + i, term, block)
        offset = offset - term.astype(F32)
    parts = [rows[:start]] if start else []
    return jnp.concatenate(parts + [block, rows[start + 16 :]], axis=0)


def full_query(query_t, query_o, side):
    own, other = query_t[...].astype(F32), query_o[...].astype(F32)
    return jnp.where(
        side == 0,
        jnp.concatenate([own, other], axis=0),
        jnp.concatenate([other, own], axis=0),
    )


def window(ref, first):
    part = ref[pl.ds(first, MAX_BANDS)]
    return part.reshape(-1, 128).astype(BF16)


PACKED = 56
CHUNKS = ((0, 224), (224, 224), (448, 224), (672, 112))
HALVES = ((0, 8), (8, 6))
NOBODY = 32
ONES = 40


def tree_max(values):
    count = values.shape[0]
    while count % 16 == 0:
        count //= 2
        values = jnp.maximum(values[:count], values[count:])
    return jnp.max(values, axis=0, keepdims=True)


def attend_kernel(
    table, slab, other, meta, taps_c, taps_f, shifts_c, shifts_f, xn, tok, query_t, query_o, proj_w,
    gains, shifts, fc1, fc2, depth, hidden, cot,
    x1_out, xm_out, o_out, ot_out, lse_out, key_c, key_f, val_c, val_f, fc1_o, fc2_o, depth_o,
    hidden_o, cot_o,
    grid_ref, query_ref, place_ref, send_sems, recv_sems,
):
    step = pl.program_id(0)
    bands = slab.shape[0]
    total = 2 * bands
    side = lax.axis_index("heads")
    peer = across()
    halo = 2 * W
    edge = pl.multiple_of((1 - side) * (cot.shape[0] - halo), 16)
    swaps = [
        link(source, target, send_sems.at[i], recv_sems.at[i], peer)
        for i, (source, target) in enumerate(
            (
                (cot.at[pl.ds(edge, halo)], cot_o),
                (depth, depth_o),
                (hidden, hidden_o),
                (fc1, fc1_o),
                (fc2, fc2_o),
            )
        )
    ]

    @pl.when(step == 0)
    def _():
        greet(peer)
        place_ref[...] = from_slots()
        query_ref[...] = full_query(query_t, query_o, side).T.astype(BF16)
        grid_ref[0] = jnp.zeros((CELLS, 128), F32)
        grid_ref[total + 1] = jnp.zeros((CELLS, 128), F32)
        grid_ref[pl.ds(1 + side * bands, bands)] = slab[...]
        grid_ref[pl.ds(1 + (1 - side) * bands, bands)] = other[...].astype(F32)
        above, below, image = meta[0], meta[1], meta[2]
        lane = lax.broadcasted_iota(jnp.int32, (total, 16, 128), 2).astype(F32)
        valid = cell_valid((total, 16, 128), 1)
        wide = jnp.broadcast_to(image.reshape(total, 1, 8, 128), (total, 2, 8, 128))
        wide = wide.reshape(total, 16, 128)
        mark = jnp.where(valid & (wide >= 0.0), wide, float(NOBODY))

        ext = grid_ref[:, 0:COARSE, :]
        own = ext[1:-1]
        local = keep_lanes(shifts_c[2:3, :], True)
        mixed = own + depthwise_coarse(ext, above, below, pad_taps(taps_c[...], True)) + local
        val_c[...] = jnp.where(lane < 3.0, 1.0, mixed).astype(BF16)
        place = lane - 64.0
        one = (place >= ONES) & (place < ONES + 3)
        tag = jnp.where((place == mark) | one, 1.0, 0.0)
        keys = jnp.where(lane < 64.0, own, tag)
        key_c[...] = keys.astype(BF16)

        ext = grid_ref[:, COARSE:CELLS, :]
        local = keep_lanes(swap_lanes(shifts_f[2:3, :]), False)
        rows = depthwise_fine(ext, above, below, pad_taps(taps_f[...], False))
        tag = jnp.where((lane == mark) | ((lane >= ONES) & (lane < ONES + 3)), 1.0, 0.0)
        one = (lane >= 64.0) & (lane < 67.0)
        for row in range(2):
            for column in range(2):
                at = (2 * row + column) * 16
                own = ext[1:-1, at : at + 16, :]
                mixed = own + rows[row][column] + local
                cell = (2 * row + column) * 14
                val_f[:, cell : cell + 14, :] = jnp.where(one, 1.0, mixed)[:, 0:14]
                keys = jnp.where(lane >= 64.0, own.astype(BF16).astype(F32), tag)
                key_f[:, cell : cell + 14, :] = keys[:, 0:14]
        met(1)
        for swap in swaps:
            swap.start()

    each = xn.shape[0]
    images = [table[0, side * bands + each * step + i] for i in range(each)]
    firsts = [table[1, side * bands + each * step + i] for i in range(each)]
    queries = [
        dot(xn[i], query_ref[...]).astype(BF16).astype(F32).T.astype(BF16) for i in range(each)
    ]
    turned, windows = {}, {}

    def score(unit):
        i, head, part = unit
        fine = head >= 2
        start, size = CHUNKS[part]
        rows = slice(start, start + size)
        if not head & 1:
            if part == 0:
                windows[i, fine] = [
                    window(ref, firsts[i]) for ref in ((key_f, val_f) if fine else (key_c, val_c))
                ]
            turned[i, fine, part] = windows[i, fine][1][rows].T
        keys = windows[i, fine][0][rows]
        return dot(keys, score_rows(queries[i], head, images[i], fine))

    outs = [[None] * 4 for _ in range(each)]
    mixed = {}
    lse_out[...] = jnp.zeros(lse_out.shape, F32)

    def mix(unit, scores):
        i, head, part = unit
        fine = head >= 2
        top = tree_max(scores) * EXP_SCALE
        expo = jnp.exp2(scores * EXP_SCALE - top).astype(BF16)
        row = 32 * (head & 1) + (0 if fine else 64)
        vals = turned[i, fine, part][row : row + 32]
        left = jnp.concatenate([vals, jnp.ones((16, CHUNKS[part][1]), BF16)], axis=0)
        done = mixed.setdefault((i, head), [])
        done.append((top, dot(left, expo)))
        if len(done) < (4 if fine else 1):
            return
        top = functools.reduce(jnp.maximum, [part_top for part_top, _ in done])
        total = None
        for part_top, value in done:
            value = value * jnp.exp2(part_top - top)
            total = value if total is None else total + value
        sums = total[32:33]
        lse_out[i, head : head + 1, :] = top + jnp.log2(sums)
        outs[i][head] = total[0:32] * (1.0 / sums)

    waiting = []
    for i in range(each):
        for head, parts in ((2, 4), (0, 1), (3, 4), (1, 1)):
            for part in range(parts):
                waiting.append(((i, head, part), score((i, head, part))))
                if len(waiting) > 6:
                    mix(*waiting.pop(0))
    for unit, scores in waiting:
        mix(unit, scores)
    place = place_ref[...]
    joined = []
    for i in range(each):
        live = jnp.where(images[i] >= 0, 1.0, 0.0)
        out_t = jnp.concatenate(outs[i], axis=0) * live
        ot_out[i] = out_t
        joined.append(dot(place, out_t.T.astype(BF16)).astype(BF16))
    heads_out = jnp.concatenate(joined, axis=0)
    o_out[...] = heads_out
    middle = tok[...].astype(F32) + dot(heads_out, proj_w[...]) + shifts[1:2, :]
    x1_out[...] = middle
    hat, _ = norm_hat(middle)
    xm_out[...] = (hat * gains[1:2, :] + shifts[2:3, :]).astype(BF16)

    @pl.when(step == pl.num_programs(0) - 1)
    def _():
        for swap in swaps:
            swap.wait()


def shift_right(values):
    column = lax.broadcasted_iota(jnp.int32, values.shape, 0)
    return jnp.where(column == 0, 0.0, pltpu.roll(values, 1, 0))


def shift_left(values):
    column = lax.broadcasted_iota(jnp.int32, values.shape, 0)
    return jnp.where(column == W - 1, 0.0, pltpu.roll(values, W - 1, 0))


def mask_lanes():
    lane = lax.broadcasted_iota(jnp.int32, (W, 128), 1)
    column = lax.broadcasted_iota(jnp.int32, (W, 128), 0)
    tap = jnp.where(lane < 32, lane & 15, 15)
    parts = []
    for a in range(3):
        hit = tap == 3 * a + 1
        hit = hit | ((tap == 3 * a) & (column > 0)) | ((tap == 3 * a + 2) & (column < W - 1))
        if a == 1:
            hit = hit | (tap == TAPS)
        parts.append(jnp.where(hit, 1.0, 0.0))
    return parts


def hidden_kernel(
    table, x1_in, xm, cot, cot_o, heads_in, fc1, fc1_o, fc2, fc2_o, depth, depth_o, hidden, hidden_o,
    gains, shifts, proj_w,
    out, dx1_out, do_out, split_g, mid_g,
    xm_ext, halo_ref, moved, wide, wide_t, weights, weights_t, taps, bias, base_ref, fc2_t, dy, dy_t, act, du,
    sums, dxm, out_acc, x1, heads_out, send_sem, recv_sem, load_sems,
):
    side = lax.axis_index("heads")
    peer = across()
    tokens = x1.shape[0]
    rows = tokens // W
    bands = tokens // BAND
    halo = 2 * W
    extra = wide.shape[0] - tokens
    mine = fc1.shape[1]
    width = 2 * mine
    halo_at = pl.multiple_of((1 - side) * (halo + tokens), 16)
    halo_row = 1 + (1 - side) * (rows + 1)
    greet(peer)
    loads = fetch(((x1_in, x1), (heads_in, heads_out)), load_sems)
    edge = pl.multiple_of((1 - side) * (tokens - halo), 16)
    swap = link(xm.at[pl.ds(edge, halo)], halo_ref, send_sem, recv_sem, peer)

    def live_band(band):
        return jnp.where(table[0, band] >= 0, 1.0, 0.0)

    def neighbour(row):
        place = side * rows - 2 + row
        band = jnp.maximum(place, 0) >> 2
        up = jnp.where((place & 3) == 0, table[2, band], 1)
        down = jnp.where((place & 3) == 3, table[2, band + 1], 1)
        return up.astype(F32), down.astype(F32)

    xm_ext[0:halo, :] = jnp.zeros((halo, 128), BF16)
    xm_ext[halo + tokens : tokens + 2 * halo, :] = jnp.zeros((halo, 128), BF16)
    xm_ext[halo : halo + tokens, :] = xm[...]
    for band in range(bands):
        at = slice(band * BAND, (band + 1) * BAND)
        dy[at, :] = (cot[at, :].astype(F32) * live_band(side * bands + band)).astype(BF16)
    tail = cot_o[...].astype(F32)
    tail = jnp.where(side == 0, tail[:W], tail[W:]) * live_band((1 - side) * bands + side * (bands - 1))
    tail = jnp.concatenate([tail, jnp.zeros((extra - W, 128), F32)], axis=0)
    dy[tokens : tokens + extra, :] = tail.astype(BF16)

    taps[...] = jnp.zeros(taps.shape, F32)
    bias[...] = jnp.zeros(bias.shape, F32)
    for part, (taps_ref, shift_ref, fc1_ref, fc2_ref) in enumerate(
        ((depth, hidden, fc1, fc2), (depth_o, hidden_o, fc1_o, fc2_o))
    ):
        lanes = slice(part * mine, part * mine + mine)
        taps[0:TAPS, lanes] = taps_ref[...]
        taps[TAPS : TAPS + 1, lanes] = shift_ref[0:1, :]
        bias[0:TAPS, lanes] = taps_ref[...] * shift_ref[0:1, :]
        bias[TAPS : TAPS + 1, lanes] = shift_ref[0:1, :] + shift_ref[1:2, :]
        fc2_t[:, lanes] = fc2_ref[...].T
        base_ref[:, lanes] = fc1_ref[...]
        base = fc1_ref[...].astype(F32)
        for k in range(TAPS):
            factor = taps_ref[k : k + 1, :] + (1.0 if k == 4 else 0.0)
            weights[k * 128 : k * 128 + 128, lanes] = (base * (factor * ROOT)).astype(BF16)
    scaled = bias[...] * ROOT
    high = scaled.astype(BF16)
    weights[TAPS * 128 : TAPS * 128 + 16, :] = high
    weights[TAPS * 128 + 16 : TAPS * 128 + 32, :] = (scaled - high.astype(F32)).astype(BF16)
    weights[TAPS * 128 + 32 : WIDE, :] = jnp.zeros((96, width), BF16)

    met(1)
    swap.start()

    def move_rows(pair, carry):
        both = xm_ext[pl.ds(pl.multiple_of(pair * halo, 16), halo), :].astype(F32)
        for i in range(2):
            row = both[W * i : W * i + W]
            moved[0, 2 * pair + i] = shift_right(row)
            moved[1, 2 * pair + i] = row
            moved[2, 2 * pair + i] = shift_left(row)
        return carry

    lax.fori_loop(1, rows // 2 + 1, move_rows, 0, unroll=2)
    swap.wait()
    xm_ext[pl.ds(halo_at, halo), :] = halo_ref[...]
    move_rows(0, 0)
    move_rows(rows // 2 + 1, 0)

    masks = mask_lanes()

    def gather_row(row, block):
        up, down = neighbour(row)
        if block == TAPS:
            return masks[0] * up + masks[1] + masks[2] * down
        a, b = divmod(block, 3)
        values = moved[b, row + a - 1]
        return values if a == 1 else values * (up if a == 0 else down)

    inner = masks[0] + masks[1] + masks[2]

    def gather_band(band, carry):
        row = 2 + 4 * band
        up, _ = neighbour(row)
        _, down = neighbour(row + 3)
        for block in range(TAPS + 1):
            if block == TAPS:
                first = masks[0] * up + masks[1] + masks[2]
                last = masks[0] + masks[1] + masks[2] * down
                parts = [first, inner, inner, last]
            else:
                a, b = divmod(block, 3)
                parts = [moved[b, row + i + a - 1] for i in range(4)]
                if a == 0:
                    parts[0] = parts[0] * up
                elif a == 2:
                    parts[3] = parts[3] * down
            both = jnp.concatenate(parts, axis=0).astype(BF16)
            wide[pl.ds(pl.multiple_of(band * BAND, 16), BAND), block * 128 : block * 128 + 128] = both
        return carry

    lax.fori_loop(0, bands, gather_band, 0)
    for block in range(TAPS + 1):
        lanes = slice(block * 128, block * 128 + 128)
        tail = jnp.concatenate([gather_row(halo_row, block), jnp.zeros((extra - W, 128), F32)], axis=0)
        wide[tokens : tokens + extra, lanes] = tail.astype(BF16)

    def fc2_part(n):
        ref, at = (fc2, n * SPAN) if n * SPAN < mine else (fc2_o, n * SPAN - mine)
        return ref[at : at + SPAN, :]

    def one_block(at, own):
        total = None
        coming = dot(wide[at, :], weights[:, 0:SPAN])
        for n in range(width // SPAN):
            lanes = slice(n * SPAN, n * SPAN + SPAN)
            spread = coming
            if (n + 1) * SPAN < width:
                coming = dot(wide[at, :], weights[:, (n + 1) * SPAN : (n + 2) * SPAN])
            grad = dot(dy[at, :], fc2_t[:, lanes])
            bell = jnp.exp2(spread * spread * -LOG2E)
            share = 1.0 + lax.erf(spread)
            du[at, lanes] = (grad * (share + spread * bell * 1.1283791670955126)).astype(BF16)
            if own:
                active = (spread * share).astype(BF16)
                act[at, lanes] = active
                part = dot(active, fc2_part(n))
                total = part if total is None else total + part
        return total

    size = 896

    def own_block(block, carry):
        at = pl.ds(pl.multiple_of(block * size, 128), size)
        for part in range(TAPS + 1):
            kept = min(128, KEPT - part * 128)
            turned = wide[at, part * 128 : part * 128 + 128].T
            wide_t[part * 128 : part * 128 + kept, at] = turned[0:kept]
        dy_t[:, at] = dy[at, :].T
        out_acc[at, :] = one_block(at, True) * ROOT
        return carry

    lax.fori_loop(0, tokens // size, own_block, 0)
    one_block(slice(tokens, tokens + extra), False)

    def fold(half):
        lanes = pl.ds(pl.multiple_of(half * SPAN, SPAN), SPAN)
        base = base_ref[:, lanes].astype(F32)
        grad = sums[4 * 128 : 5 * 128, :]
        marks = sums[TAPS * 128 : KEPT, :]
        mean = marks[TAPS : TAPS + 1]
        bias_g = mean
        rows_g = []
        factors = taps[:, lanes]
        for k in range(TAPS):
            part = sums[k * 128 : k * 128 + 128, :]
            mark = marks[k : k + 1]
            factor = factors[k : k + 1]
            grad = grad + part * factor
            bias_g = bias_g + mark * factor
            rows_g.append(jnp.sum(part * base, axis=0, keepdims=True) + mark * factors[TAPS : TAPS + 1])
        rows_g = jnp.concatenate(rows_g + [bias_g, mean, jnp.zeros((5, SPAN), F32)], axis=0)
        for i in range(SPAN // 128):
            core, row = divmod(i, STEP // 128)
            piece = slice(i * 128, i * 128 + 128)
            split_g[half, core, row * 128 : row * 128 + 128, :] = grad[:, piece] * 0.5
            split_g[half, core, 512 + 16 * row : 528 + 16 * row, :] = rows_g[:, piece] * 0.5

    def gradients(half, carry):
        lanes = pl.ds(pl.multiple_of(half * SPAN, SPAN), SPAN)
        for part in (slice(0, 592), slice(592, KEPT)):
            sums[part, :] = dot(wide_t[part, :], du[0:tokens, lanes])
        turned = dot(dy_t[...], act[:, lanes]).T * ROOT
        for core in range(2):
            split_g[half, core, 256:512, :] = turned[core * STEP : core * STEP + STEP]
        for k in range(TAPS):
            weights_t[lanes, k * 128 : k * 128 + 128] = weights[k * 128 : k * 128 + 128, lanes].T
        fold(half)
        return carry

    lax.fori_loop(0, width // SPAN, gradients, 0)

    groups = ((4, 1, 7, 0), (3, 6, 2, 5), (8,))

    def collect_row(group, base, row):
        total = [None] * 3
        for i, k in enumerate(group):
            a, b = divmod(k, 3)
            source = row + 3 - a
            part = moved[base + i, source]
            if a != 1:
                up, down = neighbour(source)
                part = part * (up if a == 0 else down)
            total[b] = part if total[b] is None else total[b] + part
        if total[0] is not None:
            total[0] = shift_left(total[0])
        if total[2] is not None:
            total[2] = shift_right(total[2])
        total = functools.reduce(jnp.add, [part for part in total if part is not None])
        at = pl.ds(pl.multiple_of(row * W, 8), W)
        if group[0] == 4:
            dxm[at, :] = total
        else:
            dxm[at, :] += total

    for number, group in enumerate(groups):
        base = 4 * (number & 1)
        for i in range(len(group)):
            moved[base + i, 1] = jnp.zeros((W, 128), F32)
            moved[base + i, rows + 2] = jnp.zeros((W, 128), F32)

        def back(at):
            parts = [weights_t[:, k * 128 : k * 128 + 128] for k in group]
            return dot(du[at, :], jnp.concatenate(parts, axis=1))

        tail = back(slice(tokens, tokens + extra))
        for i in range(len(group)):
            moved[base + i, halo_row] = tail[0:W, i * 128 : i * 128 + 128]

        def back_block(block, carry):
            result = back(pl.ds(pl.multiple_of(block * 4 * BAND, 16), 4 * BAND))
            for i in range(len(group)):
                moved[base + i, pl.ds(2 + 16 * block, 16)] = result[
                    :, i * 128 : i * 128 + 128
                ].reshape(16, W, 128)
            if number:
                for i in range(16):
                    collect_row(groups[number - 1], 4 - base, 16 * block + i)
            return carry

        lax.fori_loop(0, bands // 4, back_block, 0)

    def last_rows(row, carry):
        collect_row(groups[-1], 4 * ((len(groups) - 1) & 1), row)
        return carry

    lax.fori_loop(0, rows, last_rows, 0, unroll=4)

    mid_g[...] = jnp.zeros(mid_g.shape, F32)
    for load in loads:
        load.wait()
    place = to_slots()
    proj = proj_w[...].astype(F32)
    proj_sw = jnp.concatenate([proj[64:], proj[:64]], axis=0).T.astype(BF16)

    def fold_up(values):
        return jnp.sum(jnp.sum(values.reshape(-1, 64, 128), axis=0).reshape(8, 8, 128), axis=0)

    def two_bands(block, carry):
        at = pl.ds(pl.multiple_of(block * 2 * BAND, 16), 2 * BAND)
        middle = x1[at, :]
        result = middle + out_acc[at, :] + shifts[3:4, :]
        hat, inverse = norm_hat(middle)
        grad = dxm[at, :] * ROOT
        grad_y = dy[at, :].astype(F32)
        dx1 = grad_y + norm_back(grad * gains[1:2, :], hat, inverse)
        dx1_out[at, :] = dx1
        dz = dx1.astype(BF16)
        mid_g[8:136, :] += dot_in(heads_out[at, :], dz)
        do = dot(dz, proj_sw)
        for i in range(2):
            band = 2 * block + i
            live = live_band(side * bands + band)
            part = slice(i * BAND, (i + 1) * BAND)
            here = pl.ds(pl.multiple_of(band * BAND, 16), BAND)
            out[here, :] = (result[part] * live).astype(BF16)
            do_out[band] = dot(place, (do[part] * live).astype(BF16)).astype(BF16)
        terms = (grad * hat, grad, dz.astype(F32), grad_y)
        return tuple(total + fold_up(term) for total, term in zip(carry, terms))

    zero = jnp.zeros((8, 128), F32)
    totals = lax.fori_loop(0, bands // 2, two_bands, (zero,) * 4)
    for i in range(4):
        mid_g[i : i + 1, :] = jnp.sum(totals[i], axis=0, keepdims=True)


def stages(levels, shared):
    rest = list(range(2, levels))
    pairs = [rest[i : i + 2] for i in range(0, len(rest), 2)]
    return [[0], ["x", 1]] + pairs if shared else [[0], [1]] + pairs + [["x"]]


def group_size(levels, rows):
    unit = 16 * 2 ** (levels - 1)
    return -(-rows // unit) * unit


def stage_shapes(levels, shared, rows):
    halves, shapes = 2, [(1, 2, rows, 128)]
    for dims in stages(levels, shared)[1:]:
        if "x" in dims:
            halves = 1
        rows >>= sum(1 for dim in dims if dim != "x")
        shapes.append((2 ** len(dims) - 1, halves, rows, 128))
    return shapes


def group_scratch(levels, shared, rows):
    buffers = [pltpu.VMEM(part, BF16) for part in stage_shapes(levels, shared, rows)]
    return [pltpu.VMEM((2, rows, 128), F32)] + buffers + buffers


def group_links(levels, shared):
    return sum(2 ** len(dims) - 1 for dims in stages(levels, shared))


def everyone(levels):
    batch, side = lax.axis_index("batch"), lax.axis_index("heads")
    peers = []
    for dims in stages(levels, True):
        for flips in range(1, 2 ** len(dims)):
            peers.append(flipped(batch, side, dims, flips))
    return peers


def flipped(batch, side, dims, flips):
    for i, dim in enumerate(dims):
        if flips >> i & 1:
            if dim == "x":
                side = 1 - side
            else:
                batch = batch + (1 - 2 * ((batch // 2**dim) % 2)) * 2**dim
    return batch, side


class Group:
    def __init__(self, levels, shared, buffers, sems, base):
        self.stages = stages(levels, shared)
        count = len(self.stages)
        self.cur, self.sends, self.recvs = buffers[0], buffers[1 : 1 + count], buffers[1 + count :]
        self.sems, self.base = sems, base
        self.batch, self.side = lax.axis_index("batch"), lax.axis_index("heads")
        self.core = self.batch % 2
        at, rows = 0, self.cur.shape[1]
        self.kept, self.given = [(at, rows)], [None]
        for dims in self.stages[1:]:
            bits = [dim for dim in dims if dim != "x"]
            starts = []
            for flips in range(2 ** len(dims)):
                batch, _ = flipped(self.batch, self.side, dims, flips)
                start = at
                for i, bit in enumerate(bits):
                    start = start + ((batch // 2**bit) % 2) * (rows >> (i + 1))
                starts.append(pl.multiple_of(start, 16))
            rows >>= len(bits)
            at = starts[0]
            self.kept.append((at, rows))
            self.given.append(starts)
        self.left = list(range(count))

    def link(self, stage, flips):
        number = self.base + sum(2 ** len(part) - 1 for part in self.stages[:stage]) + flips - 1
        peer = flipped(self.batch, self.side, self.stages[stage], flips)
        source, target = self.sends[stage].at[flips - 1], self.recvs[stage].at[flips - 1]
        return link(source, target, self.sems[0].at[number], self.sems[1].at[number], peer)

    def wait(self, stage):
        for flips in range(1, 2 ** len(self.stages[stage])):
            self.link(stage, flips).wait()

    def add(self, stage):
        at, rows = self.kept[stage]
        here, recv = pl.ds(at, rows), self.recvs[stage]
        if recv.shape[1] == 2:
            total = self.cur[:, here, :]
            for i in range(recv.shape[0]):
                total = total + recv[i].astype(F32)
            self.cur[:, here, :] = total
            return
        total = self.cur[self.side, here, :]
        for i in range(recv.shape[0]):
            total = total + recv[i, 0].astype(F32)
        self.cur[self.side, here, :] = total

    def advance(self, count=1, pieces=None):
        for number in self.left[:count]:
            self.phase(number, pieces)
        del self.left[:count]

    def phase(self, number, pieces):
        count = len(self.stages)
        if number == 0:
            for half in range(2):
                for row, value in pieces(half, 1 - self.core):
                    self.sends[0][0, half, row : row + value.shape[0], :] = value.astype(BF16)
            self.link(0, 1).start()
            for half in range(2):
                for row, value in pieces(half, self.core):
                    self.cur[half, row : row + value.shape[0], :] = value
        else:
            self.wait(number - 1)
            self.add(number - 1)
            dims = self.stages[number]
            _, rows = self.kept[number]
            for flips in range(1, 2 ** len(dims)):
                crossing = "x" in dims and flips >> dims.index("x") & 1
                here = pl.ds(self.given[number][flips], rows)
                if self.sends[number].shape[1] == 2:
                    self.sends[number][flips - 1] = self.cur[:, here, :].astype(BF16)
                else:
                    half = 1 - self.side if crossing else self.side
                    self.sends[number][flips - 1, 0] = self.cur[half, here, :].astype(BF16)
                self.link(number, flips).start()

    def finish(self):
        self.wait(len(self.stages) - 1)
        self.add(len(self.stages) - 1)
        at, rows = self.kept[-1]
        return self.cur[self.side, pl.ds(at, rows), :].astype(BF16)


class Gather:
    def __init__(self, levels, out, shared, sems, base):
        self.stages, self.out, self.shared = stages(levels, True), out, shared
        self.sems, self.base = sems, base
        self.batch, self.side = lax.axis_index("batch"), lax.axis_index("heads")
        self.core = self.batch % 2
        at, count = 0, out.shape[2]
        self.kept = [(at, count)]
        for dims in self.stages[1:]:
            for bit in dims:
                if bit != "x":
                    count //= 2
                    at = at + ((self.batch // 2**bit) % 2) * count
            self.kept.append((at, count))
        self.left = list(range(len(self.stages)))

    def links(self, stage):
        dims = self.stages[stage]
        at, count = self.kept[stage]
        number = self.base + sum(2 ** len(part) for part in self.stages[:stage])
        mine = self.out.at[self.core, self.side, pl.ds(at, count)]
        for flips in range(1, 2 ** len(dims)):
            part = mine
            if "x" in dims and flips >> dims.index("x") & 1:
                if not self.shared:
                    continue
                part = self.out.at[self.core, self.side, pl.ds(at, count), pl.ds(0, self.shared)]
            yield self.made(part, number, flipped(self.batch, self.side, dims, flips))
            number += 1
        if stage == 0 and self.shared:
            part = self.out.at[self.core, 1 - self.side, :, pl.ds(0, self.shared)]
            yield self.made(part, number, flipped(self.batch, self.side, dims, 1))

    def made(self, part, number, peer):
        return link(part, part, self.sems[0].at[number], self.sems[1].at[number], peer)

    def begin(self, pieces):
        at, _ = self.kept[-1]
        row = 0
        for piece in pieces:
            self.out[self.core, self.side, at, row : row + piece.shape[0], :] = piece
            row += piece.shape[0]
        for made in self.links(len(self.stages) - 1):
            made.start()

    def advance(self):
        stage = len(self.left) - 1
        for made in self.links(stage):
            made.wait()
        if stage:
            for made in self.links(stage - 1):
                made.start()
        del self.left[-1]


def attend_back_kernel(
    table, key_c, key_f, val_c, val_f, xn, query_t, query_o, do_ref, ot_ref, lse, output,
    dq_out, own_out, send_out, output_out,
    acc_c, acc_f, query_ref, turned_c, turned_f, keys_ref, vals_ref, kept,
):
    step = pl.program_id(0)
    each = xn.shape[0]
    bands = each * pl.num_programs(0)
    side = lax.axis_index("heads")

    @pl.when(step == 0)
    def _():
        acc_c[...] = jnp.zeros(acc_c.shape, F32)
        acc_f[...] = jnp.zeros(acc_f.shape, F32)
        query_ref[...] = full_query(query_t, query_o, side).T.astype(BF16)

    output_out[...] = output[...]
    firsts = [table[1, side * bands + each * step + i] for i in range(each)]
    for i in range(each):

        @pl.when((step == 0) | (kept[i] != firsts[i]))
        def _():
            kept[i] = firsts[i]
            keys = window(key_f, firsts[i])
            keys_ref[i] = keys
            vals_ref[i] = window(val_f, firsts[i])
            for part, (start, count) in enumerate(HALVES):
                rows = slice(start * PACKED, (start + count) * PACKED)
                turned_f[i, part, :, 0 : count * PACKED] = keys[rows].T[64:128]
            turned_c[i] = window(key_c, firsts[i]).T[0:64]

    queries, query_rows, grads_t, grads_low = [], [], [], []
    for i in range(each):
        query = dot(xn[i], query_ref[...]).astype(BF16)
        queries.append(query)
        query_rows.append(query.astype(F32).T.astype(BF16))
        grads_t.append(do_ref[i].astype(F32).T)
        grads_low.append(grads_t[i].astype(BF16))
    dq = [[None] * 4 for _ in range(each)]

    def products(unit):
        i, head, part = unit
        fine = head >= 2
        image = table[0, side * bands + each * step + i]
        start, count = HALVES[part]
        if fine:
            rows = slice(start * PACKED, (start + count) * PACKED)
            keys, vals = keys_ref[i, rows], vals_ref[i, rows]
        else:
            keys, vals = window(key_c, firsts[i]), window(val_c, firsts[i])
        swapped = (head + 2) & 3
        delta = jnp.sum(
            ot_ref[i, 32 * head : 32 * head + 32]
            * grads_t[i][32 * swapped : 32 * swapped + 32],
            axis=0,
            keepdims=True,
        )
        offset = lse[i, head : head + 1, :] * (-1.0 / EXP_SCALE)
        left = score_rows(query_rows[i], head, image, fine)
        left = with_offset(left, ONES + (0 if fine else 64), offset)
        right = with_offset(head_rows(grads_low[i], swapped), 64 if fine else 0, -delta)
        return dot(keys, left), dot(vals, right)

    held = {}

    def back(unit, score, prob_grad):
        i, head, part = unit
        fine = head >= 2
        swapped = (head + 2) & 3
        prob = jnp.exp2(score * EXP_SCALE)
        score_grad = (prob * prob_grad).astype(BF16)
        row = 32 * (head & 1)
        start, count = HALVES[part]
        turned = turned_c[i, row : row + 32]
        if fine:
            turned = turned_f[i, part, row : row + 32, 0 : count * PACKED]
        grad = dot(turned, score_grad)
        dq[i][head] = grad if part == 0 else dq[i][head] + grad
        pair = held.setdefault((i, fine, part), ([], []))
        pair[0].extend([score_grad, prob.astype(BF16)])
        pair[1].extend([head_lanes(queries[i], head), head_lanes(do_ref[i], swapped)])
        if head & 1:
            both = dot(jnp.concatenate(pair[0], axis=1), jnp.concatenate(pair[1], axis=0))
            if fine:
                at = pl.ds(firsts[i] + start, count)
                acc_f[at, 0:PACKED, :] += both.reshape(count, PACKED, 128)
            else:
                acc_c[pl.ds(firsts[i], MAX_BANDS)] += both.reshape(MAX_BANDS, COARSE, 128)

    waiting = []
    for i in range(each):
        for head, parts in ((2, 2), (3, 2), (0, 1), (1, 1)):
            for part in range(parts):
                waiting.append(((i, head, part), *products((i, head, part))))
                if len(waiting) > 3:
                    back(*waiting.pop(0))
    for unit in waiting:
        back(*unit)
    for i in range(each):
        dq_out[i] = (jnp.concatenate(dq[i], axis=0).T * SCALE).astype(BF16)

    @pl.when(step == pl.num_programs(0) - 1)
    def _():
        span = bands + 1
        lane = lax.broadcasted_iota(jnp.int32, (1, 128), 1)
        scale_c = jnp.where(lane < 64, SCALE, 1.0)
        scale_f = jnp.where(lane < 64, 1.0, SCALE)
        for dest, at, kind in (
            (own_out, side * (bands - 1), F32),
            (send_out, (1 - side) * (bands - 1), BF16),
        ):
            dest[:, 0:COARSE, :] = (acc_c[pl.ds(at, span)] * scale_c).astype(kind)
            for cell in range(4):
                part = acc_f[pl.ds(at, span), 14 * cell : 14 * cell + 16, :] * scale_f
                part = jnp.where(cell_valid(part.shape, 1), part, 0.0)
                row = COARSE + 16 * cell
                dest[:, row : row + 16, :] = part.astype(kind)


def tail_kernel(
    levels, own_in, given, split_in, mid_g, slab_in, other, meta, xn_in, hat_in, dq_in, query_t,
    query_o, dx1_in, inv_in, gains,
    red_c_in, conv_c_in, gain_c, shifts_c, kv_c, taps_c_ref,
    red_f_in, conv_f_in, gain_f, shifts_f, kv_f, taps_f_ref,
    tok_grad, early, joint, little,
    pack, small, small_in, small_sems, recv, grad_ref, val_ref, dxn, send_sem, recv_sem, send_sems, recv_sems, turned_c, turned_f,
    dx1, inv, hat_ref, own, split_g, slab, xn, dq, red_c, conv_c, red_f, conv_f, xt, load_sems,
    *buffers,
):
    bands = xn.shape[0]
    side = lax.axis_index("heads")
    greet(*everyone(levels))
    early_pairs = (
        (split_in, split_g), (dq_in, dq), (xn_in, xn), (own_in, own), (slab_in, slab),
        (conv_c_in, conv_c), (conv_f_in, conv_f),
    )
    loads = fetch(early_pairs, load_sems)
    met(len(everyone(levels)))
    swaps = [
        remote(given.at[:, here], recv.at[:, here], send_sem.at[i], recv_sem.at[i], across())
        for i, here in enumerate((pl.ds(0, COARSE), pl.ds(COARSE, FINE)))
    ]
    late_pairs = (
        (red_c_in, red_c), (red_f_in, red_f), (hat_in, hat_ref), (inv_in, inv), (dx1_in, dx1),
    )
    loads += fetch(late_pairs, load_sems.at[pl.ds(len(early_pairs), len(late_pairs))])
    sems = (send_sems, recv_sems)
    split_count, shared_count = (1 + 2 * len(stages(levels, shared)) for shared in (False, True))
    before = Group(levels, False, buffers[:split_count], sems, 0)
    base = group_links(levels, False)
    buffers = buffers[split_count:]
    conv = Group(levels, True, buffers[:shared_count], sems, base)
    base += group_links(levels, True)
    rest = Group(levels, True, buffers[shared_count:], sems, base)
    base += group_links(levels, True)
    early_rows, late_rows, later_rows = (group.cur.shape[1] for group in (before, conv, rest))
    gather = Gather(levels, joint, joint.shape[3], sems, base)
    base += group_links(levels, True) + len(stages(levels, True))
    gather_split = Gather(levels, early, 0, sems, base)

    def split_pieces(half, which):
        yield 0, split_g[(half + side) % 2, which]
        if early_rows > SPLIT:
            yield SPLIT, jnp.zeros((early_rows - SPLIT, 128), F32)

    def shared_pieces(first, used, rows):
        def pieces(half, which):
            at = pl.multiple_of(first + used * (2 * half + which), 16)
            yield 0, pack[pl.ds(at, used), :]
            if rows > used:
                yield used, jnp.zeros((rows - used, 128), F32)

        return pieces

    batch, order = lax.axis_index("batch"), stages(levels, True)

    def small_links(stage):
        before = sum(2 ** len(dims) - 1 for dims in order[:stage])
        for flips in range(1, 2 ** len(order[stage])):
            at = before + flips - 1
            yield at, link(
                small.at[stage], small_in.at[at], small_sems.at[0, at], small_sems.at[1, at],
                flipped(batch, side, order[stage], flips),
            )

    def small_phase(stage):
        if stage:
            total = small[stage - 1]
            for at, made in small_links(stage - 1):
                made.wait()
                total = total + small_in[at]
            if stage == len(order):
                little[...] = total
                return
            small[stage] = total
        for _, made in small_links(stage):
            made.start()

    for load in loads[:7]:
        load.wait()
    before.advance(1, split_pieces)

    start = 0
    parts = []
    for count in (conv_c.shape[0], conv_f.shape[0], 128, 128, 128, 128):
        parts.append(pack.at[start : start + count])
        start += count
    conv_c_g, conv_f_g, kv_c_g, kv_f_g, query_g, proj_g = parts
    small_c, small_f, front_g = small.at[0, 0:16], small.at[0, 16:32], small.at[0, 32:40]
    small[0, 40:48, :] = mid_g[0:8, :]
    proj_g[...] = mid_g[8:136, :]
    taps_c, taps_f = pad_taps(taps_c_ref[...], True), pad_taps(taps_f_ref[...], False)
    kv_f_sw = swap_lanes(kv_f[...])

    val_ref[0] = jnp.zeros((CELLS, 128), F32)
    val_ref[bands + 1] = jnp.zeros((CELLS, 128), F32)
    val_ref[1 : bands + 1] = slab[...]
    val_ref[pl.ds((1 - side) * (bands + 1), 1)] = other[
        pl.ds(side * (bands - 1), 1)
    ].astype(F32)
    at = pl.ds(side * bands, bands)
    above, below = meta[0, at], meta[1, at]
    grid = xn[...].reshape(bands, 16, 16, 128)
    slot_grads = dq[...].reshape(bands, 16, 16, 128)
    total = None
    for i in range(16):
        turned = grid[:, i].reshape(bands * 16, 128).T
        xt[i] = turned
        part = dot(turned, slot_grads[:, i].reshape(bands * 16, 128))
        total = part if total is None else total + part
    query_g[...] = total
    full = full_query(query_t, query_o, side).astype(BF16)
    grad_ref[0] = jnp.zeros((CELLS, 128), F32)
    grad_ref[bands + 1] = jnp.zeros((CELLS, 128), F32)
    turned_c[...] = conv_c[...].T
    turned_f[...] = conv_f[...].T
    before.advance()
    swaps[0].wait()
    here = pl.ds(1 - side, bands + 1)
    for load in loads[7:]:
        load.wait()
    grad_ref[here, 0:COARSE] = own[:, 0:COARSE] + recv[:, 0:COARSE].astype(F32)
    lane = lax.broadcasted_iota(jnp.int32, (1, 1, 128), 2)

    def tap_sum(values, grads):
        return fold_rows(values * grads)

    def reduce_back(pair, red, conv, gain, shifts, kv, small, kv_g):
        hat, inverse = norm_hat(red[...])
        normed = hat * gain[...] + shifts[1:2, :]
        cdf, bell = gauss(normed)
        active = (normed * cdf).astype(BF16)
        kv_g[...] = dot_in(active, pair)
        small[9:10, :] = jnp.sum(pair.astype(F32), axis=0, keepdims=True)
        grad = dot_t(pair, kv) * gelu_slope(normed, cdf, bell)
        small[11:12, :] = jnp.sum(grad * hat, axis=0, keepdims=True)
        small[12:13, :] = jnp.sum(grad, axis=0, keepdims=True)
        dc = norm_back(grad * gain[...], hat, inverse).astype(BF16)
        small[13:14, :] = jnp.sum(dc.astype(F32), axis=0, keepdims=True)
        return dc

    small_c[...] = jnp.zeros(small_c.shape, F32)
    small_f[...] = jnp.zeros(small_f.shape, F32)

    vals = val_ref[:, 0:COARSE, :]
    ext = grad_ref[:, 0:COARSE, :]
    ext = jnp.where(lane < 64, ext, ext.astype(BF16).astype(F32))
    mid = ext[1:-1]
    near = (by_band(vals[:-2], above), vals[1:-1], by_band(vals[2:], below))
    for a in range(3):
        for b in range(3):
            moved = near[a] if b == 1 else roll_cells(near[a], 1 - b)
            small_c[3 * a + b : 3 * a + b + 1, :] = jnp.sum(
                tap_sum(moved, mid), axis=0, keepdims=True
            )
    small_c[10:11, :] = jnp.sum(mid.reshape(-1, 128), axis=0, keepdims=True)
    pair = mid + depthwise_coarse(ext, above, below, taps_c, flip=True)
    pair = jnp.where(cell_valid(pair.shape, 1), pair, 0.0)
    pair = pair.reshape(bands * COARSE, 128).astype(BF16)
    dc_c = reduce_back(pair, red_c, conv_c, gain_c, shifts_c, kv_c[...], small_c, kv_c_g)
    for i in range(16):
        part = slice(i * 128, (i + 1) * 128)
        conv_c_g[part, :] = dot(xt[i], dc_c)

    conv.advance(1, shared_pieces(0, CONV, late_rows))
    before.advance()
    swaps[1].wait()
    grad_ref[here, COARSE:CELLS] = own[:, COARSE:CELLS] + recv[:, COARSE:CELLS].astype(F32)
    vals = val_ref[:, COARSE:CELLS, :]
    ext = grad_ref[:, COARSE:CELLS, :]
    ext = jnp.where(lane >= 64, ext, ext.astype(BF16).astype(F32))
    rows = depthwise_fine(ext, above, below, taps_f, flip=True)
    near = fine_rows(vals, above, below)
    mids = fine_rows(ext, above, below)[1]
    for a in range(3):
        for b in range(3):
            total = jnp.zeros((8, 128), F32)
            for row in range(2):
                even, odd = near[a][row][:, 0], near[a][row][:, 1]
                grad_even, grad_odd = mids[row][:, 0], mids[row][:, 1]
                if b == 0:
                    moved = (roll_cells(odd, 1), even)
                elif b == 1:
                    moved = (even, odd)
                else:
                    moved = (odd, roll_cells(even, -1))
                total = total + tap_sum(moved[0], grad_even) + tap_sum(moved[1], grad_odd)
            small_f[3 * a + b : 3 * a + b + 1, :] = jnp.sum(total, axis=0, keepdims=True)
    small_f[10:11, :] = jnp.sum(ext[1:-1].reshape(-1, 128), axis=0, keepdims=True)
    valid = cell_valid((bands, 16, 128), 1)
    blocks = []
    for row in range(2):
        for column in range(2):
            block = jnp.where(valid, mids[row][:, column] + rows[row][column], 0.0)
            blocks.append(block.astype(BF16).reshape(bands, 1, 16, 128))
    pair = jnp.concatenate(blocks, axis=1).reshape(bands * FINE, 128)
    conv.advance()
    dc_f = reduce_back(pair, red_f, conv_f, gain_f, shifts_f, kv_f_sw, small_f, kv_f_g)
    cells_f = [
        dc_f.reshape(bands, 4, 16, 128)[:, i].reshape(bands * 16, 128) for i in range(4)
    ]
    for i in range(4):
        part = slice(i * 128, (i + 1) * 128)
        total = None
        for row in range(2):
            for column in range(2):
                product = dot(xt[fine_slot(i, row, column)], cells_f[2 * row + column])
                total = product if total is None else total + product
        conv_f_g[part, :] = total
    rest.advance(1, shared_pieces(4 * CONV, REST, later_rows))
    conv.advance()
    before.advance()
    for part in range(4):
        for row in range(2):
            for column in range(2):
                slot = fine_slot(part, row, column)
                left = [slot_grads[:, slot].reshape(bands * 16, 128), dc_c, cells_f[2 * row + column]]
                right = [full, turned_c[:, slot * 128 : slot * 128 + 128]]
                right.append(turned_f[:, part * 128 : part * 128 + 128])
                back = dot(jnp.concatenate(left, axis=1), jnp.concatenate(right, axis=0))
                dxn[:, 16 * slot : 16 * slot + 16, :] = back.reshape(bands, 16, 128)
    front_g[...] = jnp.zeros(front_g.shape, F32)
    sums = jnp.zeros((8, 128), F32)
    along = jnp.zeros((8, 128), F32)
    for band in range(bands):
        grad = dxn[band]
        sums = sums + fold_rows(grad)
        along = along + fold_rows(grad * hat_ref[band].astype(F32))
    front_g[0:1, :] = jnp.sum(along, axis=0, keepdims=True)
    front_g[1:2, :] = jnp.sum(sums, axis=0, keepdims=True)

    small_phase(0)
    place = from_slots()

    def one_band(band):
        at = slice(band * BAND, (band + 1) * BAND)
        back = norm_back(dxn[band] * gains[0:1, :], hat_ref[band].astype(F32), 1.0)
        tok_grad[at, :] = dx1[at, :] + dot(place, back.astype(BF16)) * inv[at, :]

    began = len(before.left) + 1
    done = 0
    total = max(len(rest.left) + 1 + len(gather.left), began + len(gather_split.left))
    for number in range(1, total + 1):
        while done < bands and done * total < number * bands:
            one_band(done)
            done += 1
        if rest.left:
            rest.advance()
            conv.advance()
        elif number + len(gather.left) == total:
            conv.advance(len(conv.left))
            gather.begin([conv.finish(), rest.finish()])
        else:
            gather.advance()
        if before.left:
            before.advance()
        elif number == began:
            gather_split.begin([before.finish()])
        elif gather_split.left:
            gather_split.advance()
        if number <= len(order):
            small_phase(number)


def shared_rows(start, count):
    done = 0
    while done < count:
        group = 0 if start + done < 4 * CONV else 1
        if group == 0:
            quarter, row = divmod(start + done, CONV)
            size = min(count - done, CONV - row)
        else:
            quarter, row = divmod(start + done - 4 * CONV, REST)
            size = min(count - done, REST - row)
        yield group, quarter % 2, quarter // 2, row, done, size
        done += size


def unpack_kernel(
    levels,     early, joint, little, tok_grad,
    tok_grad_out, gains, shifts, query, conv_c, gain_c, shifts_c, kv_c, taps_c, conv_f, gain_f, shifts_f, kv_f,
    taps_f, proj, hidden, fc1, depth, fc2,
):
    tok_grad_out[...] = tok_grad[...]

    unpack_grads(
        levels, early, joint, little, gains, shifts, query, conv_c, gain_c, shifts_c, kv_c, taps_c,
        conv_f, gain_f, shifts_f, kv_f, taps_f, proj, hidden, fc1, depth, fc2,
    )


def unpack_grads(
    levels, early, joint, little,
    gains, shifts, query, conv_c, gain_c, shifts_c, kv_c, taps_c, conv_f, gain_f, shifts_f, kv_f,
    taps_f, proj, hidden, fc1, depth, fc2,
):
    side = lax.axis_index("heads")
    half = query.shape[0]
    first = group_size(levels, CONV) // joint.shape[2]
    spans = (slice(0, first), slice(first, joint.shape[3]))

    def quarter_rows(group, core, h):
        ref, rows = (early, slice(None)) if group == 2 else (joint, spans[group])
        return ref[core, h, :, rows, :].reshape(-1, 128)


    def rows_of(start, count):
        pieces = [
            quarter_rows(group, core, h)[at : at + size].astype(F32)
            for group, core, h, at, _, size in shared_rows(start, count)
        ]
        return pieces[0] if len(pieces) == 1 else jnp.concatenate(pieces, axis=0)

    start = 0
    for ref in (conv_c, conv_f, kv_c):
        count = ref.shape[0]
        for group, core, h, at, offset, size in shared_rows(start, count):
            ref[offset : offset + size, :] = quarter_rows(group, core, h)[at : at + size].astype(F32)
        start += count
    kv_f[...] = swap_lanes(rows_of(start, 128))
    both = rows_of(start + 128, 128)
    query[...] = jnp.where(side == 0, both[:, :half], both[:, half:]).T
    proj[...] = rows_of(start + 256, 128)
    small = little[...]
    coarse, fine, front, mid = small[0:16], small[16:32], small[32:40], small[40:48]
    taps_c[...] = coarse[0:9, half:]
    taps_f[...] = fine[0:9, :half]
    gain_c[...] = coarse[11:12]
    gain_f[...] = fine[11:12]
    shifts_c[0:1, :] = coarse[13:14]
    shifts_c[1:2, :] = coarse[12:13]
    shifts_c[2:3, :] = jnp.concatenate([coarse[9:10, half:], coarse[10:11, half:]], axis=1)
    shifts_f[0:1, :] = fine[13:14]
    shifts_f[1:2, :] = fine[12:13]
    shifts_f[2:3, :] = jnp.concatenate([fine[9:10, :half], fine[10:11, :half]], axis=1)
    gains[0:1, :] = front[0:1]
    gains[1:2, :] = mid[0:1]
    shifts[0:1, :] = front[1:2]
    shifts[1:2, :] = mid[2:3]
    shifts[2:3, :] = mid[1:2]
    shifts[3:4, :] = mid[3:4]
    for core in range(2):
        split = quarter_rows(2, core, side)
        for i in range(2):
            lanes = slice(core * STEP + i * 128, core * STEP + i * 128 + 128)
            fc1[:, lanes] = split[i * 128 : i * 128 + 128].astype(F32)
            block = split[512 + 16 * i : 528 + 16 * i].astype(F32)
            depth[:, lanes] = block[0:9]
            hidden[:, lanes] = block[9:11]
        fc2[core * STEP : core * STEP + STEP, :] = split[256:512].astype(F32)


SMEM = pl.BlockSpec(memory_space=pltpu.SMEM)
VMEM = pl.BlockSpec(memory_space=pltpu.VMEM)
HBM = pl.BlockSpec(memory_space=pl.ANY)


def shape(dims, kind=F32):
    return jax.ShapeDtypeStruct(dims, kind)


def params(limit=56):
    return pltpu.CompilerParams(vmem_limit_bytes=limit * MIB)


def sending(number, limit=56):
    return pltpu.CompilerParams(
        vmem_limit_bytes=limit * MIB, collective_id=number, has_side_effects=True
    )


def per_device(
    size, tokens, image_bands, cotangent, front_gains, front_shifts, query_w, coarse_conv,
    coarse_gain, coarse_shifts, coarse_kv, coarse_taps, fine_conv, fine_gain, fine_shifts, fine_kv,
    fine_taps, proj_w, hidden_shifts, fc1_w, depth_taps, fc2_w,
):
    count = tokens.shape[0]
    rows = count // W
    bands = count // BAND
    total = 2 * bands
    halo = 2 * W
    half = coarse_kv.shape[1] // 2
    mine = fc1_w.shape[1]
    hidden = 2 * mine
    gain_c, gain_f = coarse_gain[None], fine_gain[None]
    semaphores = pltpu.SemaphoreType.DMA
    levels = size.bit_length() - 1
    query_t = query_w.T

    (
        table, meta, xn, hat, inverse, red_c, red_f, slab, other, query_o,
    ) = pl.pallas_call(
        front_kernel,
        out_shape=(
            shape((3, 32), jnp.int32),
            shape((3, total, 8, 128)),
            shape((bands, SLOTS, 128), BF16),
            shape((bands, SLOTS, 128), BF16),
            shape((count, 128)),
            shape((bands * COARSE, 128)),
            shape((bands * FINE, 128)),
            shape((bands, CELLS, 128)),
            shape((bands, CELLS, 128), BF16),
            shape(query_t.shape, BF16),
        ),
        in_specs=[SMEM] + [VMEM] * 12,
        out_specs=[SMEM] + [VMEM] * 9,
        scratch_shapes=[pltpu.VMEM((bands, CELLS, 128), BF16), semaphores((8,)), semaphores((8,))],
        compiler_params=sending(1),
        name="front",
    )(
        image_bands, tokens, front_gains, front_shifts, coarse_conv, gain_c, coarse_shifts,
        coarse_kv, fine_conv, gain_f, fine_shifts, fine_kv,
        query_t,
    )

    each = 4 if bands % 4 == 0 else 2
    some_bands = pl.BlockSpec((each * BAND, 128), lambda i: (i, 0))
    some_slots = pl.BlockSpec((each, SLOTS, 128), lambda i: (i, 0, 0))
    two_slots = pl.BlockSpec((2, SLOTS, 128), lambda i: (i, 0, 0))
    (
        x1, xm, heads_out, out_t, lse, key_c, key_f, val_c, val_f, fc1_o, fc2_o, depth_o, hidden_o,
        cot_o,
    ) = pl.pallas_call(
        attend_kernel,
        grid=(bands // each,),
        out_shape=(
            shape((count, 128)),
            shape((count, 128), BF16),
            shape((count, 128), BF16),
            shape((bands, 128, SLOTS)),
            shape((bands, 8, SLOTS)),
            shape((total, COARSE, 128), BF16),
            shape((total, PACKED, 128)),
            shape((total, COARSE, 128), BF16),
            shape((total, PACKED, 128)),
            shape(fc1_w.shape, BF16),
            shape(fc2_w.shape, BF16),
            shape(depth_taps.shape),
            shape(hidden_shifts.shape),
            shape((halo, 128), BF16),
        ),
        in_specs=[SMEM] + [VMEM] * 7 + [some_slots, some_bands] + [VMEM] * 5 + [HBM] * 5,
        out_specs=[
            some_bands,
            some_bands,
            some_bands,
            pl.BlockSpec((each, 128, SLOTS), lambda i: (i, 0, 0)),
            pl.BlockSpec((each, 8, SLOTS), lambda i: (i, 0, 0)),
        ]
        + [VMEM] * 4
        + [HBM] * 5,
        scratch_shapes=[
            pltpu.VMEM((total + 2, CELLS, 128), F32),
            pltpu.VMEM((128, 128), BF16),
            pltpu.VMEM((BAND, SLOTS), BF16),
            semaphores((5,)),
            semaphores((5,)),
        ],
        compiler_params=sending(4),
        name="attend",
    )(
        table, slab, other, meta, coarse_taps, fine_taps, coarse_shifts, fine_shifts, xn, tokens,
        query_t, query_o, proj_w, front_gains, front_shifts, fc1_w, fc2_w, depth_taps,
        hidden_shifts, cotangent,
    )

    extra = 64
    output, dx1, out_grad, split_g, mid_g = pl.pallas_call(
        hidden_kernel,
        out_shape=(
            shape((count, 128), BF16),
            shape((count, 128)),
            shape((bands, SLOTS, 128), BF16),
            shape((2, 2, SPLIT, 128)),
            shape((136, 128)),
        ),
        in_specs=[SMEM, HBM] + [VMEM] * 3 + [HBM] + [VMEM] * 11,
        out_specs=[VMEM] * 5,
        scratch_shapes=[
            pltpu.VMEM((count + 2 * halo, 128), BF16),
            pltpu.VMEM((halo, 128), BF16),
            pltpu.VMEM((8, rows + 4, W, 128), F32),
            pltpu.VMEM((count + extra, WIDE), BF16),
            pltpu.VMEM((KEPT, count), BF16),
            pltpu.VMEM((WIDE, hidden), BF16),
            pltpu.VMEM((hidden, TAPS * 128), BF16),
            pltpu.VMEM((16, hidden), F32),
            pltpu.VMEM((16, hidden), F32),
            pltpu.VMEM((128, hidden), BF16),
            pltpu.VMEM((128, hidden), BF16),
            pltpu.VMEM((count + extra, 128), BF16),
            pltpu.VMEM((128, count), BF16),
            pltpu.VMEM((count, hidden), BF16),
            pltpu.VMEM((count + extra, hidden), BF16),
            pltpu.VMEM((KEPT, SPAN), F32),
            pltpu.VMEM((count, 128), F32),
            pltpu.VMEM((count, 128), F32),
            pltpu.VMEM((count, 128), F32),
            pltpu.VMEM((count, 128), BF16),
            semaphores(()),
            semaphores(()),
            semaphores((2,)),
        ],
        compiler_params=sending(2, 63),
        name="hidden",
    )(
        table, x1, xm, cotangent, cot_o, heads_out, fc1_w, fc1_o, fc2_w, fc2_o, depth_taps, depth_o,
        hidden_shifts, hidden_o, front_gains, front_shifts, proj_w,
    )

    dq, grad_own, grad_send, output = pl.pallas_call(
        attend_back_kernel,
        grid=(bands // 2,),
        out_shape=(
            shape((bands, SLOTS, 128), BF16),
            shape((bands + 1, CELLS, 128)),
            shape((bands + 1, CELLS, 128), BF16),
            shape((count, 128), BF16),
        ),
        in_specs=[SMEM]
        + [VMEM] * 4
        + [
            two_slots,
            VMEM,
            VMEM,
            two_slots,
            pl.BlockSpec((2, 128, SLOTS), lambda i: (i, 0, 0)),
            pl.BlockSpec((2, 8, SLOTS), lambda i: (i, 0, 0)),
            pl.BlockSpec((2 * BAND, 128), lambda i: (i, 0)),
        ],
        out_specs=[two_slots, VMEM, VMEM, pl.BlockSpec((2 * BAND, 128), lambda i: (i, 0))],
        scratch_shapes=[
            pltpu.VMEM((total, COARSE, 128), F32),
            pltpu.VMEM((total, FINE, 128), F32),
            pltpu.VMEM((128, 128), BF16),
            pltpu.VMEM((2, 64, MAX_BANDS * COARSE), BF16),
            pltpu.VMEM((2, 2, 64, HALVES[0][1] * PACKED), BF16),
            pltpu.VMEM((2, MAX_BANDS * PACKED, 128), BF16),
            pltpu.VMEM((2, MAX_BANDS * PACKED, 128), BF16),
            pltpu.SMEM((2,), jnp.int32),
        ],
        compiler_params=params(),
        name="attend_back",
    )(table, key_c, key_f, val_c, val_f, xn, query_t, query_o, out_grad, out_t, lse, output)

    peers = sum(2 ** len(dims) - 1 for dims in stages(levels, True))
    links = group_links(levels, False) + 4 * group_links(levels, True) + 2 * len(stages(levels, True)) + 1
    early_rows, late_rows, later_rows = (group_size(levels, part) for part in (SPLIT, CONV, REST))
    pieces = 2 ** (levels - 1)
    joint_rows = (late_rows + later_rows) // pieces
    tokens_grad, early, joint, little = pl.pallas_call(
        functools.partial(tail_kernel, levels),
        out_shape=(
            shape((count, 128)),
            shape((2, 2, pieces, early_rows // pieces, 128), BF16),
            shape((2, 2, pieces, joint_rows, 128), BF16),
            shape((SMALL, 128)),
        ),
        in_specs=[HBM] * 3 + [VMEM, HBM] + [VMEM] * 2 + [HBM] * 3 + [VMEM] * 2 + [HBM] * 2
        + [VMEM] + ([HBM] * 2 + [VMEM] * 4) * 2,
        out_specs=[VMEM] * 4,
        scratch_shapes=[
            pltpu.VMEM((4 * QUARTER, 128), F32),
            pltpu.VMEM((len(stages(levels, True)), SMALL, 128), F32),
            pltpu.VMEM((peers, SMALL, 128), F32),
            semaphores((2, peers)),
            pltpu.VMEM((bands + 1, CELLS, 128), BF16),
            pltpu.VMEM((bands + 2, CELLS, 128), F32),
            pltpu.VMEM((bands + 2, CELLS, 128), F32),
            pltpu.VMEM((bands, SLOTS, 128), F32),
            semaphores((2,)),
            semaphores((2,)),
            semaphores((links,)),
            semaphores((links,)),
            pltpu.VMEM((128, coarse_conv.shape[0]), BF16),
            pltpu.VMEM((128, fine_conv.shape[0]), BF16),
            pltpu.VMEM((count, 128), F32),
            pltpu.VMEM((count, 128), F32),
            pltpu.VMEM((bands, SLOTS, 128), BF16),
            pltpu.VMEM(grad_own.shape, F32),
            pltpu.VMEM(split_g.shape, F32),
            pltpu.VMEM(slab.shape, F32),
            pltpu.VMEM(xn.shape, BF16),
            pltpu.VMEM(dq.shape, BF16),
            pltpu.VMEM(red_c.shape, F32),
            pltpu.VMEM(coarse_conv.shape, BF16),
            pltpu.VMEM(red_f.shape, F32),
            pltpu.VMEM(fine_conv.shape, BF16),
            pltpu.VMEM((16, 128, bands * 16), BF16),
            semaphores((12,)),
        ]
        + group_scratch(levels, False, early_rows)
        + group_scratch(levels, True, late_rows)
        + group_scratch(levels, True, later_rows),
        compiler_params=sending(0),
        name="tail",
    )(
        grad_own, grad_send, split_g, mid_g, slab, other, meta, xn, hat, dq, query_t, query_o, dx1,
        inverse, front_gains,
        red_c, coarse_conv, gain_c, coarse_shifts, coarse_kv, coarse_taps,
        red_f, fine_conv, gain_f, fine_shifts, fine_kv, fine_taps,
    )
    grads = pl.pallas_call(
        functools.partial(unpack_kernel, levels),
        out_shape=(
            shape((count, 128)),
            shape((2, 128)),
            shape((4, 128)),
            shape((half, 128)),
            shape(coarse_conv.shape),
            shape((1, 128)),
            shape((3, 128)),
            shape((128, 128)),
            shape((9, half)),
            shape(fine_conv.shape),
            shape((1, 128)),
            shape((3, 128)),
            shape((128, 128)),
            shape((9, half)),
            shape((128, 128)),
            shape((2, mine)),
            shape((128, mine)),
            shape((9, mine)),
            shape((mine, 128)),
        ),
        in_specs=[VMEM] * 4,
        out_specs=[VMEM] * 19,
        compiler_params=params(),
        name="unpack",
    )(early, joint, little, tokens_grad)
    grads = [output] + list(grads)
    grads[4] = grads[4].T
    for at in (6, 11):
        grads[at] = grads[at].reshape(128)
    return tuple(grads)


def solution(mesh):
    tokens = P(("batch", "heads"), None)
    columns = P(None, "heads")
    return jax.shard_map(
        functools.partial(per_device, mesh.shape["batch"]),
        mesh=mesh,
        in_specs=(tokens, P("batch", None), tokens, P(), P(), columns)
        + (P(),) * 11
        + (columns, columns, columns, P("heads", None)),
        out_specs=(tokens, tokens, P(), P(), columns)
        + (P(),) * 11
        + (columns, columns, columns, P("heads", None)),
        check_vma=False,
    )
```

```python
import functools

import jax
import jax.numpy as jnp
from jax import lax
from jax.experimental import pallas as pl
from jax.experimental.pallas import tpu as pltpu
from jax.sharding import PartitionSpec as P

W = 56
BAND = 4 * W
SLOTS = 256
COARSE = 16
FINE = 64
CELLS = COARSE + FINE
MAX_BANDS = 14
EPS = 1e-06
F32 = jnp.float32
BF16 = jnp.bfloat16
SCALE = 32**-0.5
LOG2E = 1.4426950408889634
ROOT = 0.7071067811865476
EXP_SCALE = SCALE * LOG2E
BIG = -1e9
MIB = 1024 * 1024
STEP = 256
SPAN = 512
MESH = pl.DeviceIdType.MESH
TAPS = 9
KEPT = TAPS * 128 + 16
WIDE = (TAPS + 1) * 128
QUARTER = 768
CONV = 512
REST = QUARTER - CONV
SMALL = 48
SPLIT = 544


def dot(left, right):
    return jnp.dot(left, right, preferred_element_type=F32)


def dot_t(left, right):
    return lax.dot_general(left, right, (((1,), (1,)), ((), ())), preferred_element_type=F32)


def dot_in(left, right):
    return lax.dot_general(left, right, (((0,), (0,)), ((), ())), preferred_element_type=F32)


def gauss(values):
    return 0.5 + 0.5 * lax.erf(values * ROOT), jnp.exp2(values * values * (-0.5 * LOG2E))


def gelu_slope(values, cdf, bell):
    return cdf + values * bell * 0.3989422804014327


def fold_rows(values):
    wide = jnp.sum(values.reshape(-1, 64, 128), axis=0)
    return jnp.sum(wide.reshape(8, 8, 128), axis=0)


def norm_hat(values):
    centred = values - jnp.mean(values, axis=-1, keepdims=True)
    inverse = lax.rsqrt(jnp.mean(centred * centred, axis=-1, keepdims=True) + EPS)
    return centred * inverse, inverse


def norm_back(grad_scaled, hat, inverse):
    centre = jnp.mean(grad_scaled, axis=-1, keepdims=True)
    along = jnp.mean(grad_scaled * hat, axis=-1, keepdims=True)
    return inverse * (grad_scaled - centre - hat * along)


def slot_map(slot, token):
    a, b, c = slot >> 6, (slot >> 4) & 3, slot & 15
    hit = (token == a * W + 4 * c + b) & (c < 14)
    return jnp.where(hit, 1.0, 0.0).astype(BF16)


def to_slots():
    shape = (SLOTS, BAND)
    return slot_map(
        lax.broadcasted_iota(jnp.int32, shape, 0), lax.broadcasted_iota(jnp.int32, shape, 1)
    )


def from_slots():
    shape = (BAND, SLOTS)
    return slot_map(
        lax.broadcasted_iota(jnp.int32, shape, 1), lax.broadcasted_iota(jnp.int32, shape, 0)
    )


def cell_valid(shape, axis):
    return (lax.broadcasted_iota(jnp.int32, shape, axis) & 15) < 14


def roll_cells(values, step):
    lead = values.shape[:-2]
    flat = values.reshape(-1, values.shape[-1])
    flat = pltpu.roll(flat, step % flat.shape[0], 0)
    return flat.reshape(lead + values.shape[-2:])


def by_band(values, mask):
    count = values.shape[0]
    wide = values.reshape(count, -1, 8, 128) * mask.reshape(count, 1, 8, 128)
    return wide.reshape(values.shape)


def row_taps(taps, flip):
    order = [8 - i for i in range(9)] if flip else list(range(9))
    return [taps[i : i + 1, :] for i in order]


def depthwise_coarse(ext, above, below, taps, flip=False):
    t = row_taps(taps, flip)
    up, mid, down = by_band(ext[:-2], above), ext[1:-1], by_band(ext[2:], below)
    left, centre, right = (up * t[b] + mid * t[3 + b] + down * t[6 + b] for b in range(3))
    return centre + roll_cells(left, 1) + roll_cells(right, -1)


def fine_rows(ext, above, below):
    bands = ext.shape[0] - 2
    grid = ext.reshape(bands + 2, 2, 2, 16, 128)
    first, second = grid[:, 0], grid[:, 1]
    up = (by_band(second[:-2], above), first[1:-1])
    mid = (first[1:-1], second[1:-1])
    down = (second[1:-1], by_band(first[2:], below))
    return up, mid, down


def depthwise_fine(ext, above, below, taps, flip=False):
    t = row_taps(taps, flip)
    ups, mids, downs = fine_rows(ext, above, below)
    rows = []
    for up, mid, down in zip(ups, mids, downs):
        left, centre, right = (up * t[b] + mid * t[3 + b] + down * t[6 + b] for b in range(3))
        even = centre[:, 0] + roll_cells(left[:, 1], 1) + right[:, 1]
        odd = centre[:, 1] + left[:, 0] + roll_cells(right[:, 0], -1)
        rows.append((even, odd))
    return rows


def greet(*peers):
    barrier = pltpu.get_barrier_semaphore()
    for peer in peers:
        pl.semaphore_signal(barrier, inc=1, device_id=peer, device_id_type=MESH)


def met(count):
    pl.semaphore_wait(pltpu.get_barrier_semaphore(), count)


def fetch(pairs, sems):
    loads = [pltpu.make_async_copy(source, target, sems.at[i]) for i, (source, target) in enumerate(pairs)]
    for load in loads:
        load.start()
    return loads


def link(source, target, send_sem, recv_sem, peer):
    return pltpu.make_async_remote_copy(
        src_ref=source,
        dst_ref=target,
        send_sem=send_sem,
        recv_sem=recv_sem,
        device_id=peer,
        device_id_type=MESH,
    )


def remote(source, target, send_sem, recv_sem, peer):
    made = link(source, target, send_sem, recv_sem, peer)
    made.start()
    return made


def across():
    return (lax.axis_index("batch"), 1 - lax.axis_index("heads"))


def swap_lanes(values):
    half = values.shape[1] // 2
    return jnp.concatenate([values[:, half:], values[:, :half]], axis=1)


def keep_lanes(values, upper):
    lane = lax.broadcasted_iota(jnp.int32, values.shape, 1)
    return jnp.where((lane >= 64) if upper else (lane < 64), values, 0.0)


def pad_taps(taps, upper):
    gap = jnp.zeros(taps.shape, F32)
    return jnp.concatenate([gap, taps] if upper else [taps, gap], axis=1)


def band_tables(heights, table, meta, total):
    count = heights.shape[1]
    number = jnp.int32(0)
    start = jnp.int32(0)
    end = heights[0, 0]
    last = jnp.int32(-2)
    images, sames = [], []
    for band in range(total):
        passed = band >= end
        number = jnp.where(passed, number + 1, number)
        start = jnp.where(passed, end, start)
        grown = heights[0, jnp.minimum(number, count - 1)]
        grown = jnp.where(number < count, grown, 0)
        end = jnp.where(passed, end + grown, end)
        image = jnp.where(band < end, number, -1)
        same = jnp.where(image == last, 1, 0)
        last = image
        table[0, band] = image
        table[1, band] = jnp.minimum(start, total - MAX_BANDS)
        table[2, band] = same
        images.append(image)
        sames.append(same)
    for band in range(total, table.shape[1]):
        for row in range(3):
            table[row, band] = jnp.int32(0)
    sames.append(jnp.int32(0))
    for band in range(total):
        for row, value in enumerate((sames[band], sames[band + 1], images[band])):
            meta[row, band] = jnp.full((8, 128), value.astype(F32), F32)


def front_kernel(
    heights, tok, gains, shifts, conv_c, gain_c, shifts_c, kv_c, conv_f, gain_f, shifts_f, kv_f,
    query_t,
    table, meta, xn_out, hat_out, inv_out, red_c, red_f, slab, other, query_o,
    send, send_sems, recv_sems,
):
    bands = xn_out.shape[0]
    peer = across()
    greet(peer)
    copies = []

    def give(source, target):
        at = len(copies)
        copies.append(remote(source, target, send_sems.at[at], recv_sems.at[at], peer))

    place = to_slots()

    def norm_bands(first, count):
        rows = slice(first * BAND, (first + count) * BAND)
        hat, inverse = norm_hat(tok[rows, :].astype(F32))
        inv_out[rows, :] = jnp.broadcast_to(inverse, hat.shape)
        normed = (hat * gains[0:1, :] + shifts[0:1, :]).astype(BF16)
        sides = jnp.concatenate([normed, hat.astype(BF16)], axis=1)
        for band in range(count):
            both = dot(place, sides[band * BAND : (band + 1) * BAND]).astype(BF16)
            xn_out[first + band] = both[:, :128]
            hat_out[first + band] = both[:, 128:]

    def reduce(patches, conv, gain, shift, kv, out, at):
        red = dot(patches, conv) + shift[0:1, :]
        out[at : at + red.shape[0], :] = red
        hat, _ = norm_hat(red)
        normed = hat * gain[...] + shift[1:2, :]
        cdf, _ = gauss(normed)
        return dot((normed * cdf).astype(BF16), kv)

    kv_f_sw = swap_lanes(kv_f[...])
    part = bands // 2
    for first in (0, part):
        norm_bands(first, part)
        grid = xn_out[first : first + part].reshape(part, 16, 16, 128)
        patches = jnp.concatenate([fine_patch(grid, i) for i in range(4)], axis=1)
        pair = reduce(patches, conv_f[...], gain_f, shifts_f, kv_f_sw, red_f, first * FINE)
        pair = pair + keep_lanes(shifts_f[2:3, :], False)
        pair = jnp.where(cell_valid(pair.shape, 0), pair, 0.0).reshape(part, FINE, 128)
        slab[first : first + part, COARSE:CELLS, :] = pair
        send[first : first + part, COARSE:CELLS, :] = pair.astype(BF16)
        here = (pl.ds(first, part), pl.ds(COARSE, FINE))
        if first == 0:
            met(1)
        give(send.at[here], other.at[here])
        if first == 0:
            give(query_t, query_o)
    grid = xn_out[...].reshape(bands, 16, 16, 128)
    patches = jnp.concatenate([grid[:, i].reshape(bands * 16, 128) for i in range(16)], axis=1)
    pair = reduce(patches, conv_c[...], gain_c, shifts_c, kv_c[...], red_c, 0)
    pair = pair + keep_lanes(swap_lanes(shifts_c[2:3, :]), True)
    pair = jnp.where(cell_valid(pair.shape, 0), pair, 0.0).reshape(bands, COARSE, 128)
    slab[:, 0:COARSE, :] = pair
    send[:, 0:COARSE, :] = pair.astype(BF16)
    here = pl.ds(0, COARSE)
    give(send.at[:, here], other.at[:, here])
    band_tables(heights, table, meta, 2 * bands)
    for made in copies:
        made.wait()


def fine_slot(part, row, column):
    return (2 * row + (part >> 1)) * 4 + 2 * column + (part & 1)


def fine_patch(grid, part):
    bands = grid.shape[0]
    blocks = [
        grid[:, fine_slot(part, row, column)].reshape(bands, 1, 16, 128)
        for row in range(2)
        for column in range(2)
    ]
    return jnp.concatenate(blocks, axis=1).reshape(bands * FINE, 128)


def head_lanes(values, head):
    lane = lax.broadcasted_iota(jnp.int32, values.shape, 1)
    return jnp.where((lane >> 5) == head, values, jnp.zeros((), BF16))


def head_rows(values, head):
    row = lax.broadcasted_iota(jnp.int32, values.shape, 0)
    return jnp.where((row >> 5) == head, values, jnp.zeros((), BF16))


def score_rows(query_t, head, image, fine):
    row = lax.broadcasted_iota(jnp.int32, query_t.shape, 0)
    tag = row if fine else row - 64
    fill = jnp.where((tag >= 0) & (tag <= NOBODY) & (tag != image), BIG, 0.0).astype(BF16)
    return jnp.where((row >> 5) == head, query_t, fill)


def with_offset(rows, at, offset):
    start = at // 16 * 16
    block = rows[start : start + 16]
    row = lax.broadcasted_iota(jnp.int32, block.shape, 0)
    for i in range(3):
        term = offset.astype(BF16)
        block = jnp.where(row == at - start + i, term, block)
        offset = offset - term.astype(F32)
    parts = [rows[:start]] if start else []
    return jnp.concatenate(parts + [block, rows[start + 16 :]], axis=0)


def full_query(query_t, query_o, side):
    own, other = query_t[...].astype(F32), query_o[...].astype(F32)
    return jnp.where(
        side == 0,
        jnp.concatenate([own, other], axis=0),
        jnp.concatenate([other, own], axis=0),
    )


def window(ref, first):
    part = ref[pl.ds(first, MAX_BANDS)]
    return part.reshape(-1, 128).astype(BF16)


PACKED = 56
CHUNKS = ((0, 224), (224, 224), (448, 224), (672, 112))
HALVES = ((0, 8), (8, 6))
NOBODY = 32
ONES = 40


def tree_max(values):
    count = values.shape[0]
    while count % 16 == 0:
        count //= 2
        values = jnp.maximum(values[:count], values[count:])
    return jnp.max(values, axis=0, keepdims=True)


def attend_kernel(
    table, slab, other, meta, taps_c, taps_f, shifts_c, shifts_f, xn, tok, query_t, query_o, proj_w,
    gains, shifts, fc1, fc2, depth, hidden, cot,
    x1_out, xm_out, o_out, ot_out, lse_out, key_c, key_f, val_c, val_f, fc1_o, fc2_o, depth_o,
    hidden_o, cot_o,
    grid_ref, query_ref, place_ref, send_sems, recv_sems,
):
    step = pl.program_id(0)
    bands = slab.shape[0]
    total = 2 * bands
    side = lax.axis_index("heads")
    peer = across()
    halo = 2 * W
    edge = pl.multiple_of((1 - side) * (cot.shape[0] - halo), 16)
    swaps = [
        link(source, target, send_sems.at[i], recv_sems.at[i], peer)
        for i, (source, target) in enumerate(
            (
                (cot.at[pl.ds(edge, halo)], cot_o),
                (depth, depth_o),
                (hidden, hidden_o),
                (fc1, fc1_o),
                (fc2, fc2_o),
            )
        )
    ]

    @pl.when(step == 0)
    def _():
        greet(peer)
        place_ref[...] = from_slots()
        query_ref[...] = full_query(query_t, query_o, side).T.astype(BF16)
        grid_ref[0] = jnp.zeros((CELLS, 128), F32)
        grid_ref[total + 1] = jnp.zeros((CELLS, 128), F32)
        grid_ref[pl.ds(1 + side * bands, bands)] = slab[...]
        grid_ref[pl.ds(1 + (1 - side) * bands, bands)] = other[...].astype(F32)
        above, below, image = meta[0], meta[1], meta[2]
        lane = lax.broadcasted_iota(jnp.int32, (total, 16, 128), 2).astype(F32)
        valid = cell_valid((total, 16, 128), 1)
        wide = jnp.broadcast_to(image.reshape(total, 1, 8, 128), (total, 2, 8, 128))
        wide = wide.reshape(total, 16, 128)
        mark = jnp.where(valid & (wide >= 0.0), wide, float(NOBODY))

        ext = grid_ref[:, 0:COARSE, :]
        own = ext[1:-1]
        local = keep_lanes(shifts_c[2:3, :], True)
        mixed = own + depthwise_coarse(ext, above, below, pad_taps(taps_c[...], True)) + local
        val_c[...] = jnp.where(lane < 3.0, 1.0, mixed).astype(BF16)
        place = lane - 64.0
        one = (place >= ONES) & (place < ONES + 3)
        tag = jnp.where((place == mark) | one, 1.0, 0.0)
        keys = jnp.where(lane < 64.0, own, tag)
        key_c[...] = keys.astype(BF16)

        ext = grid_ref[:, COARSE:CELLS, :]
        local = keep_lanes(swap_lanes(shifts_f[2:3, :]), False)
        rows = depthwise_fine(ext, above, below, pad_taps(taps_f[...], False))
        tag = jnp.where((lane == mark) | ((lane >= ONES) & (lane < ONES + 3)), 1.0, 0.0)
        one = (lane >= 64.0) & (lane < 67.0)
        for row in range(2):
            for column in range(2):
                at = (2 * row + column) * 16
                own = ext[1:-1, at : at + 16, :]
                mixed = own + rows[row][column] + local
                cell = (2 * row + column) * 14
                val_f[:, cell : cell + 14, :] = jnp.where(one, 1.0, mixed)[:, 0:14]
                keys = jnp.where(lane >= 64.0, own.astype(BF16).astype(F32), tag)
                key_f[:, cell : cell + 14, :] = keys[:, 0:14]
        met(1)
        for swap in swaps:
            swap.start()

    each = xn.shape[0]
    images = [table[0, side * bands + each * step + i] for i in range(each)]
    firsts = [table[1, side * bands + each * step + i] for i in range(each)]
    queries = [
        dot(xn[i], query_ref[...]).astype(BF16).astype(F32).T.astype(BF16) for i in range(each)
    ]
    turned, windows = {}, {}

    def score(unit):
        i, head, part = unit
        fine = head >= 2
        start, size = CHUNKS[part]
        rows = slice(start, start + size)
        if not head & 1:
            if part == 0:
                windows[i, fine] = [
                    window(ref, firsts[i]) for ref in ((key_f, val_f) if fine else (key_c, val_c))
                ]
            turned[i, fine, part] = windows[i, fine][1][rows].T
        keys = windows[i, fine][0][rows]
        return dot(keys, score_rows(queries[i], head, images[i], fine))

    outs = [[None] * 4 for _ in range(each)]
    mixed = {}
    lse_out[...] = jnp.zeros(lse_out.shape, F32)

    def mix(unit, scores):
        i, head, part = unit
        fine = head >= 2
        top = tree_max(scores) * EXP_SCALE
        expo = jnp.exp2(scores * EXP_SCALE - top).astype(BF16)
        row = 32 * (head & 1) + (0 if fine else 64)
        vals = turned[i, fine, part][row : row + 32]
        left = jnp.concatenate([vals, jnp.ones((16, CHUNKS[part][1]), BF16)], axis=0)
        done = mixed.setdefault((i, head), [])
        done.append((top, dot(left, expo)))
        if len(done) < (4 if fine else 1):
            return
        top = functools.reduce(jnp.maximum, [part_top for part_top, _ in done])
        total = None
        for part_top, value in done:
            value = value * jnp.exp2(part_top - top)
            total = value if total is None else total + value
        sums = total[32:33]
        lse_out[i, head : head + 1, :] = top + jnp.log2(sums)
        outs[i][head] = total[0:32] * (1.0 / sums)

    waiting = []
    for i in range(each):
        for head, parts in ((2, 4), (0, 1), (3, 4), (1, 1)):
            for part in range(parts):
                waiting.append(((i, head, part), score((i, head, part))))
                if len(waiting) > 6:
                    mix(*waiting.pop(0))
    for unit, scores in waiting:
        mix(unit, scores)
    place = place_ref[...]
    joined = []
    for i in range(each):
        live = jnp.where(images[i] >= 0, 1.0, 0.0)
        out_t = jnp.concatenate(outs[i], axis=0) * live
        ot_out[i] = out_t
        joined.append(dot(place, out_t.T.astype(BF16)).astype(BF16))
    heads_out = jnp.concatenate(joined, axis=0)
    o_out[...] = heads_out
    middle = tok[...].astype(F32) + dot(heads_out, proj_w[...]) + shifts[1:2, :]
    x1_out[...] = middle
    hat, _ = norm_hat(middle)
    xm_out[...] = (hat * gains[1:2, :] + shifts[2:3, :]).astype(BF16)

    @pl.when(step == pl.num_programs(0) - 1)
    def _():
        for swap in swaps:
            swap.wait()


def shift_right(values):
    column = lax.broadcasted_iota(jnp.int32, values.shape, 0)
    return jnp.where(column == 0, 0.0, pltpu.roll(values, 1, 0))


def shift_left(values):
    column = lax.broadcasted_iota(jnp.int32, values.shape, 0)
    return jnp.where(column == W - 1, 0.0, pltpu.roll(values, W - 1, 0))


def mask_lanes():
    lane = lax.broadcasted_iota(jnp.int32, (W, 128), 1)
    column = lax.broadcasted_iota(jnp.int32, (W, 128), 0)
    tap = jnp.where(lane < 32, lane & 15, 15)
    parts = []
    for a in range(3):
        hit = tap == 3 * a + 1
        hit = hit | ((tap == 3 * a) & (column > 0)) | ((tap == 3 * a + 2) & (column < W - 1))
        if a == 1:
            hit = hit | (tap == TAPS)
        parts.append(jnp.where(hit, 1.0, 0.0))
    return parts


def hidden_kernel(
    table, x1_in, xm, cot, cot_o, heads_in, fc1, fc1_o, fc2, fc2_o, depth, depth_o, hidden, hidden_o,
    gains, shifts, proj_w,
    out, dx1_out, do_out, split_g, mid_g,
    xm_ext, halo_ref, moved, wide, wide_t, weights, weights_t, taps, bias, base_ref, fc2_t, dy, dy_t, act, du,
    sums, dxm, out_acc, x1, heads_out, send_sem, recv_sem, load_sems,
):
    side = lax.axis_index("heads")
    peer = across()
    tokens = x1.shape[0]
    rows = tokens // W
    bands = tokens // BAND
    halo = 2 * W
    extra = wide.shape[0] - tokens
    mine = fc1.shape[1]
    width = 2 * mine
    halo_at = pl.multiple_of((1 - side) * (halo + tokens), 16)
    halo_row = 1 + (1 - side) * (rows + 1)
    greet(peer)
    loads = fetch(((x1_in, x1), (heads_in, heads_out)), load_sems)
    edge = pl.multiple_of((1 - side) * (tokens - halo), 16)
    swap = link(xm.at[pl.ds(edge, halo)], halo_ref, send_sem, recv_sem, peer)

    def live_band(band):
        return jnp.where(table[0, band] >= 0, 1.0, 0.0)

    def neighbour(row):
        place = side * rows - 2 + row
        band = jnp.maximum(place, 0) >> 2
        up = jnp.where((place & 3) == 0, table[2, band], 1)
        down = jnp.where((place & 3) == 3, table[2, band + 1], 1)
        return up.astype(F32), down.astype(F32)

    xm_ext[0:halo, :] = jnp.zeros((halo, 128), BF16)
    xm_ext[halo + tokens : tokens + 2 * halo, :] = jnp.zeros((halo, 128), BF16)
    xm_ext[halo : halo + tokens, :] = xm[...]
    for band in range(bands):
        at = slice(band * BAND, (band + 1) * BAND)
        dy[at, :] = (cot[at, :].astype(F32) * live_band(side * bands + band)).astype(BF16)
    tail = cot_o[...].astype(F32)
    tail = jnp.where(side == 0, tail[:W], tail[W:]) * live_band((1 - side) * bands + side * (bands - 1))
    tail = jnp.concatenate([tail, jnp.zeros((extra - W, 128), F32)], axis=0)
    dy[tokens : tokens + extra, :] = tail.astype(BF16)

    taps[...] = jnp.zeros(taps.shape, F32)
    bias[...] = jnp.zeros(bias.shape, F32)
    for part, (taps_ref, shift_ref, fc1_ref, fc2_ref) in enumerate(
        ((depth, hidden, fc1, fc2), (depth_o, hidden_o, fc1_o, fc2_o))
    ):
        lanes = slice(part * mine, part * mine + mine)
        taps[0:TAPS, lanes] = taps_ref[...]
        taps[TAPS : TAPS + 1, lanes] = shift_ref[0:1, :]
        bias[0:TAPS, lanes] = taps_ref[...] * shift_ref[0:1, :]
        bias[TAPS : TAPS + 1, lanes] = shift_ref[0:1, :] + shift_ref[1:2, :]
        fc2_t[:, lanes] = fc2_ref[...].T
        base_ref[:, lanes] = fc1_ref[...]
        base = fc1_ref[...].astype(F32)
        for k in range(TAPS):
            factor = taps_ref[k : k + 1, :] + (1.0 if k == 4 else 0.0)
            weights[k * 128 : k * 128 + 128, lanes] = (base * (factor * ROOT)).astype(BF16)
    scaled = bias[...] * ROOT
    high = scaled.astype(BF16)
    weights[TAPS * 128 : TAPS * 128 + 16, :] = high
    weights[TAPS * 128 + 16 : TAPS * 128 + 32, :] = (scaled - high.astype(F32)).astype(BF16)
    weights[TAPS * 128 + 32 : WIDE, :] = jnp.zeros((96, width), BF16)

    met(1)
    swap.start()

    def move_rows(pair, carry):
        both = xm_ext[pl.ds(pl.multiple_of(pair * halo, 16), halo), :].astype(F32)
        for i in range(2):
            row = both[W * i : W * i + W]
            moved[0, 2 * pair + i] = shift_right(row)
            moved[1, 2 * pair + i] = row
            moved[2, 2 * pair + i] = shift_left(row)
        return carry

    lax.fori_loop(1, rows // 2 + 1, move_rows, 0, unroll=2)
    swap.wait()
    xm_ext[pl.ds(halo_at, halo), :] = halo_ref[...]
    move_rows(0, 0)
    move_rows(rows // 2 + 1, 0)

    masks = mask_lanes()

    def gather_row(row, block):
        up, down = neighbour(row)
        if block == TAPS:
            return masks[0] * up + masks[1] + masks[2] * down
        a, b = divmod(block, 3)
        values = moved[b, row + a - 1]
        return values if a == 1 else values * (up if a == 0 else down)

    inner = masks[0] + masks[1] + masks[2]

    def gather_band(band, carry):
        row = 2 + 4 * band
        up, _ = neighbour(row)
        _, down = neighbour(row + 3)
        for block in range(TAPS + 1):
            if block == TAPS:
                first = masks[0] * up + masks[1] + masks[2]
                last = masks[0] + masks[1] + masks[2] * down
                parts = [first, inner, inner, last]
            else:
                a, b = divmod(block, 3)
                parts = [moved[b, row + i + a - 1] for i in range(4)]
                if a == 0:
                    parts[0] = parts[0] * up
                elif a == 2:
                    parts[3] = parts[3] * down
            both = jnp.concatenate(parts, axis=0).astype(BF16)
            wide[pl.ds(pl.multiple_of(band * BAND, 16), BAND), block * 128 : block * 128 + 128] = both
        return carry

    lax.fori_loop(0, bands, gather_band, 0)
    for block in range(TAPS + 1):
        lanes = slice(block * 128, block * 128 + 128)
        tail = jnp.concatenate([gather_row(halo_row, block), jnp.zeros((extra - W, 128), F32)], axis=0)
        wide[tokens : tokens + extra, lanes] = tail.astype(BF16)

    def fc2_part(n):
        ref, at = (fc2, n * SPAN) if n * SPAN < mine else (fc2_o, n * SPAN - mine)
        return ref[at : at + SPAN, :]

    def one_block(at, own):
        total = None
        coming = dot(wide[at, :], weights[:, 0:SPAN])
        for n in range(width // SPAN):
            lanes = slice(n * SPAN, n * SPAN + SPAN)
            spread = coming
            if (n + 1) * SPAN < width:
                coming = dot(wide[at, :], weights[:, (n + 1) * SPAN : (n + 2) * SPAN])
            grad = dot(dy[at, :], fc2_t[:, lanes])
            bell = jnp.exp2(spread * spread * -LOG2E)
            share = 1.0 + lax.erf(spread)
            du[at, lanes] = (grad * (share + spread * bell * 1.1283791670955126)).astype(BF16)
            if own:
                active = (spread * share).astype(BF16)
                act[at, lanes] = active
                part = dot(active, fc2_part(n))
                total = part if total is None else total + part
        return total

    size = 896

    def own_block(block, carry):
        at = pl.ds(pl.multiple_of(block * size, 128), size)
        for part in range(TAPS + 1):
            kept = min(128, KEPT - part * 128)
            turned = wide[at, part * 128 : part * 128 + 128].T
            wide_t[part * 128 : part * 128 + kept, at] = turned[0:kept]
        dy_t[:, at] = dy[at, :].T
        out_acc[at, :] = one_block(at, True) * ROOT
        return carry

    lax.fori_loop(0, tokens // size, own_block, 0)
    one_block(slice(tokens, tokens + extra), False)

    def fold(half):
        lanes = pl.ds(pl.multiple_of(half * SPAN, SPAN), SPAN)
        base = base_ref[:, lanes].astype(F32)
        grad = sums[4 * 128 : 5 * 128, :]
        marks = sums[TAPS * 128 : KEPT, :]
        mean = marks[TAPS : TAPS + 1]
        bias_g = mean
        rows_g = []
        factors = taps[:, lanes]
        for k in range(TAPS):
            part = sums[k * 128 : k * 128 + 128, :]
            mark = marks[k : k + 1]
            factor = factors[k : k + 1]
            grad = grad + part * factor
            bias_g = bias_g + mark * factor
            rows_g.append(jnp.sum(part * base, axis=0, keepdims=True) + mark * factors[TAPS : TAPS + 1])
        rows_g = jnp.concatenate(rows_g + [bias_g, mean, jnp.zeros((5, SPAN), F32)], axis=0)
        for i in range(SPAN // 128):
            core, row = divmod(i, STEP // 128)
            piece = slice(i * 128, i * 128 + 128)
            split_g[half, core, row * 128 : row * 128 + 128, :] = grad[:, piece] * 0.5
            split_g[half, core, 512 + 16 * row : 528 + 16 * row, :] = rows_g[:, piece] * 0.5

    def gradients(half, carry):
        lanes = pl.ds(pl.multiple_of(half * SPAN, SPAN), SPAN)
        for part in (slice(0, 592), slice(592, KEPT)):
            sums[part, :] = dot(wide_t[part, :], du[0:tokens, lanes])
        turned = dot(dy_t[...], act[:, lanes]).T * ROOT
        for core in range(2):
            split_g[half, core, 256:512, :] = turned[core * STEP : core * STEP + STEP]
        for k in range(TAPS):
            weights_t[lanes, k * 128 : k * 128 + 128] = weights[k * 128 : k * 128 + 128, lanes].T
        fold(half)
        return carry

    lax.fori_loop(0, width // SPAN, gradients, 0)

    groups = ((4, 1, 7, 0), (3, 6, 2, 5), (8,))

    def collect_row(group, base, row):
        total = [None] * 3
        for i, k in enumerate(group):
            a, b = divmod(k, 3)
            source = row + 3 - a
            part = moved[base + i, source]
            if a != 1:
                up, down = neighbour(source)
                part = part * (up if a == 0 else down)
            total[b] = part if total[b] is None else total[b] + part
        if total[0] is not None:
            total[0] = shift_left(total[0])
        if total[2] is not None:
            total[2] = shift_right(total[2])
        total = functools.reduce(jnp.add, [part for part in total if part is not None])
        at = pl.ds(pl.multiple_of(row * W, 8), W)
        if group[0] == 4:
            dxm[at, :] = total
        else:
            dxm[at, :] += total

    for number, group in enumerate(groups):
        base = 4 * (number & 1)
        for i in range(len(group)):
            moved[base + i, 1] = jnp.zeros((W, 128), F32)
            moved[base + i, rows + 2] = jnp.zeros((W, 128), F32)

        def back(at):
            parts = [weights_t[:, k * 128 : k * 128 + 128] for k in group]
            return dot(du[at, :], jnp.concatenate(parts, axis=1))

        tail = back(slice(tokens, tokens + extra))
        for i in range(len(group)):
            moved[base + i, halo_row] = tail[0:W, i * 128 : i * 128 + 128]

        def back_block(block, carry):
            result = back(pl.ds(pl.multiple_of(block * 4 * BAND, 16), 4 * BAND))
            for i in range(len(group)):
                moved[base + i, pl.ds(2 + 16 * block, 16)] = result[
                    :, i * 128 : i * 128 + 128
                ].reshape(16, W, 128)
            if number:
                for i in range(16):
                    collect_row(groups[number - 1], 4 - base, 16 * block + i)
            return carry

        lax.fori_loop(0, bands // 4, back_block, 0)

    def last_rows(row, carry):
        collect_row(groups[-1], 4 * ((len(groups) - 1) & 1), row)
        return carry

    lax.fori_loop(0, rows, last_rows, 0, unroll=4)

    mid_g[...] = jnp.zeros(mid_g.shape, F32)
    for load in loads:
        load.wait()
    place = to_slots()
    proj = proj_w[...].astype(F32)
    proj_sw = jnp.concatenate([proj[64:], proj[:64]], axis=0).T.astype(BF16)

    def fold_up(values):
        return jnp.sum(jnp.sum(values.reshape(-1, 64, 128), axis=0).reshape(8, 8, 128), axis=0)

    def two_bands(block, carry):
        at = pl.ds(pl.multiple_of(block * 2 * BAND, 16), 2 * BAND)
        middle = x1[at, :]
        result = middle + out_acc[at, :] + shifts[3:4, :]
        hat, inverse = norm_hat(middle)
        grad = dxm[at, :] * ROOT
        grad_y = dy[at, :].astype(F32)
        dx1 = grad_y + norm_back(grad * gains[1:2, :], hat, inverse)
        dx1_out[at, :] = dx1
        dz = dx1.astype(BF16)
        mid_g[8:136, :] += dot_in(heads_out[at, :], dz)
        do = dot(dz, proj_sw)
        for i in range(2):
            band = 2 * block + i
            live = live_band(side * bands + band)
            part = slice(i * BAND, (i + 1) * BAND)
            here = pl.ds(pl.multiple_of(band * BAND, 16), BAND)
            out[here, :] = (result[part] * live).astype(BF16)
            do_out[band] = dot(place, (do[part] * live).astype(BF16)).astype(BF16)
        terms = (grad * hat, grad, dz.astype(F32), grad_y)
        return tuple(total + fold_up(term) for total, term in zip(carry, terms))

    zero = jnp.zeros((8, 128), F32)
    totals = lax.fori_loop(0, bands // 2, two_bands, (zero,) * 4)
    for i in range(4):
        mid_g[i : i + 1, :] = jnp.sum(totals[i], axis=0, keepdims=True)


def stages(levels, shared):
    rest = list(range(2, levels))
    pairs = [rest[i : i + 2] for i in range(0, len(rest), 2)]
    return [[0], ["x", 1]] + pairs if shared else [[0], [1]] + pairs + [["x"]]


def group_size(levels, rows):
    unit = 16 * 2 ** (levels - 1)
    return -(-rows // unit) * unit


def stage_shapes(levels, shared, rows):
    halves, shapes = 2, [(1, 2, rows, 128)]
    for dims in stages(levels, shared)[1:]:
        if "x" in dims:
            halves = 1
        rows >>= sum(1 for dim in dims if dim != "x")
        shapes.append((2 ** len(dims) - 1, halves, rows, 128))
    return shapes


def group_scratch(levels, shared, rows):
    buffers = [pltpu.VMEM(part, BF16) for part in stage_shapes(levels, shared, rows)]
    return [pltpu.VMEM((2, rows, 128), F32)] + buffers + buffers


def group_links(levels, shared):
    return sum(2 ** len(dims) - 1 for dims in stages(levels, shared))


def everyone(levels):
    batch, side = lax.axis_index("batch"), lax.axis_index("heads")
    peers = []
    for dims in stages(levels, True):
        for flips in range(1, 2 ** len(dims)):
            peers.append(flipped(batch, side, dims, flips))
    return peers


def flipped(batch, side, dims, flips):
    for i, dim in enumerate(dims):
        if flips >> i & 1:
            if dim == "x":
                side = 1 - side
            else:
                batch = batch + (1 - 2 * ((batch // 2**dim) % 2)) * 2**dim
    return batch, side


class Group:
    def __init__(self, levels, shared, buffers, sems, base):
        self.stages = stages(levels, shared)
        count = len(self.stages)
        self.cur, self.sends, self.recvs = buffers[0], buffers[1 : 1 + count], buffers[1 + count :]
        self.sems, self.base = sems, base
        self.batch, self.side = lax.axis_index("batch"), lax.axis_index("heads")
        self.core = self.batch % 2
        at, rows = 0, self.cur.shape[1]
        self.kept, self.given = [(at, rows)], [None]
        for dims in self.stages[1:]:
            bits = [dim for dim in dims if dim != "x"]
            starts = []
            for flips in range(2 ** len(dims)):
                batch, _ = flipped(self.batch, self.side, dims, flips)
                start = at
                for i, bit in enumerate(bits):
                    start = start + ((batch // 2**bit) % 2) * (rows >> (i + 1))
                starts.append(pl.multiple_of(start, 16))
            rows >>= len(bits)
            at = starts[0]
            self.kept.append((at, rows))
            self.given.append(starts)
        self.left = list(range(count))

    def link(self, stage, flips):
        number = self.base + sum(2 ** len(part) - 1 for part in self.stages[:stage]) + flips - 1
        peer = flipped(self.batch, self.side, self.stages[stage], flips)
        source, target = self.sends[stage].at[flips - 1], self.recvs[stage].at[flips - 1]
        return link(source, target, self.sems[0].at[number], self.sems[1].at[number], peer)

    def wait(self, stage):
        for flips in range(1, 2 ** len(self.stages[stage])):
            self.link(stage, flips).wait()

    def add(self, stage):
        at, rows = self.kept[stage]
        here, recv = pl.ds(at, rows), self.recvs[stage]
        if recv.shape[1] == 2:
            total = self.cur[:, here, :]
            for i in range(recv.shape[0]):
                total = total + recv[i].astype(F32)
            self.cur[:, here, :] = total
            return
        total = self.cur[self.side, here, :]
        for i in range(recv.shape[0]):
            total = total + recv[i, 0].astype(F32)
        self.cur[self.side, here, :] = total

    def advance(self, count=1, pieces=None):
        for number in self.left[:count]:
            self.phase(number, pieces)
        del self.left[:count]

    def phase(self, number, pieces):
        count = len(self.stages)
        if number == 0:
            for half in range(2):
                for row, value in pieces(half, 1 - self.core):
                    self.sends[0][0, half, row : row + value.shape[0], :] = value.astype(BF16)
            self.link(0, 1).start()
            for half in range(2):
                for row, value in pieces(half, self.core):
                    self.cur[half, row : row + value.shape[0], :] = value
        else:
            self.wait(number - 1)
            self.add(number - 1)
            dims = self.stages[number]
            _, rows = self.kept[number]
            for flips in range(1, 2 ** len(dims)):
                crossing = "x" in dims and flips >> dims.index("x") & 1
                here = pl.ds(self.given[number][flips], rows)
                if self.sends[number].shape[1] == 2:
                    self.sends[number][flips - 1] = self.cur[:, here, :].astype(BF16)
                else:
                    half = 1 - self.side if crossing else self.side
                    self.sends[number][flips - 1, 0] = self.cur[half, here, :].astype(BF16)
                self.link(number, flips).start()

    def finish(self):
        self.wait(len(self.stages) - 1)
        self.add(len(self.stages) - 1)
        at, rows = self.kept[-1]
        return self.cur[self.side, pl.ds(at, rows), :].astype(BF16)


class Gather:
    def __init__(self, levels, out, shared, sems, base):
        self.stages, self.out, self.shared = stages(levels, True), out, shared
        self.sems, self.base = sems, base
        self.batch, self.side = lax.axis_index("batch"), lax.axis_index("heads")
        self.core = self.batch % 2
        at, count = 0, out.shape[2]
        self.kept = [(at, count)]
        for dims in self.stages[1:]:
            for bit in dims:
                if bit != "x":
                    count //= 2
                    at = at + ((self.batch // 2**bit) % 2) * count
            self.kept.append((at, count))
        self.left = list(range(len(self.stages)))

    def links(self, stage):
        dims = self.stages[stage]
        at, count = self.kept[stage]
        number = self.base + sum(2 ** len(part) for part in self.stages[:stage])
        mine = self.out.at[self.core, self.side, pl.ds(at, count)]
        for flips in range(1, 2 ** len(dims)):
            part = mine
            if "x" in dims and flips >> dims.index("x") & 1:
                if not self.shared:
                    continue
                part = self.out.at[self.core, self.side, pl.ds(at, count), pl.ds(0, self.shared)]
            yield self.made(part, number, flipped(self.batch, self.side, dims, flips))
            number += 1
        if stage == 0 and self.shared:
            part = self.out.at[self.core, 1 - self.side, :, pl.ds(0, self.shared)]
            yield self.made(part, number, flipped(self.batch, self.side, dims, 1))

    def made(self, part, number, peer):
        return link(part, part, self.sems[0].at[number], self.sems[1].at[number], peer)

    def begin(self, pieces):
        at, _ = self.kept[-1]
        row = 0
        for piece in pieces:
            self.out[self.core, self.side, at, row : row + piece.shape[0], :] = piece
            row += piece.shape[0]
        for made in self.links(len(self.stages) - 1):
            made.start()

    def advance(self):
        stage = len(self.left) - 1
        for made in self.links(stage):
            made.wait()
        if stage:
            for made in self.links(stage - 1):
                made.start()
        del self.left[-1]


def attend_back_kernel(
    table, key_c, key_f, val_c, val_f, xn, query_t, query_o, do_ref, ot_ref, lse, output,
    dq_out, own_out, send_out, output_out,
    acc_c, acc_f, query_ref, turned_c, turned_f, keys_ref, vals_ref, kept,
):
    step = pl.program_id(0)
    each = xn.shape[0]
    bands = each * pl.num_programs(0)
    side = lax.axis_index("heads")

    @pl.when(step == 0)
    def _():
        acc_c[...] = jnp.zeros(acc_c.shape, F32)
        acc_f[...] = jnp.zeros(acc_f.shape, F32)
        query_ref[...] = full_query(query_t, query_o, side).T.astype(BF16)

    output_out[...] = output[...]
    firsts = [table[1, side * bands + each * step + i] for i in range(each)]
    for i in range(each):

        @pl.when((step == 0) | (kept[i] != firsts[i]))
        def _():
            kept[i] = firsts[i]
            keys = window(key_f, firsts[i])
            keys_ref[i] = keys
            vals_ref[i] = window(val_f, firsts[i])
            for part, (start, count) in enumerate(HALVES):
                rows = slice(start * PACKED, (start + count) * PACKED)
                turned_f[i, part, :, 0 : count * PACKED] = keys[rows].T[64:128]
            turned_c[i] = window(key_c, firsts[i]).T[0:64]

    queries, query_rows, grads_t, grads_low = [], [], [], []
    for i in range(each):
        query = dot(xn[i], query_ref[...]).astype(BF16)
        queries.append(query)
        query_rows.append(query.astype(F32).T.astype(BF16))
        grads_t.append(do_ref[i].astype(F32).T)
        grads_low.append(grads_t[i].astype(BF16))
    dq = [[None] * 4 for _ in range(each)]

    def products(unit):
        i, head, part = unit
        fine = head >= 2
        image = table[0, side * bands + each * step + i]
        start, count = HALVES[part]
        if fine:
            rows = slice(start * PACKED, (start + count) * PACKED)
            keys, vals = keys_ref[i, rows], vals_ref[i, rows]
        else:
            keys, vals = window(key_c, firsts[i]), window(val_c, firsts[i])
        swapped = (head + 2) & 3
        delta = jnp.sum(
            ot_ref[i, 32 * head : 32 * head + 32]
            * grads_t[i][32 * swapped : 32 * swapped + 32],
            axis=0,
            keepdims=True,
        )
        offset = lse[i, head : head + 1, :] * (-1.0 / EXP_SCALE)
        left = score_rows(query_rows[i], head, image, fine)
        left = with_offset(left, ONES + (0 if fine else 64), offset)
        right = with_offset(head_rows(grads_low[i], swapped), 64 if fine else 0, -delta)
        return dot(keys, left), dot(vals, right)

    held = {}

    def back(unit, score, prob_grad):
        i, head, part = unit
        fine = head >= 2
        swapped = (head + 2) & 3
        prob = jnp.exp2(score * EXP_SCALE)
        score_grad = (prob * prob_grad).astype(BF16)
        row = 32 * (head & 1)
        start, count = HALVES[part]
        turned = turned_c[i, row : row + 32]
        if fine:
            turned = turned_f[i, part, row : row + 32, 0 : count * PACKED]
        grad = dot(turned, score_grad)
        dq[i][head] = grad if part == 0 else dq[i][head] + grad
        pair = held.setdefault((i, fine, part), ([], []))
        pair[0].extend([score_grad, prob.astype(BF16)])
        pair[1].extend([head_lanes(queries[i], head), head_lanes(do_ref[i], swapped)])
        if head & 1:
            both = dot(jnp.concatenate(pair[0], axis=1), jnp.concatenate(pair[1], axis=0))
            if fine:
                at = pl.ds(firsts[i] + start, count)
                acc_f[at, 0:PACKED, :] += both.reshape(count, PACKED, 128)
            else:
                acc_c[pl.ds(firsts[i], MAX_BANDS)] += both.reshape(MAX_BANDS, COARSE, 128)

    waiting = []
    for i in range(each):
        for head, parts in ((2, 2), (3, 2), (0, 1), (1, 1)):
            for part in range(parts):
                waiting.append(((i, head, part), *products((i, head, part))))
                if len(waiting) > 3:
                    back(*waiting.pop(0))
    for unit in waiting:
        back(*unit)
    for i in range(each):
        dq_out[i] = (jnp.concatenate(dq[i], axis=0).T * SCALE).astype(BF16)

    @pl.when(step == pl.num_programs(0) - 1)
    def _():
        span = bands + 1
        lane = lax.broadcasted_iota(jnp.int32, (1, 128), 1)
        scale_c = jnp.where(lane < 64, SCALE, 1.0)
        scale_f = jnp.where(lane < 64, 1.0, SCALE)
        for dest, at, kind in (
            (own_out, side * (bands - 1), F32),
            (send_out, (1 - side) * (bands - 1), BF16),
        ):
            dest[:, 0:COARSE, :] = (acc_c[pl.ds(at, span)] * scale_c).astype(kind)
            for cell in range(4):
                part = acc_f[pl.ds(at, span), 14 * cell : 14 * cell + 16, :] * scale_f
                part = jnp.where(cell_valid(part.shape, 1), part, 0.0)
                row = COARSE + 16 * cell
                dest[:, row : row + 16, :] = part.astype(kind)


def tail_kernel(
    levels, own_in, given, split_in, mid_g, slab_in, other, meta, xn_in, hat_in, dq_in, query_t,
    query_o, dx1_in, inv_in, gains,
    red_c_in, conv_c_in, gain_c, shifts_c, kv_c, taps_c_ref,
    red_f_in, conv_f_in, gain_f, shifts_f, kv_f, taps_f_ref,
    tok_grad, early, joint, little,
    pack, small, small_in, small_sems, recv, grad_ref, val_ref, dxn, send_sem, recv_sem, send_sems, recv_sems, turned_c, turned_f,
    dx1, inv, hat_ref, own, split_g, slab, xn, dq, red_c, conv_c, red_f, conv_f, xt, load_sems,
    *buffers,
):
    bands = xn.shape[0]
    side = lax.axis_index("heads")
    greet(*everyone(levels))
    early_pairs = (
        (split_in, split_g), (dq_in, dq), (xn_in, xn), (own_in, own), (slab_in, slab),
        (conv_c_in, conv_c), (conv_f_in, conv_f),
    )
    loads = fetch(early_pairs, load_sems)
    met(len(everyone(levels)))
    swaps = [
        remote(given.at[:, here], recv.at[:, here], send_sem.at[i], recv_sem.at[i], across())
        for i, here in enumerate((pl.ds(0, COARSE), pl.ds(COARSE, FINE)))
    ]
    late_pairs = (
        (red_c_in, red_c), (red_f_in, red_f), (hat_in, hat_ref), (inv_in, inv), (dx1_in, dx1),
    )
    loads += fetch(late_pairs, load_sems.at[pl.ds(len(early_pairs), len(late_pairs))])
    sems = (send_sems, recv_sems)
    split_count, shared_count = (1 + 2 * len(stages(levels, shared)) for shared in (False, True))
    before = Group(levels, False, buffers[:split_count], sems, 0)
    base = group_links(levels, False)
    buffers = buffers[split_count:]
    conv = Group(levels, True, buffers[:shared_count], sems, base)
    base += group_links(levels, True)
    rest = Group(levels, True, buffers[shared_count:], sems, base)
    base += group_links(levels, True)
    early_rows, late_rows, later_rows = (group.cur.shape[1] for group in (before, conv, rest))
    gather = Gather(levels, joint, joint.shape[3], sems, base)
    base += group_links(levels, True) + len(stages(levels, True))
    gather_split = Gather(levels, early, 0, sems, base)

    def split_pieces(half, which):
        yield 0, split_g[(half + side) % 2, which]
        if early_rows > SPLIT:
            yield SPLIT, jnp.zeros((early_rows - SPLIT, 128), F32)

    def shared_pieces(first, used, rows):
        def pieces(half, which):
            at = pl.multiple_of(first + used * (2 * half + which), 16)
            yield 0, pack[pl.ds(at, used), :]
            if rows > used:
                yield used, jnp.zeros((rows - used, 128), F32)

        return pieces

    batch, order = lax.axis_index("batch"), stages(levels, True)

    def small_links(stage):
        before = sum(2 ** len(dims) - 1 for dims in order[:stage])
        for flips in range(1, 2 ** len(order[stage])):
            at = before + flips - 1
            yield at, link(
                small.at[stage], small_in.at[at], small_sems.at[0, at], small_sems.at[1, at],
                flipped(batch, side, order[stage], flips),
            )

    def small_phase(stage):
        if stage:
            total = small[stage - 1]
            for at, made in small_links(stage - 1):
                made.wait()
                total = total + small_in[at]
            if stage == len(order):
                little[...] = total
                return
            small[stage] = total
        for _, made in small_links(stage):
            made.start()

    for load in loads[:7]:
        load.wait()
    before.advance(1, split_pieces)

    start = 0
    parts = []
    for count in (conv_c.shape[0], conv_f.shape[0], 128, 128, 128, 128):
        parts.append(pack.at[start : start + count])
        start += count
    conv_c_g, conv_f_g, kv_c_g, kv_f_g, query_g, proj_g = parts
    small_c, small_f, front_g = small.at[0, 0:16], small.at[0, 16:32], small.at[0, 32:40]
    small[0, 40:48, :] = mid_g[0:8, :]
    proj_g[...] = mid_g[8:136, :]
    taps_c, taps_f = pad_taps(taps_c_ref[...], True), pad_taps(taps_f_ref[...], False)
    kv_f_sw = swap_lanes(kv_f[...])

    val_ref[0] = jnp.zeros((CELLS, 128), F32)
    val_ref[bands + 1] = jnp.zeros((CELLS, 128), F32)
    val_ref[1 : bands + 1] = slab[...]
    val_ref[pl.ds((1 - side) * (bands + 1), 1)] = other[
        pl.ds(side * (bands - 1), 1)
    ].astype(F32)
    at = pl.ds(side * bands, bands)
    above, below = meta[0, at], meta[1, at]
    grid = xn[...].reshape(bands, 16, 16, 128)
    slot_grads = dq[...].reshape(bands, 16, 16, 128)
    total = None
    for i in range(16):
        turned = grid[:, i].reshape(bands * 16, 128).T
        xt[i] = turned
        part = dot(turned, slot_grads[:, i].reshape(bands * 16, 128))
        total = part if total is None else total + part
    query_g[...] = total
    full = full_query(query_t, query_o, side).astype(BF16)
    dxn[...] = dot(dq[...].reshape(-1, 128), full).reshape(bands, SLOTS, 128)
    grad_ref[0] = jnp.zeros((CELLS, 128), F32)
    grad_ref[bands + 1] = jnp.zeros((CELLS, 128), F32)
    turned_c[...] = conv_c[...].T
    turned_f[...] = conv_f[...].T
    before.advance()
    swaps[0].wait()
    here = pl.ds(1 - side, bands + 1)
    for load in loads[7:]:
        load.wait()
    grad_ref[here, 0:COARSE] = own[:, 0:COARSE] + recv[:, 0:COARSE].astype(F32)
    lane = lax.broadcasted_iota(jnp.int32, (1, 1, 128), 2)

    def tap_sum(values, grads):
        return fold_rows(values * grads)

    def reduce_back(pair, red, conv, gain, shifts, kv, small, kv_g):
        hat, inverse = norm_hat(red[...])
        normed = hat * gain[...] + shifts[1:2, :]
        cdf, bell = gauss(normed)
        active = (normed * cdf).astype(BF16)
        kv_g[...] = dot_in(active, pair)
        small[9:10, :] = jnp.sum(pair.astype(F32), axis=0, keepdims=True)
        grad = dot_t(pair, kv) * gelu_slope(normed, cdf, bell)
        small[11:12, :] = jnp.sum(grad * hat, axis=0, keepdims=True)
        small[12:13, :] = jnp.sum(grad, axis=0, keepdims=True)
        dc = norm_back(grad * gain[...], hat, inverse).astype(BF16)
        small[13:14, :] = jnp.sum(dc.astype(F32), axis=0, keepdims=True)
        return dc

    small_c[...] = jnp.zeros(small_c.shape, F32)
    small_f[...] = jnp.zeros(small_f.shape, F32)

    vals = val_ref[:, 0:COARSE, :]
    ext = grad_ref[:, 0:COARSE, :]
    ext = jnp.where(lane < 64, ext, ext.astype(BF16).astype(F32))
    mid = ext[1:-1]
    near = (by_band(vals[:-2], above), vals[1:-1], by_band(vals[2:], below))
    for a in range(3):
        for b in range(3):
            moved = near[a] if b == 1 else roll_cells(near[a], 1 - b)
            small_c[3 * a + b : 3 * a + b + 1, :] = jnp.sum(
                tap_sum(moved, mid), axis=0, keepdims=True
            )
    small_c[10:11, :] = jnp.sum(mid.reshape(-1, 128), axis=0, keepdims=True)
    pair = mid + depthwise_coarse(ext, above, below, taps_c, flip=True)
    pair = jnp.where(cell_valid(pair.shape, 1), pair, 0.0)
    pair = pair.reshape(bands * COARSE, 128).astype(BF16)
    dc = reduce_back(pair, red_c, conv_c, gain_c, shifts_c, kv_c[...], small_c, kv_c_g)
    for i in range(16):
        part = slice(i * 128, (i + 1) * 128)
        conv_c_g[part, :] = dot(xt[i], dc)
        back = dot(dc, turned_c[:, part]).reshape(bands, 16, 128)
        dxn[:, 16 * i : 16 * i + 16, :] += back

    conv.advance(1, shared_pieces(0, CONV, late_rows))
    before.advance()
    swaps[1].wait()
    grad_ref[here, COARSE:CELLS] = own[:, COARSE:CELLS] + recv[:, COARSE:CELLS].astype(F32)
    vals = val_ref[:, COARSE:CELLS, :]
    ext = grad_ref[:, COARSE:CELLS, :]
    ext = jnp.where(lane >= 64, ext, ext.astype(BF16).astype(F32))
    rows = depthwise_fine(ext, above, below, taps_f, flip=True)
    near = fine_rows(vals, above, below)
    mids = fine_rows(ext, above, below)[1]
    for a in range(3):
        for b in range(3):
            total = jnp.zeros((8, 128), F32)
            for row in range(2):
                even, odd = near[a][row][:, 0], near[a][row][:, 1]
                grad_even, grad_odd = mids[row][:, 0], mids[row][:, 1]
                if b == 0:
                    moved = (roll_cells(odd, 1), even)
                elif b == 1:
                    moved = (even, odd)
                else:
                    moved = (odd, roll_cells(even, -1))
                total = total + tap_sum(moved[0], grad_even) + tap_sum(moved[1], grad_odd)
            small_f[3 * a + b : 3 * a + b + 1, :] = jnp.sum(total, axis=0, keepdims=True)
    small_f[10:11, :] = jnp.sum(ext[1:-1].reshape(-1, 128), axis=0, keepdims=True)
    valid = cell_valid((bands, 16, 128), 1)
    blocks = []
    for row in range(2):
        for column in range(2):
            block = jnp.where(valid, mids[row][:, column] + rows[row][column], 0.0)
            blocks.append(block.astype(BF16).reshape(bands, 1, 16, 128))
    pair = jnp.concatenate(blocks, axis=1).reshape(bands * FINE, 128)
    conv.advance()
    dc = reduce_back(pair, red_f, conv_f, gain_f, shifts_f, kv_f_sw, small_f, kv_f_g)
    for i in range(4):
        part = slice(i * 128, (i + 1) * 128)
        total = None
        for row in range(2):
            for column in range(2):
                cells = dc.reshape(bands, 4, 16, 128)[:, 2 * row + column].reshape(bands * 16, 128)
                product = dot(xt[fine_slot(i, row, column)], cells)
                total = product if total is None else total + product
        conv_f_g[part, :] = total
        back = dot(dc, turned_f[:, part]).reshape(bands, 4, 16, 128)
        for row in range(2):
            for column in range(2):
                slot = 16 * fine_slot(i, row, column)
                dxn[:, slot : slot + 16, :] += back[:, 2 * row + column]

    front_g[...] = jnp.zeros(front_g.shape, F32)
    sums = jnp.zeros((8, 128), F32)
    along = jnp.zeros((8, 128), F32)
    for band in range(bands):
        grad = dxn[band]
        sums = sums + fold_rows(grad)
        along = along + fold_rows(grad * hat_ref[band].astype(F32))
    front_g[0:1, :] = jnp.sum(along, axis=0, keepdims=True)
    front_g[1:2, :] = jnp.sum(sums, axis=0, keepdims=True)

    small_phase(0)
    rest.advance(1, shared_pieces(4 * CONV, REST, later_rows))
    conv.advance()
    before.advance()
    place = from_slots()

    def one_band(band):
        at = slice(band * BAND, (band + 1) * BAND)
        back = norm_back(dxn[band] * gains[0:1, :], hat_ref[band].astype(F32), 1.0)
        tok_grad[at, :] = dx1[at, :] + dot(place, back.astype(BF16)) * inv[at, :]

    began = len(before.left) + 1
    done = 0
    total = max(len(rest.left) + 1 + len(gather.left), began + len(gather_split.left))
    for number in range(1, total + 1):
        while done < bands and done * total < number * bands:
            one_band(done)
            done += 1
        if rest.left:
            rest.advance()
            conv.advance()
        elif number + len(gather.left) == total:
            conv.advance(len(conv.left))
            gather.begin([conv.finish(), rest.finish()])
        else:
            gather.advance()
        if before.left:
            before.advance()
        elif number == began:
            gather_split.begin([before.finish()])
        elif gather_split.left:
            gather_split.advance()
        if number <= len(order):
            small_phase(number)


def shared_rows(start, count):
    done = 0
    while done < count:
        group = 0 if start + done < 4 * CONV else 1
        if group == 0:
            quarter, row = divmod(start + done, CONV)
            size = min(count - done, CONV - row)
        else:
            quarter, row = divmod(start + done - 4 * CONV, REST)
            size = min(count - done, REST - row)
        yield group, quarter % 2, quarter // 2, row, done, size
        done += size


def unpack_kernel(
    levels,     early, joint, little, tok_grad,
    tok_grad_out, gains, shifts, query, conv_c, gain_c, shifts_c, kv_c, taps_c, conv_f, gain_f, shifts_f, kv_f,
    taps_f, proj, hidden, fc1, depth, fc2,
):
    tok_grad_out[...] = tok_grad[...]

    unpack_grads(
        levels, early, joint, little, gains, shifts, query, conv_c, gain_c, shifts_c, kv_c, taps_c,
        conv_f, gain_f, shifts_f, kv_f, taps_f, proj, hidden, fc1, depth, fc2,
    )


def unpack_grads(
    levels, early, joint, little,
    gains, shifts, query, conv_c, gain_c, shifts_c, kv_c, taps_c, conv_f, gain_f, shifts_f, kv_f,
    taps_f, proj, hidden, fc1, depth, fc2,
):
    side = lax.axis_index("heads")
    half = query.shape[0]
    first = group_size(levels, CONV) // joint.shape[2]
    spans = (slice(0, first), slice(first, joint.shape[3]))

    def quarter_rows(group, core, h):
        ref, rows = (early, slice(None)) if group == 2 else (joint, spans[group])
        return ref[core, h, :, rows, :].reshape(-1, 128)


    def rows_of(start, count):
        pieces = [
            quarter_rows(group, core, h)[at : at + size].astype(F32)
            for group, core, h, at, _, size in shared_rows(start, count)
        ]
        return pieces[0] if len(pieces) == 1 else jnp.concatenate(pieces, axis=0)

    start = 0
    for ref in (conv_c, conv_f, kv_c):
        count = ref.shape[0]
        for group, core, h, at, offset, size in shared_rows(start, count):
            ref[offset : offset + size, :] = quarter_rows(group, core, h)[at : at + size].astype(F32)
        start += count
    kv_f[...] = swap_lanes(rows_of(start, 128))
    both = rows_of(start + 128, 128)
    query[...] = jnp.where(side == 0, both[:, :half], both[:, half:]).T
    proj[...] = rows_of(start + 256, 128)
    small = little[...]
    coarse, fine, front, mid = small[0:16], small[16:32], small[32:40], small[40:48]
    taps_c[...] = coarse[0:9, half:]
    taps_f[...] = fine[0:9, :half]
    gain_c[...] = coarse[11:12]
    gain_f[...] = fine[11:12]
    shifts_c[0:1, :] = coarse[13:14]
    shifts_c[1:2, :] = coarse[12:13]
    shifts_c[2:3, :] = jnp.concatenate([coarse[9:10, half:], coarse[10:11, half:]], axis=1)
    shifts_f[0:1, :] = fine[13:14]
    shifts_f[1:2, :] = fine[12:13]
    shifts_f[2:3, :] = jnp.concatenate([fine[9:10, :half], fine[10:11, :half]], axis=1)
    gains[0:1, :] = front[0:1]
    gains[1:2, :] = mid[0:1]
    shifts[0:1, :] = front[1:2]
    shifts[1:2, :] = mid[2:3]
    shifts[2:3, :] = mid[1:2]
    shifts[3:4, :] = mid[3:4]
    for core in range(2):
        split = quarter_rows(2, core, side)
        for i in range(2):
            lanes = slice(core * STEP + i * 128, core * STEP + i * 128 + 128)
            fc1[:, lanes] = split[i * 128 : i * 128 + 128].astype(F32)
            block = split[512 + 16 * i : 528 + 16 * i].astype(F32)
            depth[:, lanes] = block[0:9]
            hidden[:, lanes] = block[9:11]
        fc2[core * STEP : core * STEP + STEP, :] = split[256:512].astype(F32)


SMEM = pl.BlockSpec(memory_space=pltpu.SMEM)
VMEM = pl.BlockSpec(memory_space=pltpu.VMEM)
HBM = pl.BlockSpec(memory_space=pl.ANY)


def shape(dims, kind=F32):
    return jax.ShapeDtypeStruct(dims, kind)


def params(limit=56):
    return pltpu.CompilerParams(vmem_limit_bytes=limit * MIB)


def sending(number, limit=56):
    return pltpu.CompilerParams(
        vmem_limit_bytes=limit * MIB, collective_id=number, has_side_effects=True
    )


def per_device(
    size, tokens, image_bands, cotangent, front_gains, front_shifts, query_w, coarse_conv,
    coarse_gain, coarse_shifts, coarse_kv, coarse_taps, fine_conv, fine_gain, fine_shifts, fine_kv,
    fine_taps, proj_w, hidden_shifts, fc1_w, depth_taps, fc2_w,
):
    count = tokens.shape[0]
    rows = count // W
    bands = count // BAND
    total = 2 * bands
    halo = 2 * W
    half = coarse_kv.shape[1] // 2
    mine = fc1_w.shape[1]
    hidden = 2 * mine
    gain_c, gain_f = coarse_gain[None], fine_gain[None]
    semaphores = pltpu.SemaphoreType.DMA
    levels = size.bit_length() - 1
    query_t = query_w.T

    (
        table, meta, xn, hat, inverse, red_c, red_f, slab, other, query_o,
    ) = pl.pallas_call(
        front_kernel,
        out_shape=(
            shape((3, 32), jnp.int32),
            shape((3, total, 8, 128)),
            shape((bands, SLOTS, 128), BF16),
            shape((bands, SLOTS, 128), BF16),
            shape((count, 128)),
            shape((bands * COARSE, 128)),
            shape((bands * FINE, 128)),
            shape((bands, CELLS, 128)),
            shape((bands, CELLS, 128), BF16),
            shape(query_t.shape, BF16),
        ),
        in_specs=[SMEM] + [VMEM] * 12,
        out_specs=[SMEM] + [VMEM] * 9,
        scratch_shapes=[pltpu.VMEM((bands, CELLS, 128), BF16), semaphores((8,)), semaphores((8,))],
        compiler_params=sending(1),
        name="front",
    )(
        image_bands, tokens, front_gains, front_shifts, coarse_conv, gain_c, coarse_shifts,
        coarse_kv, fine_conv, gain_f, fine_shifts, fine_kv,
        query_t,
    )

    each = 4 if bands % 4 == 0 else 2
    some_bands = pl.BlockSpec((each * BAND, 128), lambda i: (i, 0))
    some_slots = pl.BlockSpec((each, SLOTS, 128), lambda i: (i, 0, 0))
    back = 3 if bands % 3 == 0 else 2
    back_slots = pl.BlockSpec((back, SLOTS, 128), lambda i: (i, 0, 0))
    (
        x1, xm, heads_out, out_t, lse, key_c, key_f, val_c, val_f, fc1_o, fc2_o, depth_o, hidden_o,
        cot_o,
    ) = pl.pallas_call(
        attend_kernel,
        grid=(bands // each,),
        out_shape=(
            shape((count, 128)),
            shape((count, 128), BF16),
            shape((count, 128), BF16),
            shape((bands, 128, SLOTS)),
            shape((bands, 8, SLOTS)),
            shape((total, COARSE, 128), BF16),
            shape((total, PACKED, 128)),
            shape((total, COARSE, 128), BF16),
            shape((total, PACKED, 128)),
            shape(fc1_w.shape, BF16),
            shape(fc2_w.shape, BF16),
            shape(depth_taps.shape),
            shape(hidden_shifts.shape),
            shape((halo, 128), BF16),
        ),
        in_specs=[SMEM] + [VMEM] * 7 + [some_slots, some_bands] + [VMEM] * 5 + [HBM] * 5,
        out_specs=[
            some_bands,
            some_bands,
            some_bands,
            pl.BlockSpec((each, 128, SLOTS), lambda i: (i, 0, 0)),
            pl.BlockSpec((each, 8, SLOTS), lambda i: (i, 0, 0)),
        ]
        + [VMEM] * 4
        + [HBM] * 5,
        scratch_shapes=[
            pltpu.VMEM((total + 2, CELLS, 128), F32),
            pltpu.VMEM((128, 128), BF16),
            pltpu.VMEM((BAND, SLOTS), BF16),
            semaphores((5,)),
            semaphores((5,)),
        ],
        compiler_params=sending(4),
        name="attend",
    )(
        table, slab, other, meta, coarse_taps, fine_taps, coarse_shifts, fine_shifts, xn, tokens,
        query_t, query_o, proj_w, front_gains, front_shifts, fc1_w, fc2_w, depth_taps,
        hidden_shifts, cotangent,
    )

    extra = 64
    output, dx1, out_grad, split_g, mid_g = pl.pallas_call(
        hidden_kernel,
        out_shape=(
            shape((count, 128), BF16),
            shape((count, 128)),
            shape((bands, SLOTS, 128), BF16),
            shape((2, 2, SPLIT, 128)),
            shape((136, 128)),
        ),
        in_specs=[SMEM, HBM] + [VMEM] * 3 + [HBM] + [VMEM] * 11,
        out_specs=[VMEM] * 5,
        scratch_shapes=[
            pltpu.VMEM((count + 2 * halo, 128), BF16),
            pltpu.VMEM((halo, 128), BF16),
            pltpu.VMEM((8, rows + 4, W, 128), F32),
            pltpu.VMEM((count + extra, WIDE), BF16),
            pltpu.VMEM((KEPT, count), BF16),
            pltpu.VMEM((WIDE, hidden), BF16),
            pltpu.VMEM((hidden, TAPS * 128), BF16),
            pltpu.VMEM((16, hidden), F32),
            pltpu.VMEM((16, hidden), F32),
            pltpu.VMEM((128, hidden), BF16),
            pltpu.VMEM((128, hidden), BF16),
            pltpu.VMEM((count + extra, 128), BF16),
            pltpu.VMEM((128, count), BF16),
            pltpu.VMEM((count, hidden), BF16),
            pltpu.VMEM((count + extra, hidden), BF16),
            pltpu.VMEM((KEPT, SPAN), F32),
            pltpu.VMEM((count, 128), F32),
            pltpu.VMEM((count, 128), F32),
            pltpu.VMEM((count, 128), F32),
            pltpu.VMEM((count, 128), BF16),
            semaphores(()),
            semaphores(()),
            semaphores((2,)),
        ],
        compiler_params=sending(2, 63),
        name="hidden",
    )(
        table, x1, xm, cotangent, cot_o, heads_out, fc1_w, fc1_o, fc2_w, fc2_o, depth_taps, depth_o,
        hidden_shifts, hidden_o, front_gains, front_shifts, proj_w,
    )

    dq, grad_own, grad_send, output = pl.pallas_call(
        attend_back_kernel,
        grid=(bands // back,),
        out_shape=(
            shape((bands, SLOTS, 128), BF16),
            shape((bands + 1, CELLS, 128)),
            shape((bands + 1, CELLS, 128), BF16),
            shape((count, 128), BF16),
        ),
        in_specs=[SMEM]
        + [VMEM] * 4
        + [
            back_slots,
            VMEM,
            VMEM,
            back_slots,
            pl.BlockSpec((back, 128, SLOTS), lambda i: (i, 0, 0)),
            pl.BlockSpec((back, 8, SLOTS), lambda i: (i, 0, 0)),
            pl.BlockSpec((back * BAND, 128), lambda i: (i, 0)),
        ],
        out_specs=[back_slots, VMEM, VMEM, pl.BlockSpec((back * BAND, 128), lambda i: (i, 0))],
        scratch_shapes=[
            pltpu.VMEM((total, COARSE, 128), F32),
            pltpu.VMEM((total, FINE, 128), F32),
            pltpu.VMEM((128, 128), BF16),
            pltpu.VMEM((back, 64, MAX_BANDS * COARSE), BF16),
            pltpu.VMEM((back, 2, 64, HALVES[0][1] * PACKED), BF16),
            pltpu.VMEM((back, MAX_BANDS * PACKED, 128), BF16),
            pltpu.VMEM((back, MAX_BANDS * PACKED, 128), BF16),
            pltpu.SMEM((back,), jnp.int32),
        ],
        compiler_params=params(),
        name="attend_back",
    )(table, key_c, key_f, val_c, val_f, xn, query_t, query_o, out_grad, out_t, lse, output)

    peers = sum(2 ** len(dims) - 1 for dims in stages(levels, True))
    links = group_links(levels, False) + 4 * group_links(levels, True) + 2 * len(stages(levels, True)) + 1
    early_rows, late_rows, later_rows = (group_size(levels, part) for part in (SPLIT, CONV, REST))
    pieces = 2 ** (levels - 1)
    joint_rows = (late_rows + later_rows) // pieces
    tokens_grad, early, joint, little = pl.pallas_call(
        functools.partial(tail_kernel, levels),
        out_shape=(
            shape((count, 128)),
            shape((2, 2, pieces, early_rows // pieces, 128), BF16),
            shape((2, 2, pieces, joint_rows, 128), BF16),
            shape((SMALL, 128)),
        ),
        in_specs=[HBM] * 3 + [VMEM, HBM] + [VMEM] * 2 + [HBM] * 3 + [VMEM] * 2 + [HBM] * 2
        + [VMEM] + ([HBM] * 2 + [VMEM] * 4) * 2,
        out_specs=[VMEM] * 4,
        scratch_shapes=[
            pltpu.VMEM((4 * QUARTER, 128), F32),
            pltpu.VMEM((len(stages(levels, True)), SMALL, 128), F32),
            pltpu.VMEM((peers, SMALL, 128), F32),
            semaphores((2, peers)),
            pltpu.VMEM((bands + 1, CELLS, 128), BF16),
            pltpu.VMEM((bands + 2, CELLS, 128), F32),
            pltpu.VMEM((bands + 2, CELLS, 128), F32),
            pltpu.VMEM((bands, SLOTS, 128), F32),
            semaphores((2,)),
            semaphores((2,)),
            semaphores((links,)),
            semaphores((links,)),
            pltpu.VMEM((128, coarse_conv.shape[0]), BF16),
            pltpu.VMEM((128, fine_conv.shape[0]), BF16),
            pltpu.VMEM((count, 128), F32),
            pltpu.VMEM((count, 128), F32),
            pltpu.VMEM((bands, SLOTS, 128), BF16),
            pltpu.VMEM(grad_own.shape, F32),
            pltpu.VMEM(split_g.shape, F32),
            pltpu.VMEM(slab.shape, F32),
            pltpu.VMEM(xn.shape, BF16),
            pltpu.VMEM(dq.shape, BF16),
            pltpu.VMEM(red_c.shape, F32),
            pltpu.VMEM(coarse_conv.shape, BF16),
            pltpu.VMEM(red_f.shape, F32),
            pltpu.VMEM(fine_conv.shape, BF16),
            pltpu.VMEM((16, 128, bands * 16), BF16),
            semaphores((12,)),
        ]
        + group_scratch(levels, False, early_rows)
        + group_scratch(levels, True, late_rows)
        + group_scratch(levels, True, later_rows),
        compiler_params=sending(0),
        name="tail",
    )(
        grad_own, grad_send, split_g, mid_g, slab, other, meta, xn, hat, dq, query_t, query_o, dx1,
        inverse, front_gains,
        red_c, coarse_conv, gain_c, coarse_shifts, coarse_kv, coarse_taps,
        red_f, fine_conv, gain_f, fine_shifts, fine_kv, fine_taps,
    )
    grads = pl.pallas_call(
        functools.partial(unpack_kernel, levels),
        out_shape=(
            shape((count, 128)),
            shape((2, 128)),
            shape((4, 128)),
            shape((half, 128)),
            shape(coarse_conv.shape),
            shape((1, 128)),
            shape((3, 128)),
            shape((128, 128)),
            shape((9, half)),
            shape(fine_conv.shape),
            shape((1, 128)),
            shape((3, 128)),
            shape((128, 128)),
            shape((9, half)),
            shape((128, 128)),
            shape((2, mine)),
            shape((128, mine)),
            shape((9, mine)),
            shape((mine, 128)),
        ),
        in_specs=[VMEM] * 4,
        out_specs=[VMEM] * 19,
        compiler_params=params(),
        name="unpack",
    )(early, joint, little, tokens_grad)
    grads = [output] + list(grads)
    grads[4] = grads[4].T
    for at in (6, 11):
        grads[at] = grads[at].reshape(128)
    return tuple(grads)


def solution(mesh):
    tokens = P(("batch", "heads"), None)
    columns = P(None, "heads")
    return jax.shard_map(
        functools.partial(per_device, mesh.shape["batch"]),
        mesh=mesh,
        in_specs=(tokens, P("batch", None), tokens, P(), P(), columns)
        + (P(),) * 11
        + (columns, columns, columns, P("heads", None)),
        out_specs=(tokens, tokens, P(), P(), columns)
        + (P(),) * 11
        + (columns, columns, columns, P("heads", None)),
        check_vma=False,
    )
```
